32 devices in a mesh: grp: 2 (over x), wid: 4 (over y, core), hid: 4 (over z).
Axes of the slice: x: 2, y: 2, z: 4, core: 2. Of those that a mesh axis runs over, the one named last changes fastest.
Arguments:
- student_in: bfloat16 [512, 4096], P('wid'), may hold values from -6 to 6
- norm_gain: float32 [4096], replicated, may hold values from 0.1 to 1.9
- gate_weight: bfloat16 [4096, 7168], P(None, ('grp', 'hid')), may hold values from -0.09375 to 0.09375
- up_weight: bfloat16 [4096, 7168], P(None, ('grp', 'hid')), may hold values from -0.09375 to 0.09375
- down_weight: bfloat16 [7168, 4096], P(('grp', 'hid')), may hold values from -0.0625 to 0.0625
- projection: bfloat16 [4096, 4, 2048], P(None, None, ('grp', 'hid')), may hold values from -0.09375 to 0.09375
- teacher_in: bfloat16 [512, 8192], P(None, 'wid'), may hold values from -6 to 6
- teacher_gate: bfloat16 [8192, 14336], P('wid', ('grp', 'hid')), may hold values from -0.0625 to 0.0625
- teacher_up: bfloat16 [8192, 14336], P('wid', ('grp', 'hid')), may hold values from -0.0625 to 0.0625
- teacher_down: bfloat16 [14336, 8192], P(('grp', 'hid'), 'wid'), may hold values from -0.046875 to 0.046875
Outputs:
- grad_gate: bfloat16 [4096, 7168], P('wid', ('grp', 'hid'))
- grad_up: bfloat16 [4096, 7168], P('wid', ('grp', 'hid'))
- grad_down: bfloat16 [7168, 4096], P(('grp', 'hid'), 'wid')
- grad_proj: bfloat16 [4096, 4, 2048], P('wid', None, ('grp', 'hid'))
- input_grad: float32 [512, 4096], P('wid', ('grp', 'hid'))
The draws below stay inside these ranges and needn't reach their ends.
All inputs are finite; a program needn't handle non-finite values.
Results may differ from the reference program's by a relative error of at most 0.02.
Values may be sent and summed in bfloat16 or wider, within the bound.
No kernel may reach another device: no remote copies, remote signals or barrier semaphores. Data moves between devices by JAX's collectives and lax.ppermute only.
A program may use at most 128 MiB of HBM per device.

```python
import math
import jax
import jax.numpy as jnp
from jax import lax

D_T = 8192
FF_T = 14336
D_S = 4096
FF_S = 7168
TOKENS = 512
TW = 2048
N_WID = 4


def block_levels(own_key, extent, shards, least, high):
    loudness = 1.0
    for position, shards_of in shards:
        steps = jax.random.uniform(jax.random.fold_in(jax.random.fold_in(own_key, 6), position), (shards_of,), jnp.float32, least / len(shards), high / len(shards))
        loudness = loudness * jnp.repeat(jnp.exp(steps), extent[position] // shards_of).reshape((-1,) + (1,) * (len(extent) - 1 - position))
    return loudness


def gaussian(rng, extent, width, limit, cuts=(), kind=jnp.bfloat16):
    drawn = width * jax.random.normal(rng, extent, jnp.float32)
    if cuts:
        drawn = drawn * block_levels(rng, extent, cuts, -0.22, 0.18)
    return jnp.clip(drawn, -limit, limit).astype(kind)


def setup_inputs(seed: int = 0) -> dict:
    splits = jax.random.split(jax.random.key(seed), 11)
    return {
        "student_in": gaussian(splits[0], (TOKENS, D_S), 1.0, 6.0, ((0, 4),)),
        "norm_gain": jnp.clip(1.0 + 0.18 * jax.random.normal(splits[1], (D_S,), jnp.float32), 0.1, 1.9),
        "gate_weight": gaussian(splits[2], (D_S, FF_S), D_S ** -0.5, 0.09375, ((1, 8),)),
        "up_weight": gaussian(splits[3], (D_S, FF_S), D_S ** -0.5, 0.09375, ((1, 8),)),
        "down_weight": gaussian(splits[4], (FF_S, D_S), FF_S ** -0.5, 0.0625, ((0, 8),)),
        "projection": gaussian(splits[5], (D_S, N_WID, TW), D_S ** -0.5, 0.09375, ((2, 8),)),
        "teacher_in": gaussian(splits[6], (TOKENS, D_T), 1.0, 6.0, ((1, 4),)),
        "teacher_gate": gaussian(splits[7], (D_T, FF_T), D_T ** -0.5, 0.0625, ((0, 4), (1, 8))),
        "teacher_up": gaussian(splits[8], (D_T, FF_T), D_T ** -0.5, 0.0625, ((0, 4), (1, 8))),
        "teacher_down": gaussian(splits[9], (FF_T, D_T), FF_T ** -0.5, 0.046875, ((0, 8), (1, 4))),
    }


def reference(student_in, norm_gain, gate_weight, up_weight, down_weight, projection, teacher_in, teacher_gate, teacher_up, teacher_down):
    f32 = jnp.float32
    bf16 = jnp.bfloat16
    teacher_gate_sum = jnp.dot(teacher_in, teacher_gate, preferred_element_type=f32)
    teacher_up_sum = jnp.dot(teacher_in, teacher_up, preferred_element_type=f32)
    teacher_hidden = (teacher_gate_sum * jax.nn.sigmoid(teacher_gate_sum) * teacher_up_sum).astype(bf16)
    target = jnp.dot(teacher_hidden, teacher_down, preferred_element_type=f32).astype(bf16)
    inputs = student_in.astype(f32)
    inverse_rms = lax.rsqrt(lax.optimization_barrier(jnp.mean(inputs * inputs, axis=-1, keepdims=True)) + 1e-05)
    normed = (inputs * inverse_rms * norm_gain).astype(bf16)
    gate = jnp.dot(normed, gate_weight, preferred_element_type=f32)
    up_sum = jnp.dot(normed, up_weight, preferred_element_type=f32)
    sigma = jax.nn.sigmoid(gate)
    hidden = (gate * sigma * up_sum).astype(bf16)
    branch = jnp.dot(hidden, down_weight, preferred_element_type=f32)
    summed = (inputs + branch).astype(bf16)
    proj_matrix = projection.reshape(D_S, D_T)
    features = jnp.dot(summed, proj_matrix, preferred_element_type=f32)
    feature_error = ((features - target.astype(f32)) / math.sqrt(TOKENS)).astype(bf16)
    feature_grad = jnp.dot(feature_error, proj_matrix.T, preferred_element_type=f32)
    branch_grad = feature_grad.astype(bf16)
    hidden_grad = jnp.dot(branch_grad, down_weight.T, preferred_element_type=f32)
    gate_grad = (hidden_grad * up_sum * sigma * (1.0 + gate * (1.0 - sigma))).astype(bf16)
    up_grad = (hidden_grad * gate * sigma).astype(bf16)
    normed_grad = jnp.dot(gate_grad, gate_weight.T, preferred_element_type=f32) + jnp.dot(up_grad, up_weight.T, preferred_element_type=f32)
    scaled = normed_grad * norm_gain
    moment = lax.optimization_barrier(jnp.mean(scaled * inputs, axis=-1, keepdims=True))
    input_grad = feature_grad + inverse_rms * (scaled - inputs * inverse_rms * inverse_rms * moment)
    grad_gate = jnp.dot(normed.T, gate_grad, preferred_element_type=f32).astype(bf16)
    grad_up = jnp.dot(normed.T, up_grad, preferred_element_type=f32).astype(bf16)
    grad_down = jnp.dot(hidden.T, branch_grad, preferred_element_type=f32).astype(bf16)
    grad_proj = jnp.dot(summed.T, feature_error, preferred_element_type=f32).astype(bf16).reshape(D_S, N_WID, TW)
    return (grad_gate, grad_up, grad_down, grad_proj, input_grad)
```

```python
import math

import jax
import jax.numpy as jnp
from jax import lax
from jax.sharding import PartitionSpec as P

F32 = jnp.float32
BF16 = jnp.bfloat16
CORES = 2


def dot(a, b):
    return jnp.dot(a, b, preferred_element_type=F32)


def shift(x, axis, step):
    size = lax.axis_size(axis)
    return lax.ppermute(x, axis, [(i, (i + step) % size) for i in range(size)])


class Wid:
    def __init__(self):
        self.size = lax.axis_size("wid")
        self.cores = CORES if self.size % CORES == 0 else 1
        self.rows = self.size // self.cores
        self.index = lax.axis_index("wid")
        self.row = self.index // self.cores
        self.core = self.index % self.cores

    def at(self, drow, dcore):
        return ((self.row + drow) % self.rows) * self.cores + (self.core + dcore) % self.cores

    def send(self, x, drow, dcore):
        pairs = []
        for i in range(self.size):
            row, core = i // self.cores, i % self.cores
            pairs.append((i, ((row + drow) % self.rows) * self.cores + (core + dcore) % self.cores))
        return lax.ppermute(x, "wid", pairs)

    def gather(self, x):
        blocks = []
        for drow in range(self.rows):
            mine = x if drow == 0 else self.send(x, -drow, 0)
            blocks.append([mine] + [self.send(mine, 0, -dcore) for dcore in range(1, self.cores)])
        return blocks

    def swap(self, x):
        cols = x.shape[1] // self.size
        blocks = []
        for drow in range(self.rows):
            group = []
            for dcore in range(self.cores):
                block = lax.dynamic_slice_in_dim(x, self.at(-drow, -dcore) * cols, cols, 1)
                group.append(block if drow + dcore == 0 else self.send(block, -drow, -dcore))
            blocks.append(group)
        return blocks


def flat(blocks):
    return [b for group in blocks for b in group]


def scatter_sum(x):
    ngrp, nhid = lax.axis_size("grp"), lax.axis_size("hid")
    g, h = lax.axis_index("grp"), lax.axis_index("hid")
    cols = x.shape[1] // (ngrp * nhid)

    def block(dg, dh):
        return lax.dynamic_slice_in_dim(x, (((g + dg) % ngrp) * nhid + (h + dh) % nhid) * cols, cols, 1)

    total = None
    for dh in list(range(1, nhid)) + [0]:
        got = [shift(block(dg, dh), "grp", dg) for dg in range(1, ngrp)]
        part = block(0, dh).astype(F32)
        for r in got:
            part = part + r.astype(F32)
        if dh == 0:
            total = part if total is None else total + part
        else:
            r = shift(part.astype(BF16), "hid", dh).astype(F32)
            total = r if total is None else total + r
    return total


def gather_cols(x):
    ngrp, nhid = lax.axis_size("grp"), lax.axis_size("hid")
    g, h = lax.axis_index("grp"), lax.axis_index("hid")
    cols = x.shape[1]
    out = jnp.zeros((x.shape[0], cols * ngrp * nhid), x.dtype)
    for dh in range(nhid):
        mine = x if dh == 0 else shift(x, "hid", dh)
        for dg in range(ngrp):
            piece = mine if dg == 0 else shift(mine, "grp", dg)
            place = ((g - dg) % ngrp) * nhid + (h - dh) % nhid
            out = lax.dynamic_update_slice_in_dim(out, piece, place * cols, 1)
    return out


def shards(
    student_in,
    norm_gain,
    gate_weight,
    up_weight,
    down_weight,
    projection,
    teacher_in,
    teacher_gate,
    teacher_up,
    teacher_down,
):
    wid = Wid()
    tokens = student_in.shape[0]
    width = student_in.shape[1]
    total_tokens = tokens * wid.size
    hidden_cols = gate_weight.shape[1]

    groups = []
    for dcore in range(wid.cores):
        groups.append(
            jnp.concatenate(
                [
                    lax.dynamic_slice_in_dim(teacher_in, wid.at(drow, dcore) * tokens, tokens, 0)
                    for drow in range(wid.rows)
                ],
                axis=0,
            )
        )
    units = teacher_gate.shape[1]
    chunks = 2 if units % 256 == 0 else 1
    size = units // chunks
    feature_parts = [None] * wid.rows
    for k in range(chunks):
        sums = []
        for weight in (teacher_gate, teacher_up):
            part = weight[:, k * size : (k + 1) * size]
            got = [
                wid.send(dot(groups[dcore], part).astype(BF16), 0, dcore)
                for dcore in range(1, wid.cores)
            ]
            own = dot(groups[0], part)
            for r in got:
                own = own + r.astype(F32)
            rows = own[:tokens]
            for drow in range(1, wid.rows):
                sent = own[drow * tokens : (drow + 1) * tokens].astype(BF16)
                rows = rows + wid.send(sent, drow, 0).astype(F32)
            sums.append(rows)
        gate_rows, up_rows = sums
        teacher_hidden = (gate_rows * jax.nn.sigmoid(gate_rows) * up_rows).astype(BF16)
        down = teacher_down[k * size : (k + 1) * size]
        for drow, group in enumerate(wid.gather(teacher_hidden)):
            part = dot(jnp.concatenate(group, axis=0), down)
            feature_parts[drow] = part if feature_parts[drow] is None else feature_parts[drow] + part

    inputs = student_in.astype(F32)
    inverse_rms = lax.rsqrt(jnp.mean(inputs * inputs, axis=-1, keepdims=True) + 1e-05)
    normed = (inputs * inverse_rms * norm_gain).astype(BF16)
    gate_sum = dot(normed, gate_weight)
    up_sum = dot(normed, up_weight)
    sigma = jax.nn.sigmoid(gate_sum)
    hidden = (gate_sum * sigma * up_sum).astype(BF16)
    branch = scatter_sum(dot(hidden, down_weight).astype(BF16)).astype(BF16)
    summed = (inputs + gather_cols(branch).astype(F32)).astype(BF16)
    proj_local = projection.reshape(width, -1)
    features = dot(summed, proj_local)

    share = projection.shape[2]
    target = jnp.zeros((tokens, wid.size * share), BF16)
    for drow in range(wid.rows):
        cols = scatter_sum(feature_parts[drow].astype(BF16)).astype(BF16)
        for dcore in range(wid.cores):
            block = cols[dcore * tokens : (dcore + 1) * tokens]
            if drow + dcore:
                block = wid.send(block, drow, dcore)
            target = lax.dynamic_update_slice_in_dim(target, block, wid.at(-drow, -dcore) * share, 1)

    feature_error = ((features - target.astype(F32)) / math.sqrt(total_tokens)).astype(BF16)
    feature_share = scatter_sum(dot(feature_error, proj_local.T).astype(BF16))
    branch_grad = gather_cols(feature_share.astype(BF16))
    hidden_grad = dot(branch_grad, down_weight.T)
    gate_grad = (hidden_grad * up_sum * sigma * (1.0 + gate_sum * (1.0 - sigma))).astype(BF16)
    up_grad = (hidden_grad * gate_sum * sigma).astype(BF16)
    moment = lax.psum(
        jnp.sum(
            gate_grad.astype(F32) * gate_sum + up_grad.astype(F32) * up_sum, axis=-1, keepdims=True
        ),
        ("grp", "hid"),
    )
    normed_grad = dot(gate_grad, gate_weight.T) + dot(up_grad, up_weight.T)
    normed_share = scatter_sum(normed_grad.astype(BF16))
    share_cols = normed_share.shape[1]
    offset = lax.axis_index(("grp", "hid")) * share_cols
    gain_share = lax.dynamic_slice_in_dim(norm_gain, offset, share_cols, 0)
    inputs_share = lax.dynamic_slice_in_dim(student_in, offset, share_cols, 1).astype(F32)
    input_grad = feature_share + inverse_rms * (
        normed_share * gain_share - inputs_share * inverse_rms * (moment / width)
    )

    def columns(x):
        return jnp.concatenate(flat(wid.swap(x)), axis=0)

    def everyone(x):
        return jnp.concatenate(flat(wid.gather(x)), axis=0)

    normed_cols = columns(normed)
    grad_proj = dot(columns(summed).T, everyone(feature_error)).astype(BF16)
    grad_proj = grad_proj.reshape(-1, wid.size, share)
    grad_down = dot(everyone(hidden).T, columns(branch_grad)).astype(BF16)
    grad_gate = dot(normed_cols.T, everyone(gate_grad)).astype(BF16)
    grad_up = dot(normed_cols.T, everyone(up_grad)).astype(BF16)
    return (grad_gate, grad_up, grad_down, grad_proj, input_grad)


def solution(mesh):
    in_specs = (
        P("wid", None),
        P(),
        P(None, ("grp", "hid")),
        P(None, ("grp", "hid")),
        P(("grp", "hid"), None),
        P(None, None, ("grp", "hid")),
        P(None, "wid"),
        P("wid", ("grp", "hid")),
        P("wid", ("grp", "hid")),
        P(("grp", "hid"), "wid"),
    )
    out_specs = (
        P("wid", ("grp", "hid")),
        P("wid", ("grp", "hid")),
        P(("grp", "hid"), "wid"),
        P("wid", None, ("grp", "hid")),
        P("wid", ("grp", "hid")),
    )
    return jax.shard_map(shards, mesh=mesh, in_specs=in_specs, out_specs=out_specs, check_vma=False)
```

```python
import functools
import math

import jax
import jax.numpy as jnp
from jax import lax
from jax.experimental import pallas as pl
from jax.experimental.pallas import tpu as pltpu
from jax.sharding import PartitionSpec as P

F32 = jnp.float32
BF16 = jnp.bfloat16
CORES = 2
MIB = 1 << 20

ANY = pl.BlockSpec(memory_space=pl.ANY)
VMEM = pl.BlockSpec(memory_space=pltpu.VMEM)
SMEM = pl.BlockSpec(memory_space=pltpu.SMEM)


def dot(a, b):
    return jnp.dot(a, b, preferred_element_type=F32)


def dot_t(a, b):
    return lax.dot_general(a, b, (((1,), (1,)), ((), ())), preferred_element_type=F32)


def call(body, out_shape, in_specs, scratch, limit, flops, moved, name):
    return pl.pallas_call(
        body,
        out_shape=out_shape,
        in_specs=in_specs,
        out_specs=jax.tree.map(lambda _: VMEM, out_shape),
        scratch_shapes=scratch,
        compiler_params=pltpu.CompilerParams(vmem_limit_bytes=limit),
        cost_estimate=pl.CostEstimate(flops=flops, bytes_accessed=moved, transcendentals=0),
        name=name,
    )


def struct(shape, dtype):
    return jax.ShapeDtypeStruct(tuple(shape), dtype)


def aligned(position, size):
    return pl.ds(pl.multiple_of(position * size, size), size)


def shift(x, axis, step):
    size = lax.axis_size(axis)
    return lax.ppermute(x, axis, [(i, (i + step) % size) for i in range(size)])


class Wid:
    def __init__(self):
        self.size = lax.axis_size("wid")
        self.cores = CORES if self.size % CORES == 0 else 1
        self.rows = self.size // self.cores
        self.index = lax.axis_index("wid")
        self.row = self.index // self.cores
        self.core = self.index % self.cores

    def at(self, drow, dcore):
        return ((self.row + drow) % self.rows) * self.cores + (self.core + dcore) % self.cores

    def send(self, x, drow, dcore):
        pairs = []
        for i in range(self.size):
            row, core = i // self.cores, i % self.cores
            pairs.append((i, ((row + drow) % self.rows) * self.cores + (core + dcore) % self.cores))
        return lax.ppermute(x, "wid", pairs)

    def gather(self, x):
        blocks = []
        for drow in range(self.rows):
            mine = x if drow == 0 else self.send(x, -drow, 0)
            blocks.append([mine] + [self.send(mine, 0, -dcore) for dcore in range(1, self.cores)])
        return blocks

    def swap(self, x):
        cols = x.shape[1] // self.size
        blocks = []
        for drow in range(self.rows):
            group = []
            for dcore in range(self.cores):
                block = lax.dynamic_slice_in_dim(x, self.at(-drow, -dcore) * cols, cols, 1)
                group.append(block if drow + dcore == 0 else self.send(block, -drow, -dcore))
            blocks.append(group)
        return blocks


def flat(blocks):
    return [b for group in blocks for b in group]


class Plane:
    def __init__(self):
        self.ngrp, self.nhid = lax.axis_size("grp"), lax.axis_size("hid")
        self.size = self.ngrp * self.nhid
        self.g, self.h = lax.axis_index("grp"), lax.axis_index("hid")
        self.index = self.g * self.nhid + self.h
        steps = [(dg, dh) for dg in range(self.ngrp) for dh in range(self.nhid)]
        self.to = jnp.stack([self.place(dg, dh) for dg, dh in steps]).astype(jnp.int32)
        self.source = jnp.stack([self.place(-dg, -dh) for dg, dh in steps]).astype(jnp.int32)

    def place(self, dg, dh):
        return ((self.g + dg) % self.ngrp) * self.nhid + (self.h + dh) % self.nhid

    def split(self, x):
        cols = x.shape[1] // self.size
        return [
            lax.dynamic_slice_in_dim(x, self.place(dg, dh) * cols, cols, 1)
            for dg in range(self.ngrp)
            for dh in range(self.nhid)
        ]

    def scatter_sum(self, blocks):
        terms = None
        sums = []
        for dh in list(range(1, self.nhid)) + [0]:
            own = blocks[dh]
            got = [shift(blocks[dg * self.nhid + dh], "grp", dg) for dg in range(1, self.ngrp)]
            if dh:
                sums.append(shift(add(own, *got), "hid", dh))
            else:
                terms = [own] + got
        total = terms[0].astype(F32)
        for term in terms[1:] + sums:
            total = total + term.astype(F32)
        return total

    def gather(self, x):
        blocks = [None] * self.size
        for dh in range(self.nhid):
            mine = x if dh == 0 else shift(x, "hid", dh)
            for dg in range(self.ngrp):
                blocks[dg * self.nhid + dh] = mine if dg == 0 else shift(mine, "grp", dg)
        return blocks

    def total(self, x):
        for axis, size in (("grp", self.ngrp), ("hid", self.nhid)):
            x = sum([shift(x, axis, step) for step in range(1, size)], x)
        return x


def add(*blocks):
    def body(*refs):
        total = refs[0][...].astype(F32)
        for ref in refs[1:-1]:
            total = total + ref[...].astype(F32)
        refs[-1][...] = total.astype(BF16)

    x = blocks[0]
    return call(
        body, struct(x.shape, BF16), [VMEM] * len(blocks), [], 16 * MIB,
        x.size, 2 * x.size * (len(blocks) + 1), "add_blocks",
    )(*blocks)


def teacher_sums(wid, rows_at, teacher_in, weights, first, tiles, tile, after):
    total, depth = teacher_in.shape
    tokens = total // wid.size
    cols = tiles * tile
    held = wid.rows * tokens

    def body(at, x, gate, up, *refs):
        outs = refs[len(after) : len(after) + wid.cores]
        ordered, buf, sems = refs[len(after) + wid.cores :]

        def copy(i, t):
            source = (gate, up)[i].at[:, pl.ds(first + t * tile, tile)]
            return pltpu.make_async_copy(source, buf.at[i, t], sems.at[i, t])

        for t in range(tiles):
            for i in range(2):
                copy(i, t).start()
        for r in range(wid.size):
            ordered[r * tokens : (r + 1) * tokens, :] = x[aligned(at[r], tokens), :]
        for t in range(tiles):
            for i in range(2):
                copy(i, t).wait()
                part = dot(ordered[...], buf[i, t])
                for c in range(wid.cores):
                    out = outs[c]
                    out[i, :, t * tile : (t + 1) * tile] = part[c * held : (c + 1) * held].astype(out.dtype)

    out_shape = [struct((2, held, cols), F32 if c == 0 else BF16) for c in range(wid.cores)]
    return call(
        body, out_shape, [SMEM, VMEM, ANY, ANY] + [ANY] * len(after),
        [
            pltpu.VMEM((total, depth), BF16),
            pltpu.VMEM((2, tiles, depth, tile), BF16),
            pltpu.SemaphoreType.DMA((2, tiles)),
        ],
        40 * MIB, 4 * total * depth * cols, 4 * depth * cols, "teacher_sums",
    )(rows_at, teacher_in, *weights, *after)


def expand(at, pieces, weight, name):
    depth, width = weight.shape
    count = at.shape[0]
    cols = width // count
    rows = [row[0].shape[0] for row in pieces]
    total = sum(rows)
    number = sum(len(row) for row in pieces)
    x = flat(pieces)

    def body(where, *refs):
        ins, w, outs = refs[:number], refs[number], refs[number + 1 : number + 1 + count]
        whole, buf, sems = refs[number + 1 + count :]

        def copy(r):
            return pltpu.make_async_copy(w.at[:, aligned(where[r], cols)], buf.at[r], sems.at[r])

        for r in range(count):
            copy(r).start()
        n = row = 0
        for i, parts in enumerate(pieces):
            col = 0
            for part in parts:
                whole[row : row + rows[i], col : col + part.shape[1]] = ins[n][...]
                col += part.shape[1]
                n += 1
            row += rows[i]
        for r in range(count):
            copy(r).wait()
            outs[r][...] = dot(whole[...], buf[r]).astype(BF16)

    return call(
        body, [struct((total, cols), BF16)] * count, [SMEM] + [VMEM] * number + [ANY],
        [
            pltpu.VMEM((total, depth), BF16),
            pltpu.VMEM((count, depth, cols), BF16),
            pltpu.SemaphoreType.DMA((count,)),
        ],
        32 * MIB, 2 * total * depth * width, 2 * depth * width, name,
    )(at, *x, weight)


def student_hidden(student_in, norm_gain, gate_weight, up_weight, after):
    tokens, width = student_in.shape
    cols = gate_weight.shape[1]
    count = 8
    deep = width // count

    def body(x, gain, wg, wu, *refs):
        normed, inverse, gate, up, hidden = refs[len(after) : len(after) + 5]
        buf, sems = refs[len(after) + 5 :]

        def copy(i, k):
            return pltpu.make_async_copy(
                (wg, wu)[i].at[pl.ds(k * deep, deep), :], buf.at[i, k], sems.at[i, k]
            )

        for k in range(count):
            for i in range(2):
                copy(i, k).start()
        values = x[...].astype(F32)
        inv = lax.rsqrt(jnp.sum(values * values, axis=-1, keepdims=True) / width + 1e-05)
        inverse[...] = inv
        normed[...] = (values * inv * gain[...]).astype(BF16)
        sums = [None, None]
        for k in range(count):
            for i in range(2):
                copy(i, k).wait()
                part = dot(normed[:, k * deep : (k + 1) * deep], buf[i, k])
                sums[i] = part if k == 0 else sums[i] + part
        gate[...] = sums[0]
        up[...] = sums[1]
        hidden[...] = (sums[0] * jax.nn.sigmoid(sums[0]) * sums[1]).astype(BF16)

    return call(
        body,
        [
            struct((tokens, width), BF16),
            struct((tokens, 1), F32),
            struct((tokens, cols), F32),
            struct((tokens, cols), F32),
            struct((tokens, cols), BF16),
        ],
        [VMEM, VMEM, ANY, ANY] + [ANY] * len(after),
        [pltpu.VMEM((2, count, deep, cols), BF16), pltpu.SemaphoreType.DMA((2, count))],
        40 * MIB, 4 * tokens * width * cols, 4 * width * cols, "student_hidden",
    )(student_in, norm_gain.reshape(1, width), gate_weight, up_weight, *after)


def student_features(at, branch, student_in, matrix):
    tokens, width = student_in.shape
    count = len(branch)
    cols = width // count
    out_cols = matrix.shape[1]

    def body(where, x, *refs):
        pieces, w = refs[:count], refs[count]
        summed, features, buf, sems = refs[count + 1 :]

        def copy(r):
            return pltpu.make_async_copy(w.at[aligned(where[r], cols), :], buf.at[r], sems.at[r])

        for r in range(count):
            copy(r).start()
        total = None
        for r in range(count):
            place = aligned(where[r], cols)
            block = (x[:, place].astype(F32) + pieces[r][...].astype(F32)).astype(BF16)
            summed[:, place] = block
            copy(r).wait()
            part = dot(block, buf[r])
            total = part if total is None else total + part
        features[...] = total

    return call(
        body, [struct((tokens, width), BF16), struct((tokens, out_cols), F32)],
        [SMEM, VMEM] + [VMEM] * count + [ANY],
        [pltpu.VMEM((count, cols, out_cols), BF16), pltpu.SemaphoreType.DMA((count,))],
        32 * MIB, 2 * tokens * width * out_cols, 2 * width * out_cols, "student_features",
    )(at, student_in, *branch, matrix)


def error_grad(to, order, target, features, matrix, scale):
    tokens, out_cols = features.shape
    width = matrix.shape[0]
    count = to.shape[0]
    cols = width // count
    parts = len(target)
    share = out_cols // parts

    def body(where, place, *refs):
        pieces, feats, w = refs[:parts], refs[parts], refs[parts + 1]
        error, outs = refs[parts + 2], refs[parts + 3 : parts + 3 + count]
        held, buf, sems = refs[parts + 3 + count :]

        def copy(r):
            return pltpu.make_async_copy(w.at[aligned(where[r], cols), :], buf.at[r], sems.at[r])

        for r in range(count):
            copy(r).start()
        for r in range(parts):
            held[place[r]] = pieces[r][...]
        for r in range(parts):
            here = slice(r * share, (r + 1) * share)
            error[:, here] = ((feats[:, here] - held[r].astype(F32)) * scale).astype(BF16)
        for r in range(count):
            copy(r).wait()
            outs[r][...] = dot_t(error[...], buf[r]).astype(BF16)

    return call(
        body, [struct((tokens, out_cols), BF16)] + [struct((tokens, cols), BF16)] * count,
        [SMEM, SMEM] + [VMEM] * (parts + 1) + [ANY],
        [
            pltpu.VMEM((parts, tokens, share), BF16),
            pltpu.VMEM((count, cols, out_cols), BF16),
            pltpu.SemaphoreType.DMA((count,)),
        ],
        32 * MIB, 2 * tokens * width * out_cols, 2 * width * out_cols, "error_grad",
    )(to, order, *target, features, matrix)


def hidden_grads(at, pieces, gate, up, weight):
    tokens, units = gate.shape
    width = weight.shape[1]
    count = len(pieces)
    cols = width // count

    def body(where, gate_ref, up_ref, *refs):
        ins, w = refs[:count], refs[count]
        branch_grad, gate_grad, up_grad, moment, buf, sems = refs[count + 1 :]

        def copy(r):
            return pltpu.make_async_copy(w.at[:, aligned(where[r], cols)], buf.at[r], sems.at[r])

        for r in range(count):
            copy(r).start()
        total = None
        for r in range(count):
            block = ins[r][...]
            branch_grad[:, aligned(where[r], cols)] = block
            copy(r).wait()
            part = dot_t(block, buf[r])
            total = part if total is None else total + part
        g, u = gate_ref[...], up_ref[...]
        sigma = jax.nn.sigmoid(g)
        dg = (total * u * sigma * (1.0 + g * (1.0 - sigma))).astype(BF16)
        du = (total * g * sigma).astype(BF16)
        gate_grad[...] = dg
        up_grad[...] = du
        moment[...] = jnp.sum(dg.astype(F32) * g + du.astype(F32) * u, axis=-1, keepdims=True)

    return call(
        body,
        [
            struct((tokens, width), BF16),
            struct((tokens, units), BF16),
            struct((tokens, units), BF16),
            struct((tokens, 1), F32),
        ],
        [SMEM, VMEM, VMEM] + [VMEM] * count + [ANY],
        [pltpu.VMEM((count, units, cols), BF16), pltpu.SemaphoreType.DMA((count,))],
        32 * MIB, 2 * tokens * width * units, 2 * width * units, "hidden_grads",
    )(at, gate, up, *pieces, weight)


def normed_grads(to, gate_grad, up_grad, gate_weight, up_weight):
    tokens, units = gate_grad.shape
    width = gate_weight.shape[0]
    count = to.shape[0]
    cols = width // count

    def body(where, dg, du, wg, wu, *refs):
        outs = refs[:count]
        buf, sems = refs[count:]

        def copy(i, r):
            return pltpu.make_async_copy(
                (wg, wu)[i].at[aligned(where[r], cols), :], buf.at[i, r], sems.at[i, r]
            )

        for r in range(count):
            for i in range(2):
                copy(i, r).start()
        for r in range(count):
            copy(0, r).wait()
            copy(1, r).wait()
            outs[r][...] = (dot_t(dg[...], buf[0, r]) + dot_t(du[...], buf[1, r])).astype(BF16)

    return call(
        body, [struct((tokens, cols), BF16)] * count, [SMEM, VMEM, VMEM, ANY, ANY],
        [pltpu.VMEM((2, count, cols, units), BF16), pltpu.SemaphoreType.DMA((2, count))],
        40 * MIB, 4 * tokens * width * units, 4 * width * units, "normed_grads",
    )(to, gate_grad, up_grad, gate_weight, up_weight)


def shards(
    student_in,
    norm_gain,
    gate_weight,
    up_weight,
    down_weight,
    projection,
    teacher_in,
    teacher_gate,
    teacher_up,
    teacher_down,
):
    wid, plane = Wid(), Plane()
    tokens, width = student_in.shape
    total_tokens = tokens * wid.size
    share = projection.shape[2]

    rows_at = jnp.stack(
        [wid.at(drow, dcore) for dcore in range(wid.cores) for drow in range(wid.rows)]
    ).astype(jnp.int32)
    units = teacher_gate.shape[1]
    tile = next((t for t in (256, 128) if units % t == 0), units // 2)
    tiles = units // tile
    chunks = [(0, tiles // 2), (tiles // 2, tiles - tiles // 2)]
    after = ()
    hidden_blocks = [[[] for _ in range(wid.cores)] for _ in range(wid.rows)]
    for first, number in chunks:
        parts = teacher_sums(
            wid, rows_at, teacher_in, (teacher_gate, teacher_up), first * tile, number, tile, after
        )
        after = (parts[0],)
        own = parts[0]
        for dcore in range(1, wid.cores):
            own = own + wid.send(parts[dcore], 0, dcore).astype(F32)
        sums = own[:, :tokens]
        for drow in range(1, wid.rows):
            sent = own[:, drow * tokens : (drow + 1) * tokens].astype(BF16)
            sums = sums + wid.send(sent, drow, 0).astype(F32)
        teacher_hidden = (sums[0] * jax.nn.sigmoid(sums[0]) * sums[1]).astype(BF16)
        for drow, group in enumerate(wid.gather(teacher_hidden)):
            for dcore, block in enumerate(group):
                hidden_blocks[drow][dcore].append(block)

    normed, inverse_rms, gate_sum, up_sum, hidden = student_hidden(
        student_in, norm_gain, gate_weight, up_weight, after
    )
    branch = plane.scatter_sum(expand(plane.to, [[hidden]], down_weight, "student_down")).astype(BF16)
    matrix = projection.reshape(width, -1)
    summed, features = student_features(plane.source, plane.gather(branch), student_in, matrix)

    target, order = [], []
    for drow in range(wid.rows):
        if share % 128 == 0:
            blocks = expand(plane.to, hidden_blocks[drow], teacher_down, "teacher_down")
        else:
            rows = [jnp.concatenate(row, axis=1) for row in hidden_blocks[drow]]
            blocks = plane.split(dot(jnp.concatenate(rows, axis=0), teacher_down).astype(BF16))
        cols = plane.scatter_sum(blocks).astype(BF16)
        for dcore in range(wid.cores):
            block = cols[dcore * tokens : (dcore + 1) * tokens]
            target.append(wid.send(block, drow, dcore) if drow + dcore else block)
            order.append(wid.at(-drow, -dcore))
    order = jnp.stack(order).astype(jnp.int32)

    feature_error, *blocks = error_grad(
        plane.to, order, target, features, matrix, 1.0 / math.sqrt(total_tokens)
    )
    feature_share = plane.scatter_sum(blocks)
    branch_grad, gate_grad, up_grad, moment = hidden_grads(
        plane.source, plane.gather(feature_share.astype(BF16)), gate_sum, up_sum, down_weight
    )
    moment = plane.total(moment)
    normed_share = plane.scatter_sum(normed_grads(plane.to, gate_grad, up_grad, gate_weight, up_weight))
    share_cols = normed_share.shape[1]
    offset = plane.index * share_cols
    gain_share = lax.dynamic_slice_in_dim(norm_gain, offset, share_cols, 0)
    inputs_share = lax.dynamic_slice_in_dim(student_in, offset, share_cols, 1).astype(F32)
    input_grad = feature_share + inverse_rms * (
        normed_share * gain_share - inputs_share * inverse_rms * (moment / width)
    )

    def columns(x):
        return jnp.concatenate(flat(wid.swap(x)), axis=0)

    def everyone(x):
        return jnp.concatenate(flat(wid.gather(x)), axis=0)

    normed_cols = columns(normed)
    grad_proj = dot(columns(summed).T, everyone(feature_error)).astype(BF16)
    grad_proj = grad_proj.reshape(-1, wid.size, share)
    grad_down = dot(everyone(hidden).T, columns(branch_grad)).astype(BF16)
    grad_gate = dot(normed_cols.T, everyone(gate_grad)).astype(BF16)
    grad_up = dot(normed_cols.T, everyone(up_grad)).astype(BF16)
    return (grad_gate, grad_up, grad_down, grad_proj, input_grad)


def solution(mesh):
    in_specs = (
        P("wid", None),
        P(),
        P(None, ("grp", "hid")),
        P(None, ("grp", "hid")),
        P(("grp", "hid"), None),
        P(None, None, ("grp", "hid")),
        P(None, "wid"),
        P("wid", ("grp", "hid")),
        P("wid", ("grp", "hid")),
        P(("grp", "hid"), "wid"),
    )
    out_specs = (
        P("wid", ("grp", "hid")),
        P("wid", ("grp", "hid")),
        P(("grp", "hid"), "wid"),
        P("wid", None, ("grp", "hid")),
        P("wid", ("grp", "hid")),
    )
    return jax.shard_map(shards, mesh=mesh, in_specs=in_specs, out_specs=out_specs, check_vma=False)
```

```python
import functools
import math

import jax
import jax.numpy as jnp
from jax import lax
from jax.experimental import pallas as pl
from jax.experimental.pallas import tpu as pltpu
from jax.sharding import PartitionSpec as P

F32 = jnp.float32
BF16 = jnp.bfloat16
CORES = 2
MIB = 1 << 20

ANY = pl.BlockSpec(memory_space=pl.ANY)
VMEM = pl.BlockSpec(memory_space=pltpu.VMEM)
SMEM = pl.BlockSpec(memory_space=pltpu.SMEM)


def dot(a, b):
    return jnp.dot(a, b, preferred_element_type=F32)


def dot_t(a, b):
    return lax.dot_general(a, b, (((1,), (1,)), ((), ())), preferred_element_type=F32)


def call(body, out_shape, in_specs, scratch, flops, moved, name):
    return pl.pallas_call(
        body,
        out_shape=out_shape,
        in_specs=in_specs,
        out_specs=jax.tree.map(lambda _: VMEM, out_shape),
        scratch_shapes=scratch,
        compiler_params=pltpu.CompilerParams(vmem_limit_bytes=60 * MIB),
        cost_estimate=pl.CostEstimate(flops=flops, bytes_accessed=moved, transcendentals=0),
        name=name,
    )


def struct(shape, dtype):
    return jax.ShapeDtypeStruct(tuple(shape), dtype)


def aligned(position, size):
    return pl.ds(pl.multiple_of(position * size, size), size)


def shift(x, axis, step):
    size = lax.axis_size(axis)
    return lax.ppermute(x, axis, [(i, (i + step) % size) for i in range(size)])


class Wid:
    def __init__(self):
        self.size = lax.axis_size("wid")
        self.cores = CORES if self.size % CORES == 0 else 1
        self.rows = self.size // self.cores
        self.index = lax.axis_index("wid")
        self.row = self.index // self.cores
        self.core = self.index % self.cores

    def at(self, drow, dcore):
        return ((self.row + drow) % self.rows) * self.cores + (self.core + dcore) % self.cores

    def send(self, x, drow, dcore):
        pairs = []
        for i in range(self.size):
            row, core = i // self.cores, i % self.cores
            pairs.append((i, ((row + drow) % self.rows) * self.cores + (core + dcore) % self.cores))
        return lax.ppermute(x, "wid", pairs)

    def gather(self, x):
        blocks = []
        for drow in range(self.rows):
            mine = x if drow == 0 else self.send(x, -drow, 0)
            blocks.append([mine] + [self.send(mine, 0, -dcore) for dcore in range(1, self.cores)])
        return blocks


def flat(blocks):
    return [b for group in blocks for b in group]


class Plane:
    def __init__(self):
        self.ngrp, self.nhid = lax.axis_size("grp"), lax.axis_size("hid")
        self.size = self.ngrp * self.nhid
        self.g, self.h = lax.axis_index("grp"), lax.axis_index("hid")
        self.index = self.g * self.nhid + self.h
        steps = [(dg, dh) for dg in range(self.ngrp) for dh in range(self.nhid)]
        self.to = jnp.stack([self.place(dg, dh) for dg, dh in steps]).astype(jnp.int32)
        self.source = jnp.stack([self.place(-dg, -dh) for dg, dh in steps]).astype(jnp.int32)

    def place(self, dg, dh):
        return ((self.g + dg) % self.ngrp) * self.nhid + (self.h + dh) % self.nhid

    def split(self, x):
        cols = x.shape[1] // self.size
        return [
            lax.dynamic_slice_in_dim(x, self.place(dg, dh) * cols, cols, 1)
            for dg in range(self.ngrp)
            for dh in range(self.nhid)
        ]

    def scatter_sum(self, blocks):
        terms = None
        sums = []
        for dh in list(range(1, self.nhid)) + [0]:
            own = blocks[dh]
            got = [shift(blocks[dg * self.nhid + dh], "grp", dg) for dg in range(1, self.ngrp)]
            if dh:
                sums.append(shift(add(own, *got), "hid", dh))
            else:
                terms = [own] + got
        total = terms[0].astype(F32)
        for term in terms[1:] + sums:
            total = total + term.astype(F32)
        return total

    def gather(self, x):
        blocks = [None] * self.size
        for dh in range(self.nhid):
            mine = x if dh == 0 else shift(x, "hid", dh)
            for dg in range(self.ngrp):
                blocks[dg * self.nhid + dh] = mine if dg == 0 else shift(mine, "grp", dg)
        return blocks

    def total(self, x):
        for axis, size in (("grp", self.ngrp), ("hid", self.nhid)):
            x = sum([shift(x, axis, step) for step in range(1, size)], x)
        return x


def add(*blocks):
    def body(*refs):
        total = refs[0][...].astype(F32)
        for ref in refs[1:-1]:
            total = total + ref[...].astype(F32)
        refs[-1][...] = total.astype(BF16)

    x = blocks[0]
    return call(
        body, struct(x.shape, BF16), [VMEM] * len(blocks), [],
        x.size, 2 * x.size * (len(blocks) + 1), "add_blocks",
    )(*blocks)


def cut(at, x, whole, after):
    tokens, width = x.shape
    count = at.shape[0]
    cols = width // count

    def body(where, x_ref, *refs):
        outs = refs[len(whole) + len(after) :]
        for r in range(count):
            outs[r][...] = x_ref[:, aligned(where[r], cols)]
        for i in range(len(whole)):
            outs[count + i][...] = refs[i][...]

    out = call(
        body,
        [struct((tokens, cols), x.dtype)] * count + [struct(y.shape, y.dtype) for y in whole],
        [SMEM, VMEM] + [VMEM] * len(whole) + [ANY] * len(after), [],
        x.size, 4 * x.size, "cut",
    )(at, x, *whole, *after)
    return out[:count], out[count:]


def teacher_sums(wid, rows_at, teacher_in, weights, first, cols, after):
    total, depth = teacher_in.shape
    tokens = total // wid.size
    held = wid.rows * tokens
    pieces = 4
    deep = depth // pieces

    def body(at, x, gate, up, *refs):
        outs = refs[len(after) : len(after) + wid.rows + wid.cores - 1]
        ordered, buf, x_sems, sems = refs[len(after) + len(outs) :]

        def rows(r):
            return pltpu.make_async_copy(
                x.at[aligned(at[r], tokens), :], ordered.at[pl.ds(r * tokens, tokens), :], x_sems.at[r]
            )

        def copy(i, k):
            here = pl.ds(k * deep, deep)
            return pltpu.make_async_copy(
                (gate, up)[i].at[here, pl.ds(first, cols)], buf.at[i, here, :], sems.at[i, k]
            )

        for r in range(wid.size):
            rows(r).start()
        for i in range(2):
            for k in range(pieces):
                copy(i, k).start()
        for r in range(wid.size):
            rows(r).wait()
        for i in range(2):
            for k in range(pieces):
                copy(i, k).wait()
            part = dot(ordered[...], buf[i])
            for r in range(wid.rows):
                outs[r][i] = part[r * tokens : (r + 1) * tokens]
            for c in range(1, wid.cores):
                outs[wid.rows + c - 1][i] = part[c * held : (c + 1) * held].astype(BF16)

    return call(
        body,
        [struct((2, tokens, cols), F32)] * wid.rows + [struct((2, held, cols), BF16)] * (wid.cores - 1),
        [SMEM, ANY, ANY, ANY] + [ANY] * len(after),
        [
            pltpu.VMEM((total, depth), BF16),
            pltpu.VMEM((2, depth, cols), BF16),
            pltpu.SemaphoreType.DMA((wid.size,)),
            pltpu.SemaphoreType.DMA((2, pieces)),
        ],
        4 * total * depth * cols, 4 * depth * cols, "teacher_sums",
    )(rows_at, teacher_in, *weights, *after)


def teacher_down_part(where, group, pieces, weight, after):
    depth, width = weight.shape
    count = where.shape[0]
    slab = width // lax.axis_size("grp")
    cols = slab // count
    rows = [row[0].shape[0] for row in pieces]
    total = sum(rows)
    deeps = [part.shape[1] for part in pieces[0]]
    number = sum(len(row) for row in pieces)

    def body(place, g, *refs):
        ins, w = refs[:number], refs[number]
        outs = refs[number + 1 + len(after) : number + 1 + len(after) + count]
        whole, buf, result, sems = refs[number + 1 + len(after) + count :]

        def copy(k):
            here = pl.ds(sum(deeps[:k]), deeps[k])
            return pltpu.make_async_copy(
                w.at[here, aligned(g[0], slab)], buf.at[here, :], sems.at[k]
            )

        for k in range(len(deeps)):
            copy(k).start()
        n = row = 0
        for i, parts in enumerate(pieces):
            col = 0
            for part in parts:
                whole[row : row + rows[i], col : col + part.shape[1]] = ins[n][...]
                col += part.shape[1]
                n += 1
            row += rows[i]
        for k in range(len(deeps)):
            copy(k).wait()
            here = slice(sum(deeps[:k]), sum(deeps[: k + 1]))
            part = dot(whole[:, here], buf[here, :])
            result[...] = part if k == 0 else result[...] + part
        for r in range(count):
            outs[r][...] = result[:, aligned(place[r], cols)].astype(BF16)

    return call(
        body, [struct((total, cols), BF16)] * count,
        [SMEM, SMEM] + [VMEM] * number + [ANY] * (1 + len(after)),
        [
            pltpu.VMEM((total, depth), BF16),
            pltpu.VMEM((depth, slab), BF16),
            pltpu.VMEM((total, slab), F32),
            pltpu.SemaphoreType.DMA((len(deeps),)),
        ],
        2 * total * depth * slab, 2 * depth * slab, "teacher_down",
    )(where, group, *flat(pieces), weight, *after)


def student_down(at, x, weight):
    tokens, depth = x.shape
    width = weight.shape[1]
    count = at.shape[0]
    cols = width // count

    def body(where, x_ref, w, *refs):
        outs = refs[:count]
        buf, sems = refs[count:]

        def copy(r):
            return pltpu.make_async_copy(w.at[:, aligned(where[r], cols)], buf.at[r], sems.at[r])

        for r in range(count):
            copy(r).start()
        for r in range(count):
            copy(r).wait()
            outs[r][...] = dot(x_ref[...], buf[r]).astype(BF16)

    return call(
        body, [struct((tokens, cols), BF16)] * count, [SMEM, VMEM, ANY],
        [pltpu.VMEM((count, depth, cols), BF16), pltpu.SemaphoreType.DMA((count,))],
        2 * tokens * depth * width, 2 * depth * width, "student_down",
    )(at, x, weight)


def student_hidden(student_in, norm_gain, gate_weight, up_weight, after):
    tokens, width = student_in.shape
    cols = gate_weight.shape[1]
    count = 8
    deep = width // count

    def body(x, gain, wg, wu, *refs):
        normed, inverse, gate, up, hidden = refs[len(after) : len(after) + 5]
        buf, sems = refs[len(after) + 5 :]

        def copy(i, k):
            return pltpu.make_async_copy(
                (wg, wu)[i].at[pl.ds(k * deep, deep), :], buf.at[i, k], sems.at[i, k]
            )

        for k in range(count):
            for i in range(2):
                copy(i, k).start()
        values = x[...].astype(F32)
        inv = lax.rsqrt(jnp.sum(values * values, axis=-1, keepdims=True) / width + 1e-05)
        inverse[...] = inv
        normed[...] = (values * inv * gain[...]).astype(BF16)
        sums = [None, None]
        for k in range(count):
            for i in range(2):
                copy(i, k).wait()
                part = dot(normed[:, k * deep : (k + 1) * deep], buf[i, k])
                sums[i] = part if k == 0 else sums[i] + part
        gate[...] = sums[0]
        up[...] = sums[1]
        hidden[...] = (sums[0] * jax.nn.sigmoid(sums[0]) * sums[1]).astype(BF16)

    return call(
        body,
        [
            struct((tokens, width), BF16),
            struct((tokens, 1), F32),
            struct((tokens, cols), F32),
            struct((tokens, cols), F32),
            struct((tokens, cols), BF16),
        ],
        [VMEM, VMEM, ANY, ANY] + [ANY] * len(after),
        [pltpu.VMEM((2, count, deep, cols), BF16), pltpu.SemaphoreType.DMA((2, count))],
        4 * tokens * width * cols, 4 * width * cols, "student_hidden",
    )(student_in, norm_gain.reshape(1, width), gate_weight, up_weight, *after)


def student_features(at, branch, student_in, matrix):
    tokens, width = student_in.shape
    count = len(branch)
    cols = width // count
    out_cols = matrix.shape[1]

    def body(where, x, *refs):
        pieces, w = refs[:count], refs[count]
        summed, features, buf, sems = refs[count + 1 :]

        def copy(r):
            return pltpu.make_async_copy(w.at[aligned(where[r], cols), :], buf.at[r], sems.at[r])

        for r in range(count):
            copy(r).start()
        total = None
        for r in range(count):
            place = aligned(where[r], cols)
            block = (x[:, place].astype(F32) + pieces[r][...].astype(F32)).astype(BF16)
            summed[:, place] = block
            copy(r).wait()
            part = dot(block, buf[r])
            total = part if total is None else total + part
        features[...] = total

    return call(
        body, [struct((tokens, width), BF16), struct((tokens, out_cols), F32)],
        [SMEM, VMEM] + [VMEM] * count + [ANY],
        [pltpu.VMEM((count, cols, out_cols), BF16), pltpu.SemaphoreType.DMA((count,))],
        2 * tokens * width * out_cols, 2 * width * out_cols, "student_features",
    )(at, student_in, *branch, matrix)


def error_grad(to, order, target, features, matrix, scale, after):
    tokens, out_cols = features.shape
    width = matrix.shape[0]
    count = to.shape[0]
    cols = width // lax.axis_size(("grp", "hid"))
    parts = len(target)
    share = out_cols // parts

    def body(where, place, *refs):
        pieces, feats, w = refs[:parts], refs[parts], refs[parts + 1]
        refs = refs[parts + 2 + len(after) :]
        error, outs = refs[0], refs[1 : 1 + count]
        held, buf, sems = refs[1 + count :]

        def copy(r):
            return pltpu.make_async_copy(w.at[aligned(where[r], cols), :], buf.at[r], sems.at[r])

        for r in range(count):
            copy(r).start()
        for r in range(parts):
            held[place[r]] = pieces[r][...]
        for r in range(parts):
            here = slice(r * share, (r + 1) * share)
            error[:, here] = ((feats[:, here] - held[r].astype(F32)) * scale).astype(BF16)
        for r in range(count):
            copy(r).wait()
            outs[r][...] = dot_t(buf[r], error[...]).T.astype(BF16)

    return call(
        body, [struct((tokens, out_cols), BF16)] + [struct((tokens, cols), BF16)] * count,
        [SMEM, SMEM] + [VMEM] * (parts + 1) + [ANY] * (1 + len(after)),
        [
            pltpu.VMEM((parts, tokens, share), BF16),
            pltpu.VMEM((count, cols, out_cols), BF16),
            pltpu.SemaphoreType.DMA((count,)),
        ],
        2 * tokens * count * cols * out_cols, 2 * count * cols * out_cols, "error_grad",
    )(to, order, *target, features, matrix, *after)


def times_rows(to, xs, weights, name, after=()):
    tokens, depth = xs[0].shape
    width = weights[0].shape[0]
    count = to.shape[0]
    cols = width // lax.axis_size(("grp", "hid"))
    number = len(xs)

    def body(where, *refs):
        x, w = refs[:number], refs[number : 2 * number]
        refs = refs[2 * number + len(after) :]
        outs = refs[:count]
        buf, sems = refs[count:]

        def copy(i, r):
            return pltpu.make_async_copy(w[i].at[aligned(where[r], cols), :], buf.at[i, r], sems.at[i, r])

        for r in range(count):
            for i in range(number):
                copy(i, r).start()
        for r in range(count):
            total = None
            for i in range(number):
                copy(i, r).wait()
                part = dot_t(buf[i, r], x[i][...])
                total = part if i == 0 else total + part
            outs[r][...] = total.T.astype(BF16)

    return call(
        body, [struct((tokens, cols), BF16)] * count,
        [SMEM] + [VMEM] * number + [ANY] * (number + len(after)),
        [pltpu.VMEM((number, count, cols, depth), BF16), pltpu.SemaphoreType.DMA((number, count))],
        2 * number * tokens * count * cols * depth, 2 * number * count * cols * depth, name,
    )(to, *xs, *weights, *after)


def hidden_grads(at, pieces, gate, up, weight, after):
    tokens, units = gate.shape
    width = weight.shape[1]
    count = len(pieces)
    cols = width // count
    first = units // 2 // 128 * 128
    cuts = [(0, first), (first, units - first)]

    def body(where, gate_ref, up_ref, *refs):
        ins, w = refs[:count], refs[count]
        branch_grad, grads, moment, buf, sems = refs[count + 1 + len(after) :]

        def copy(k):
            here = pl.ds(*cuts[k])
            return pltpu.make_async_copy(w.at[here, :], buf.at[here, :], sems.at[k])

        for k in range(len(cuts)):
            copy(k).start()
        for r in range(count):
            branch_grad[:, aligned(where[r], cols)] = ins[r][...]
        total = None
        for k, (start, size) in enumerate(cuts):
            copy(k).wait()
            here = slice(start, start + size)
            grad = dot_t(buf[here, :], branch_grad[...]).T
            g, u = gate_ref[:, here], up_ref[:, here]
            sigma = jax.nn.sigmoid(g)
            dg = (grad * u * sigma * (1.0 + g * (1.0 - sigma))).astype(BF16)
            du = (grad * g * sigma).astype(BF16)
            grads[:, here] = dg
            grads[:, units + start : units + start + size] = du
            part = jnp.sum(dg.astype(F32) * g + du.astype(F32) * u, axis=-1, keepdims=True)
            total = part if total is None else total + part
        moment[...] = total

    return call(
        body,
        [
            struct((tokens, width), BF16),
            struct((tokens, 2 * units), BF16),
            struct((tokens, 1), F32),
        ],
        [SMEM, VMEM, VMEM] + [VMEM] * count + [ANY] * (1 + len(after)),
        [pltpu.VMEM((units, width), BF16), pltpu.SemaphoreType.DMA((len(cuts),))],
        2 * tokens * width * units, 2 * width * units, "hidden_grads",
    )(at, gate, up, *pieces, weight, *after)


def shards(
    student_in,
    norm_gain,
    gate_weight,
    up_weight,
    down_weight,
    projection,
    teacher_in,
    teacher_gate,
    teacher_up,
    teacher_down,
):
    wid, plane = Wid(), Plane()
    tokens, width = student_in.shape
    total_tokens = tokens * wid.size
    share = projection.shape[2]
    far, near = plane.to[plane.nhid :], plane.to[: plane.nhid]

    rows_at = jnp.stack(
        [wid.at(drow, dcore) for dcore in range(wid.cores) for drow in range(wid.rows)]
    ).astype(jnp.int32)
    units = teacher_gate.shape[1]
    tile = next((t for t in (256, 128) if units % t == 0), units // 2)
    first = units // tile // 2 * tile
    after = ()
    sums = []
    for start, size in ((0, first), (first, units - first)):
        parts = teacher_sums(
            wid, rows_at, teacher_in, (teacher_gate, teacher_up), start, size, after
        )
        after = (parts[0],)
        got = [wid.send(part, 0, c + 1) for c, part in enumerate(parts[wid.rows :])]
        rows = []
        for r in range(wid.rows):
            row = parts[r]
            for block in got:
                row = row + block[:, r * tokens : (r + 1) * tokens].astype(F32)
            rows.append(row if r == 0 else wid.send(row.astype(BF16), r, 0))
        sums.append(rows)

    normed, inverse_rms, gate_sum, up_sum, hidden = student_hidden(
        student_in, norm_gain, gate_weight, up_weight, after
    )
    branch_blocks = student_down(plane.to, hidden, down_weight)

    hidden_blocks = [[[] for _ in range(wid.rows)] for _ in range(wid.cores)]
    for rows in sums:
        gate_rows, up_rows = (sum([row[i].astype(F32) for row in rows[1:]], rows[0][i]) for i in range(2))
        teacher_hidden = (gate_rows * jax.nn.sigmoid(gate_rows) * up_rows).astype(BF16)
        for drow, group in enumerate(wid.gather(teacher_hidden)):
            for dcore, block in enumerate(group):
                hidden_blocks[dcore][drow].append(block)
    pieces = flat(hidden_blocks)
    places = [(drow, dcore) for dcore in range(wid.cores) for drow in range(wid.rows)]

    branch = plane.scatter_sum(branch_blocks).astype(BF16)
    branch_all = plane.gather(branch)

    if share % 128 == 0:
        blocks = []
        where = jnp.stack([(plane.h + dh) % plane.nhid for dh in range(plane.nhid)]).astype(jnp.int32)
        for dg in list(range(1, plane.ngrp)) + [0]:
            group = jnp.reshape((plane.g + dg) % plane.ngrp, (1,)).astype(jnp.int32)
            made = teacher_down_part(where, group, pieces, teacher_down, tuple(blocks[:1]))
            blocks = blocks + list(made) if dg else list(made) + blocks
    else:
        rows = [jnp.concatenate(row, axis=1) for row in pieces]
        blocks = plane.split(dot(jnp.concatenate(rows, axis=0), teacher_down).astype(BF16))

    matrix = lax.optimization_barrier((projection, blocks[0]))[0].reshape(width, -1)
    summed, features = student_features(plane.source, branch_all, student_in, matrix)

    target, order = [], []
    cols = plane.scatter_sum(blocks).astype(BF16)
    for i, (drow, dcore) in enumerate(places):
        block = cols[i * tokens : (i + 1) * tokens]
        target.append(wid.send(block, drow, dcore) if drow + dcore else block)
        order.append(wid.at(-drow, -dcore))
    order = jnp.stack(order).astype(jnp.int32)

    swap_at = jnp.stack([wid.at(-drow, -dcore) for drow, dcore in places]).astype(jnp.int32)

    def swap(x, whole=(), after=()):
        made, copies = cut(swap_at, x, whole, after)
        return [
            wid.send(block, -drow, -dcore) if drow + dcore else block
            for block, (drow, dcore) in zip(made, places)
        ], copies

    def everyone(x):
        groups = wid.gather(x)
        return [groups[drow][dcore] for drow, dcore in places]

    normed_cols, (hidden_late,) = swap(normed, (hidden,), (blocks[0],))
    hidden_all = everyone(hidden_late)

    made = error_grad(
        far, order, target, features, matrix, 1.0 / math.sqrt(total_tokens), tuple(normed_cols + hidden_all)
    )
    feature_error, far_blocks = made[0], made[1:]
    near_blocks = times_rows(near, [feature_error], [matrix], "error_grad_near", (far_blocks[0],))
    summed_cols, _ = swap(summed, (), (far_blocks[0],))
    error_all = everyone(feature_error)
    feature_share = plane.scatter_sum(list(near_blocks) + list(far_blocks))
    branch_grad, grads, moment = hidden_grads(
        plane.source, plane.gather(feature_share.astype(BF16)), gate_sum, up_sum, down_weight,
        tuple(summed_cols + error_all),
    )
    paired_all = everyone(grads)
    moment = plane.total(moment)
    units = gate_sum.shape[1]
    both = [grads[:, :units], grads[:, units:]]
    far_blocks = times_rows(far, both, [gate_weight, up_weight], "normed_grads")
    near_blocks = times_rows(near, both, [gate_weight, up_weight], "normed_grads_near", (far_blocks[0],))
    branch_cols, _ = swap(branch_grad, (), (far_blocks[0],))
    normed_share = plane.scatter_sum(list(near_blocks) + list(far_blocks))
    share_cols = normed_share.shape[1]
    offset = plane.index * share_cols
    gain_share = lax.dynamic_slice_in_dim(norm_gain, offset, share_cols, 0)
    inputs_share = lax.dynamic_slice_in_dim(student_in, offset, share_cols, 1).astype(F32)
    input_grad = feature_share + inverse_rms * (
        normed_share * gain_share - inputs_share * inverse_rms * (moment / width)
    )

    def stack(blocks):
        return jnp.concatenate(blocks, axis=0)

    grad_proj = dot(stack(summed_cols).T, stack(error_all)).astype(BF16)
    grad_proj = grad_proj.reshape(-1, wid.size, share)
    paired = dot(stack(normed_cols).T, stack(paired_all)).astype(BF16)
    grad_gate, grad_up = paired[:, :units], paired[:, units:]
    grad_down = dot(stack(hidden_all).T, stack(branch_cols)).astype(BF16)
    return (grad_gate, grad_up, grad_down, grad_proj, input_grad)


def solution(mesh):
    in_specs = (
        P("wid", None),
        P(),
        P(None, ("grp", "hid")),
        P(None, ("grp", "hid")),
        P(("grp", "hid"), None),
        P(None, None, ("grp", "hid")),
        P(None, "wid"),
        P("wid", ("grp", "hid")),
        P("wid", ("grp", "hid")),
        P(("grp", "hid"), "wid"),
    )
    out_specs = (
        P("wid", ("grp", "hid")),
        P("wid", ("grp", "hid")),
        P(("grp", "hid"), "wid"),
        P("wid", None, ("grp", "hid")),
        P("wid", ("grp", "hid")),
    )
    return jax.shard_map(shards, mesh=mesh, in_specs=in_specs, out_specs=out_specs, check_vma=False)
```

```python
import functools
import math

import jax
import jax.numpy as jnp
from jax import lax
from jax.experimental import pallas as pl
from jax.experimental.pallas import tpu as pltpu
from jax.sharding import PartitionSpec as P

F32 = jnp.float32
BF16 = jnp.bfloat16
CORES = 2
MIB = 1 << 20

ANY = pl.BlockSpec(memory_space=pl.ANY)
VMEM = pl.BlockSpec(memory_space=pltpu.VMEM)
SMEM = pl.BlockSpec(memory_space=pltpu.SMEM)


def dot(a, b):
    return jnp.dot(a, b, preferred_element_type=F32)


def dot_t(a, b):
    return lax.dot_general(a, b, (((1,), (1,)), ((), ())), preferred_element_type=F32)


def call(body, out_shape, in_specs, scratch, limit, flops, moved, name):
    return pl.pallas_call(
        body,
        out_shape=out_shape,
        in_specs=in_specs,
        out_specs=jax.tree.map(lambda _: VMEM, out_shape),
        scratch_shapes=scratch,
        compiler_params=pltpu.CompilerParams(vmem_limit_bytes=limit * MIB),
        cost_estimate=pl.CostEstimate(flops=flops, bytes_accessed=moved, transcendentals=0),
        name=name,
    )


def struct(shape, dtype):
    return jax.ShapeDtypeStruct(tuple(shape), dtype)


def aligned(position, size):
    return pl.ds(pl.multiple_of(position * size, size), size)


def shift(x, axis, step):
    size = lax.axis_size(axis)
    return lax.ppermute(x, axis, [(i, (i + step) % size) for i in range(size)])


class Wid:
    def __init__(self):
        self.size = lax.axis_size("wid")
        self.cores = CORES if self.size % CORES == 0 else 1
        self.rows = self.size // self.cores
        self.index = lax.axis_index("wid")
        self.row = self.index // self.cores
        self.core = self.index % self.cores

    def at(self, drow, dcore):
        return ((self.row + drow) % self.rows) * self.cores + (self.core + dcore) % self.cores

    def send(self, x, drow, dcore):
        pairs = []
        for i in range(self.size):
            row, core = i // self.cores, i % self.cores
            pairs.append((i, ((row + drow) % self.rows) * self.cores + (core + dcore) % self.cores))
        return lax.ppermute(x, "wid", pairs)

    def gather(self, x):
        blocks = []
        for drow in range(self.rows):
            mine = x if drow == 0 else self.send(x, -drow, 0)
            blocks.append([mine] + [self.send(mine, 0, -dcore) for dcore in range(1, self.cores)])
        return blocks


def flat(blocks):
    return [b for group in blocks for b in group]


class Plane:
    def __init__(self):
        self.ngrp, self.nhid = lax.axis_size("grp"), lax.axis_size("hid")
        self.size = self.ngrp * self.nhid
        self.g, self.h = lax.axis_index("grp"), lax.axis_index("hid")
        self.index = self.g * self.nhid + self.h
        steps = [(dg, dh) for dg in range(self.ngrp) for dh in range(self.nhid)]
        self.to = jnp.stack([self.place(dg, dh) for dg, dh in steps]).astype(jnp.int32)
        self.source = jnp.stack([self.place(-dg, -dh) for dg, dh in steps]).astype(jnp.int32)

    def place(self, dg, dh):
        return ((self.g + dg) % self.ngrp) * self.nhid + (self.h + dh) % self.nhid

    def split(self, x):
        cols = x.shape[1] // self.size
        return [
            lax.dynamic_slice_in_dim(x, self.place(dg, dh) * cols, cols, 1)
            for dg in range(self.ngrp)
            for dh in range(self.nhid)
        ]

    def scatter_sum(self, blocks, marker=None):
        terms = None
        sums = []
        for dh in list(range(1, self.nhid)) + [0]:
            own = blocks[dh]
            got = [shift(blocks[dg * self.nhid + dh], "grp", dg) for dg in range(1, self.ngrp)]
            if dh:
                part = add(own, *got)
                if marker is not None and dh == self.nhid - 1:
                    marker.append(part)
                sums.append(shift(part, "hid", dh))
            else:
                terms = [own] + got
        total = terms[0].astype(F32)
        for term in terms[1:] + sums:
            total = total + term.astype(F32)
        return total

    def gather(self, x):
        blocks = [None] * self.size
        for dh in range(self.nhid):
            mine = x if dh == 0 else shift(x, "hid", dh)
            for dg in range(self.ngrp):
                blocks[dg * self.nhid + dh] = mine if dg == 0 else shift(mine, "grp", dg)
        return blocks

    def total(self, x):
        for axis, size in (("grp", self.ngrp), ("hid", self.nhid)):
            x = sum([shift(x, axis, step) for step in range(1, size)], x)
        return x


def add(*blocks):
    def body(*refs):
        total = refs[0][...].astype(F32)
        for ref in refs[1:-1]:
            total = total + ref[...].astype(F32)
        refs[-1][...] = total.astype(BF16)

    x = blocks[0]
    return call(
        body, struct(x.shape, BF16), [VMEM] * len(blocks), [],
        8, x.size, 2 * x.size * (len(blocks) + 1), "add_blocks",
    )(*blocks)


def cut(at, x, whole, after):
    tokens, width = x.shape
    count = at.shape[0]
    cols = width // count

    def body(where, x_ref, *refs):
        outs = refs[len(whole) + len(after) :]
        for r in range(count):
            outs[r][...] = x_ref[:, aligned(where[r], cols)]
        for i in range(len(whole)):
            outs[count + i][...] = refs[i][...]

    out = call(
        body,
        [struct((tokens, cols), x.dtype)] * count + [struct(y.shape, y.dtype) for y in whole],
        [SMEM, VMEM] + [VMEM] * len(whole) + [ANY] * len(after), [],
        8, x.size, 4 * x.size, "cut",
    )(at, x, *whole, *after)
    return out[:count], out[count:]


def teacher_sums(wid, rows_at, teacher_in, weights, first, cols, after):
    total, depth = teacher_in.shape
    tokens = total // wid.size
    held = wid.rows * tokens
    pieces = 4
    deep = depth // pieces

    def body(at, x, gate, up, *refs):
        outs = refs[len(after) : len(after) + wid.rows + wid.cores - 1]
        ordered, buf, x_sems, sems = refs[len(after) + len(outs) :]

        def rows(r):
            return pltpu.make_async_copy(
                x.at[aligned(at[r], tokens), :], ordered.at[pl.ds(r * tokens, tokens), :], x_sems.at[r]
            )

        def copy(i, k):
            here = pl.ds(k * deep, deep)
            return pltpu.make_async_copy(
                (gate, up)[i].at[here, pl.ds(first, cols)], buf.at[i, here, :], sems.at[i, k]
            )

        for r in range(wid.size):
            rows(r).start()
        for i in range(2):
            for k in range(pieces):
                copy(i, k).start()
        for r in range(wid.size):
            rows(r).wait()
        for i in range(2):
            for k in range(pieces):
                copy(i, k).wait()
            part = dot(ordered[...], buf[i])
            for r in range(wid.rows):
                outs[r][i] = part[r * tokens : (r + 1) * tokens]
            for c in range(1, wid.cores):
                outs[wid.rows + c - 1][i] = part[c * held : (c + 1) * held].astype(BF16)

    return call(
        body,
        [struct((2, tokens, cols), F32)] * wid.rows + [struct((2, held, cols), BF16)] * (wid.cores - 1),
        [SMEM, ANY, ANY, ANY] + [ANY] * len(after),
        [
            pltpu.VMEM((total, depth), BF16),
            pltpu.VMEM((2, depth, cols), BF16),
            pltpu.SemaphoreType.DMA((wid.size,)),
            pltpu.SemaphoreType.DMA((2, pieces)),
        ],
        60, 4 * total * depth * cols, 4 * depth * cols, "teacher_sums",
    )(rows_at, teacher_in, *weights, *after)


def teacher_down_blocks(where, pieces, weight):
    depth, width = weight.shape
    count = where.shape[0]
    cols = width // count
    rows = [row[0].shape[0] for row in pieces]
    total = sum(rows)
    deeps = [part.shape[1] for part in pieces[0]]
    number = sum(len(row) for row in pieces)

    def body(place, *refs):
        ins, w = refs[:number], refs[number]
        outs = refs[number + 1 : number + 1 + count]
        whole, buf, sems = refs[number + 1 + count :]

        def copy(r):
            return pltpu.make_async_copy(w.at[:, aligned(place[r], cols)], buf.at[r], sems.at[r])

        for r in range(count):
            copy(r).start()
        n = row = 0
        for i, parts in enumerate(pieces):
            col = 0
            for part in parts:
                whole[row : row + rows[i], col : col + part.shape[1]] = ins[n][...]
                col += part.shape[1]
                n += 1
            row += rows[i]
        for r in range(count):
            copy(r).wait()
            outs[r][...] = dot(whole[...], buf[r]).astype(BF16)

    return call(
        body, [struct((total, cols), BF16)] * count, [SMEM] + [VMEM] * number + [ANY],
        [
            pltpu.VMEM((total, depth), BF16),
            pltpu.VMEM((count, depth, cols), BF16),
            pltpu.SemaphoreType.DMA((count,)),
        ],
        24, 2 * total * depth * width, 2 * depth * width, "teacher_down",
    )(where, *flat(pieces), weight)


def student_down(x, weight, count):
    tokens, depth = x.shape
    width = weight.shape[1]
    cols = width // count

    def body(x_ref, w, out, buf, sems):
        def copy(r):
            return pltpu.make_async_copy(w.at[:, pl.ds(r * cols, cols)], buf.at[r], sems.at[r])

        for r in range(count):
            copy(r).start()
        for r in range(count):
            copy(r).wait()
            out[r] = dot(x_ref[...], buf[r]).astype(BF16)

    return call(
        body, struct((count, tokens, cols), BF16), [VMEM, ANY],
        [pltpu.VMEM((count, depth, cols), BF16), pltpu.SemaphoreType.DMA((count,))],
        16, 2 * tokens * depth * width, 2 * depth * width, "student_down",
    )(x, weight)


def student_hidden(student_in, norm_gain, gate_weight, up_weight, after):
    tokens, width = student_in.shape
    cols = gate_weight.shape[1]
    count = 8
    deep = width // count

    def body(x, gain, wg, wu, *refs):
        normed, inverse, gate, up, hidden = refs[len(after) : len(after) + 5]
        buf, sems = refs[len(after) + 5 :]

        def copy(i, k):
            return pltpu.make_async_copy(
                (wg, wu)[i].at[pl.ds(k * deep, deep), :], buf.at[i, k], sems.at[i, k]
            )

        for k in range(count):
            for i in range(2):
                copy(i, k).start()
        values = x[...].astype(F32)
        inv = lax.rsqrt(jnp.sum(values * values, axis=-1, keepdims=True) / width + 1e-05)
        inverse[...] = inv
        normed[...] = (values * inv * gain[...]).astype(BF16)
        sums = [None, None]
        for k in range(count):
            for i in range(2):
                copy(i, k).wait()
                part = dot(normed[:, k * deep : (k + 1) * deep], buf[i, k])
                sums[i] = part if k == 0 else sums[i] + part
        gate[...] = sums[0]
        up[...] = sums[1]
        hidden[...] = (sums[0] * jax.nn.sigmoid(sums[0]) * sums[1]).astype(BF16)

    return call(
        body,
        [
            struct((tokens, width), BF16),
            struct((tokens, 1), F32),
            struct((tokens, cols), F32),
            struct((tokens, cols), F32),
            struct((tokens, cols), BF16),
        ],
        [VMEM, VMEM, ANY, ANY] + [ANY] * len(after),
        [pltpu.VMEM((2, count, deep, cols), BF16), pltpu.SemaphoreType.DMA((2, count))],
        32, 4 * tokens * width * cols, 4 * width * cols, "student_hidden",
    )(student_in, norm_gain.reshape(1, width), gate_weight, up_weight, *after)


def student_features(branch, student_in, matrix):
    tokens, width = student_in.shape
    count, _, cols = branch.shape
    out_cols = matrix.shape[1]

    def body(x, b, w, summed, features, buf, sems):
        def copy(r):
            return pltpu.make_async_copy(w.at[pl.ds(r * cols, cols), :], buf.at[r], sems.at[r])

        for r in range(count):
            copy(r).start()
        total = None
        for r in range(count):
            here = slice(r * cols, (r + 1) * cols)
            block = (x[:, here].astype(F32) + b[r].astype(F32)).astype(BF16)
            summed[:, here] = block
            copy(r).wait()
            part = dot(block, buf[r])
            total = part if total is None else total + part
        features[...] = total

    return call(
        body, [struct((tokens, width), BF16), struct((tokens, out_cols), F32)],
        [VMEM, VMEM, ANY],
        [pltpu.VMEM((count, cols, out_cols), BF16), pltpu.SemaphoreType.DMA((count,))],
        20, 2 * tokens * width * out_cols, 2 * width * out_cols, "student_features",
    )(student_in, branch, matrix)


def error_grad(to, order, target, features, matrix, scale, after):
    tokens, out_cols = features.shape
    width = matrix.shape[0]
    count = to.shape[0]
    cols = width // count
    parts = len(target)
    share = out_cols // parts

    def body(where, place, *refs):
        pieces, feats, w = refs[:parts], refs[parts], refs[parts + 1]
        refs = refs[parts + 2 + len(after) :]
        error, outs = refs[0], refs[1 : 1 + count]
        held, buf, sems = refs[1 + count :]

        def copy(r):
            return pltpu.make_async_copy(w.at[aligned(where[r], cols), :], buf.at[r], sems.at[r])

        for r in range(count):
            copy(r).start()
        for r in range(parts):
            held[place[r]] = pieces[r][...]
        for r in range(parts):
            here = slice(r * share, (r + 1) * share)
            error[:, here] = ((feats[:, here] - held[r].astype(F32)) * scale).astype(BF16)
        for r in range(count):
            copy(r).wait()
            outs[r][...] = dot_t(error[...], buf[r]).astype(BF16)

    return call(
        body, [struct((tokens, out_cols), BF16)] + [struct((tokens, cols), BF16)] * count,
        [SMEM, SMEM] + [VMEM] * (parts + 1) + [ANY] * (1 + len(after)),
        [
            pltpu.VMEM((parts, tokens, share), BF16),
            pltpu.VMEM((count, cols, out_cols), BF16),
            pltpu.SemaphoreType.DMA((count,)),
        ],
        20, 2 * tokens * width * out_cols, 2 * width * out_cols, "error_grad",
    )(to, order, *target, features, matrix, *after)


def hidden_grads(at, pieces, gate, up, weight, after):
    tokens, units = gate.shape
    width = weight.shape[1]
    count = len(pieces)
    cols = width // count

    def body(where, gate_ref, up_ref, *refs):
        ins, w = refs[:count], refs[count]
        branch_grad, grads, moment, buf, sems = refs[count + 1 + len(after) :]

        def copy(r):
            return pltpu.make_async_copy(w.at[:, aligned(where[r], cols)], buf.at[r], sems.at[r])

        for r in range(count):
            copy(r).start()
        total = None
        for r in range(count):
            block = ins[r][...]
            branch_grad[:, aligned(where[r], cols)] = block
            copy(r).wait()
            part = dot_t(block, buf[r])
            total = part if total is None else total + part
        g, u = gate_ref[...], up_ref[...]
        sigma = jax.nn.sigmoid(g)
        dg = (total * u * sigma * (1.0 + g * (1.0 - sigma))).astype(BF16)
        du = (total * g * sigma).astype(BF16)
        grads[:, :units] = dg
        grads[:, units:] = du
        moment[...] = jnp.sum(dg.astype(F32) * g + du.astype(F32) * u, axis=-1, keepdims=True)

    return call(
        body,
        [
            struct((tokens, width), BF16),
            struct((tokens, 2 * units), BF16),
            struct((tokens, 1), F32),
        ],
        [SMEM, VMEM, VMEM] + [VMEM] * count + [ANY] * (1 + len(after)),
        [pltpu.VMEM((count, units, cols), BF16), pltpu.SemaphoreType.DMA((count,))],
        20, 2 * tokens * width * units, 2 * width * units, "hidden_grads",
    )(at, gate, up, *pieces, weight, *after)


def normed_grads(to, grads, gate_weight, up_weight):
    tokens, units = grads.shape[0], grads.shape[1] // 2
    width = gate_weight.shape[0]
    count = to.shape[0]
    cols = width // count

    def body(where, x, wg, wu, *refs):
        outs = refs[:count]
        buf, sems = refs[count:]

        def copy(i, r):
            return pltpu.make_async_copy(
                (wg, wu)[i].at[aligned(where[r], cols), :], buf.at[i, r], sems.at[i, r]
            )

        for r in range(count):
            for i in range(2):
                copy(i, r).start()
        dg, du = x[:, :units], x[:, units:]
        for r in range(count):
            copy(0, r).wait()
            copy(1, r).wait()
            outs[r][...] = (dot_t(dg, buf[0, r]) + dot_t(du, buf[1, r])).astype(BF16)

    return call(
        body, [struct((tokens, cols), BF16)] * count, [SMEM, VMEM, ANY, ANY],
        [pltpu.VMEM((2, count, cols, units), BF16), pltpu.SemaphoreType.DMA((2, count))],
        32, 4 * tokens * width * units, 4 * width * units, "normed_grads",
    )(to, grads, gate_weight, up_weight)


def token_products(left, right):
    tokens, rows = left[0].shape
    cols = right[0].shape[1] // 2
    count = len(left)

    def body(*refs):
        lefts, rights, outs = refs[:count], refs[count : 2 * count], refs[2 * count : 2 * count + 2]
        flipped, held = refs[2 * count + 2 :]
        for r in range(count):
            here = slice(r * tokens, (r + 1) * tokens)
            flipped[:, here] = lefts[r][...].T
            held[here, :] = rights[r][...]
        for i in range(2):
            for start in range(0, cols, 256):
                size = min(256, cols - start)
                part = dot(flipped[...], held[:, i * cols + start : i * cols + start + size])
                outs[i][:, start : start + size] = part.astype(BF16)

    return call(
        body, [struct((rows, cols), BF16)] * 2, [VMEM] * (2 * count),
        [pltpu.VMEM((rows, count * tokens), BF16), pltpu.VMEM((count * tokens, 2 * cols), BF16)],
        24, 4 * count * tokens * rows * cols, 4 * rows * cols, "token_products",
    )(*left, *right)


def shards(
    student_in,
    norm_gain,
    gate_weight,
    up_weight,
    down_weight,
    projection,
    teacher_in,
    teacher_gate,
    teacher_up,
    teacher_down,
):
    wid, plane = Wid(), Plane()
    tokens, width = student_in.shape
    total_tokens = tokens * wid.size
    share = projection.shape[2]

    rows_at = jnp.stack(
        [wid.at(drow, dcore) for dcore in range(wid.cores) for drow in range(wid.rows)]
    ).astype(jnp.int32)
    units = teacher_gate.shape[1]
    tile = next((t for t in (256, 128) if units % t == 0), units // 2)
    number = max(units // tile // 3, 1)
    cuts = [0, number * tile, 2 * number * tile, units] if units // tile >= 3 else [0, units]
    after = ()
    sums = []
    for start, stop in zip(cuts, cuts[1:]):
        parts = teacher_sums(
            wid, rows_at, teacher_in, (teacher_gate, teacher_up), start, stop - start, after
        )
        got = [wid.send(part, 0, c + 1) for c, part in enumerate(parts[wid.rows :])]
        rows, sent = [], []
        for r in range(wid.rows):
            row = parts[r]
            for block in got:
                row = row + block[:, r * tokens : (r + 1) * tokens].astype(F32)
            if r:
                sent.append(row.astype(BF16))
                row = wid.send(sent[-1], r, 0)
            rows.append(row)
        sums.append((rows, parts, sent))
        after = (parts[0],) + (tuple(sums[-2][2]) if len(sums) > 1 else ())

    normed, inverse_rms, gate_sum, up_sum, hidden = student_hidden(
        student_in, norm_gain, gate_weight, up_weight, after
    )
    branch_blocks = student_down(hidden, down_weight, plane.size)

    hidden_blocks = [[[] for _ in range(wid.rows)] for _ in range(wid.cores)]
    for rows, _, _ in sums:
        gate_rows, up_rows = (sum([row[i].astype(F32) for row in rows[1:]], rows[0][i]) for i in range(2))
        teacher_hidden = (gate_rows * jax.nn.sigmoid(gate_rows) * up_rows).astype(BF16)
        for drow, group in enumerate(wid.gather(teacher_hidden)):
            for dcore, block in enumerate(group):
                hidden_blocks[dcore][drow].append(block)
    pieces = flat(hidden_blocks)
    places = [(drow, dcore) for dcore in range(wid.cores) for drow in range(wid.rows)]

    branch_blocks = lax.all_to_all(branch_blocks, ("grp", "hid"), 0, 0, tiled=True)
    branch = jnp.sum(branch_blocks.astype(F32), axis=0).astype(BF16)
    branch_all = lax.all_gather(branch, ("grp", "hid"))

    if share % 128 == 0:
        blocks = teacher_down_blocks(plane.to, pieces, teacher_down)
    else:
        rows = [jnp.concatenate(row, axis=1) for row in pieces]
        blocks = plane.split(dot(jnp.concatenate(rows, axis=0), teacher_down).astype(BF16))

    target, order, marker = [], [], []
    cols = plane.scatter_sum(blocks, marker).astype(BF16)
    for i, (drow, dcore) in enumerate(places):
        block = cols[i * tokens : (i + 1) * tokens]
        target.append(wid.send(block, drow, dcore) if drow + dcore else block)
        order.append(wid.at(-drow, -dcore))
    order = jnp.stack(order).astype(jnp.int32)

    matrix = lax.optimization_barrier((projection, marker[0]))[0].reshape(width, -1)
    summed, features = student_features(branch_all, student_in, matrix)

    swap_at = jnp.stack([wid.at(-drow, -dcore) for drow, dcore in places]).astype(jnp.int32)

    def swap(x, whole=(), after=()):
        made, copies = cut(swap_at, x, whole, after)
        return [
            wid.send(block, -drow, -dcore) if drow + dcore else block
            for block, (drow, dcore) in zip(made, places)
        ], copies

    def everyone(x):
        groups = wid.gather(x)
        return [groups[drow][dcore] for drow, dcore in places]

    normed_cols, (hidden_late,) = swap(normed, (hidden,), (blocks[0],))
    hidden_all = everyone(hidden_late)

    feature_error, *blocks = error_grad(
        plane.to, order, target, features, matrix, 1.0 / math.sqrt(total_tokens),
        tuple(normed_cols + hidden_all),
    )
    summed_cols, _ = swap(summed, (), (blocks[0],))
    error_all = everyone(feature_error)
    feature_share = plane.scatter_sum(blocks)
    branch_grad, grads, moment = hidden_grads(
        plane.source, plane.gather(feature_share.astype(BF16)), gate_sum, up_sum, down_weight,
        tuple(summed_cols + error_all),
    )
    paired_all = everyone(grads)
    moment = plane.total(moment)
    blocks = normed_grads(plane.to, grads, gate_weight, up_weight)
    branch_cols, _ = swap(branch_grad, (), (blocks[0],))
    normed_share = plane.scatter_sum(blocks)
    share_cols = normed_share.shape[1]
    offset = plane.index * share_cols
    gain_share = lax.dynamic_slice_in_dim(norm_gain, offset, share_cols, 0)
    inputs_share = lax.dynamic_slice_in_dim(student_in, offset, share_cols, 1).astype(F32)
    input_grad = feature_share + inverse_rms * (
        normed_share * gain_share - inputs_share * inverse_rms * (moment / width)
    )

    def stack(blocks):
        return jnp.concatenate(blocks, axis=0)

    grad_proj = dot(stack(summed_cols).T, stack(error_all)).astype(BF16)
    grad_proj = grad_proj.reshape(-1, wid.size, share)
    grad_gate, grad_up = token_products(normed_cols, paired_all)
    grad_down = dot(stack(hidden_all).T, stack(branch_cols)).astype(BF16)
    return (grad_gate, grad_up, grad_down, grad_proj, input_grad)


def solution(mesh):
    in_specs = (
        P("wid", None),
        P(),
        P(None, ("grp", "hid")),
        P(None, ("grp", "hid")),
        P(("grp", "hid"), None),
        P(None, None, ("grp", "hid")),
        P(None, "wid"),
        P("wid", ("grp", "hid")),
        P("wid", ("grp", "hid")),
        P(("grp", "hid"), "wid"),
    )
    out_specs = (
        P("wid", ("grp", "hid")),
        P("wid", ("grp", "hid")),
        P(("grp", "hid"), "wid"),
        P("wid", None, ("grp", "hid")),
        P("wid", ("grp", "hid")),
    )
    return jax.shard_map(shards, mesh=mesh, in_specs=in_specs, out_specs=out_specs, check_vma=False)
```

```python
import functools
import math

import jax
import jax.numpy as jnp
from jax import lax
from jax.experimental import pallas as pl
from jax.experimental.pallas import tpu as pltpu
from jax.sharding import PartitionSpec as P

F32 = jnp.float32
BF16 = jnp.bfloat16
CORES = 2
MIB = 1 << 20

SPECS = {
    "smem": pl.BlockSpec(memory_space=pltpu.SMEM),
    "vmem": pl.BlockSpec(memory_space=pltpu.VMEM),
    "any": pl.BlockSpec(memory_space=pl.ANY),
    "hbm": pl.BlockSpec(memory_space=pltpu.HBM),
    "load": pl.BlockSpec(memory_space=pltpu.HBM),
    "store": pl.BlockSpec(memory_space=pltpu.HBM),
}


def dot(a, b):
    return jnp.dot(a, b, preferred_element_type=F32)


def dot_t(a, b):
    return lax.dot_general(a, b, (((1,), (1,)), ((), ())), preferred_element_type=F32)


def size_of(x):
    return x.size * jnp.dtype(x.dtype).itemsize


def call(body, ins, outs, scratch, extra, flops, name):
    loads = [i for i, (place, _) in enumerate(ins) if place == "load"]
    stores = [i for i, (place, _) in enumerate(outs) if place == "store"]
    moved = len(loads) + len(stores)
    rooms = [pltpu.VMEM(ins[i][1].shape, ins[i][1].dtype) for i in loads]
    rooms += [pltpu.VMEM(outs[i][1].shape, outs[i][1].dtype) for i in stores]
    sems = [pltpu.SemaphoreType.DMA((moved,))] if moved else []

    def kernel(*refs):
        given, made = list(refs[: len(ins)]), list(refs[len(ins) : len(ins) + len(outs)])
        rest = refs[len(ins) + len(outs) :]
        own, held = rest[: len(scratch)], rest[len(scratch) : len(scratch) + moved]
        sem = rest[-1] if moved else None
        arriving, leaving = [], []
        for k, i in enumerate(loads):
            arriving.append(pltpu.make_async_copy(given[i], held[k], sem.at[k]))
            given[i] = held[k]
        for k, i in enumerate(stores, len(loads)):
            leaving.append(pltpu.make_async_copy(held[k], made[i], sem.at[k]))
            made[i] = held[k]
        for copy in arriving:
            copy.start()
        steps = body(given, made, own)
        next(steps)
        for copy in arriving:
            copy.wait()
        for _ in steps:
            pass
        for copy in leaving:
            copy.start()
        for copy in leaving:
            copy.wait()

    room = sum(size_of(x) for place, x in ins if place in ("vmem", "load"))
    room += sum(size_of(x) for _, x in outs)
    room += sum(math.prod(x.shape) * jnp.dtype(x.dtype).itemsize for x in scratch if hasattr(x, "memory_space") and "sem" not in str(x.memory_space))
    total = sum(size_of(x) for _, x in ins) + sum(size_of(x) for _, x in outs)
    return pl.pallas_call(
        kernel,
        out_shape=[shape for _, shape in outs],
        in_specs=[SPECS[place] for place, _ in ins],
        out_specs=[SPECS[place] for place, _ in outs],
        scratch_shapes=[*scratch, *rooms, *sems],
        compiler_params=pltpu.CompilerParams(vmem_limit_bytes=int(room + extra * MIB)),
        cost_estimate=pl.CostEstimate(flops=flops, bytes_accessed=total, transcendentals=0),
        name=name,
    )(*[x for _, x in ins])


def struct(shape, dtype):
    return jax.ShapeDtypeStruct(tuple(shape), dtype)


def aligned(position, size):
    return pl.ds(pl.multiple_of(position * size, size), size)


def shift(x, axis, step):
    size = lax.axis_size(axis)
    return lax.ppermute(x, axis, [(i, (i + step) % size) for i in range(size)])


class Wid:
    def __init__(self):
        self.size = lax.axis_size("wid")
        self.cores = CORES if self.size % CORES == 0 else 1
        self.rows = self.size // self.cores
        self.index = lax.axis_index("wid")
        self.row = self.index // self.cores
        self.core = self.index % self.cores

    def at(self, drow, dcore):
        return ((self.row + drow) % self.rows) * self.cores + (self.core + dcore) % self.cores

    def send(self, x, drow, dcore):
        pairs = []
        for i in range(self.size):
            row, core = i // self.cores, i % self.cores
            pairs.append((i, ((row + drow) % self.rows) * self.cores + (core + dcore) % self.cores))
        return lax.ppermute(x, "wid", pairs)

    def gather(self, x):
        blocks = []
        for drow in range(self.rows):
            mine = x if drow == 0 else self.send(x, -drow, 0)
            blocks.append([mine] + [self.send(mine, 0, -dcore) for dcore in range(1, self.cores)])
        return blocks


def flat(blocks):
    return [b for group in blocks for b in group]


class Plane:
    def __init__(self):
        self.ngrp, self.nhid = lax.axis_size("grp"), lax.axis_size("hid")
        self.size = self.ngrp * self.nhid
        self.g, self.h = lax.axis_index("grp"), lax.axis_index("hid")
        self.index = self.g * self.nhid + self.h
        steps = [(dg, dh) for dg in range(self.ngrp) for dh in range(self.nhid)]
        self.to = jnp.stack([self.place(dg, dh) for dg, dh in steps]).astype(jnp.int32)
        self.source = jnp.stack([self.place(-dg, -dh) for dg, dh in steps]).astype(jnp.int32)

    def place(self, dg, dh):
        return ((self.g + dg) % self.ngrp) * self.nhid + (self.h + dh) % self.nhid

    def messages(self):
        order = list(range(1, self.nhid)) + [0]
        return [order[i : i + 2] for i in range(0, self.nhid, 2)]

    def shapes(self, rows, cols):
        near = [struct((rows, cols), BF16)] * self.nhid
        far = [struct((len(m), rows, cols), BF16) for m in self.messages()] * (self.ngrp - 1)
        return [("vmem", x) for x in near + far]

    def spots(self):
        spots = [(dh, None) for dh in range(self.nhid)]
        messages = self.messages()
        for dg in range(1, self.ngrp):
            for dh in range(self.nhid):
                j = next(j for j, m in enumerate(messages) if dh in m)
                spots.append((self.nhid + (dg - 1) * len(messages) + j, messages[j].index(dh)))
        return spots

    def order(self):
        return list(range(self.nhid, self.size)) + list(range(self.nhid))

    def split(self, x):
        cols = x.shape[1] // self.size
        near = [
            lax.dynamic_slice_in_dim(x, self.place(0, dh) * cols, cols, 1) for dh in range(self.nhid)
        ]
        far = [
            jnp.stack([lax.dynamic_slice_in_dim(x, self.place(dg, dh) * cols, cols, 1) for dh in m])
            for dg in range(1, self.ngrp)
            for m in self.messages()
        ]
        return near + far

    def scatter_sum(self, blocks, marker=None):
        messages = self.messages()
        terms = [blocks[0].astype(F32)]
        for j, message in enumerate(messages):
            got = [
                shift(blocks[self.nhid + (dg - 1) * len(messages) + j], "grp", dg)
                for dg in range(1, self.ngrp)
            ]
            if message[-1] == 0:
                terms += [x[len(message) - 1].astype(F32) for x in got]
            steps = [dh for dh in message if dh]
            if steps:
                parts = add(got, [blocks[dh] for dh in steps])
                terms += [shift(part, "hid", dh).astype(F32) for part, dh in zip(parts, steps)]
                if marker is not None:
                    marker.append(parts[-1])
        return functools.reduce(lambda a, b: a + b, terms)

    def gather(self, x):
        blocks = [None] * self.size
        for dh in range(self.nhid):
            mine = x if dh == 0 else shift(x, "hid", dh)
            for dg in range(self.ngrp):
                blocks[dg * self.nhid + dh] = mine if dg == 0 else shift(mine, "grp", dg)
        return blocks

    def total(self, x):
        for axis, size in (("grp", self.ngrp), ("hid", self.nhid)):
            x = sum([shift(x, axis, step) for step in range(1, size)], x)
        return x


def add(received, own):
    def body(ins, outs, _):
        yield
        for i in range(len(own)):
            total = ins[len(received) + i][...].astype(F32)
            for j in range(len(received)):
                total = total + ins[j][i].astype(F32)
            outs[i][...] = total.astype(BF16)

    return call(
        body, [("vmem", x) for x in [*received, *own]], [("vmem", struct(x.shape, BF16)) for x in own],
        [], 2, len(own) * own[0].size, "add_blocks",
    )


def cut(at, x, place="vmem", whole=(), after=()):
    tokens, width = x.shape
    count = at.shape[0]
    cols = width // count

    def body(ins, outs, _):
        yield
        for r in range(count):
            outs[r][...] = ins[1][:, aligned(ins[0][r], cols)]
        for i in range(len(whole)):
            outs[count + i][...] = ins[2 + i][...]

    out = call(
        body, [("smem", at), (place, x)] + [("load", y) for y in whole] + [("any", y) for y in after],
        [("vmem", struct((tokens, cols), x.dtype))] * count
        + [("vmem", struct(y.shape, y.dtype)) for y in whole],
        [], 2, x.size, "cut",
    )
    return out[:count], out[count:]


def assemble(at, blocks):
    rows, cols = blocks[0].shape
    count = len(blocks)

    def body(ins, outs, _):
        yield
        for r in range(count):
            outs[0][:, aligned(ins[0][r], cols)] = ins[1 + r][...]

    return call(
        body, [("smem", at)] + [("load", x) for x in blocks],
        [("vmem", struct((rows, count * cols), BF16))], [], 2, count * rows * cols, "assemble",
    )[0]


def teacher_sums(wid, rows_at, x, weights, first, cols, after):
    total, depth = x.shape
    tokens = total // wid.size
    held = wid.rows * tokens
    pieces = 4
    deep = depth // pieces

    def body(ins, outs, own):
        at, given, gate, up = ins[:4]
        buf, sems = own[:2]
        ordered = given if rows_at is None else outs[-2]

        def rows(r):
            return pltpu.make_async_copy(
                given.at[aligned(at[r], tokens), :], ordered.at[pl.ds(r * tokens, tokens), :], own[2].at[r]
            )

        def copy(i, k):
            here = pl.ds(k * deep, deep)
            return pltpu.make_async_copy(
                (gate, up)[i].at[here, pl.ds(first, cols)], buf.at[i, here, :], sems.at[i, k]
            )

        if rows_at is not None:
            for r in range(wid.size):
                rows(r).start()
        for i in range(2):
            for k in range(pieces):
                copy(i, k).start()
        yield
        if rows_at is not None:
            for r in range(wid.size):
                rows(r).wait()
        for i in range(2):
            for k in range(pieces):
                copy(i, k).wait()
            part = dot(ordered[...], buf[i])
            for r in range(wid.rows):
                outs[r][i] = part[r * tokens : (r + 1) * tokens]
            for c in range(1, wid.cores):
                outs[wid.rows + c - 1][i] = part[c * held : (c + 1) * held].astype(BF16)
        outs[-1][...] = jnp.zeros((8, 128), F32)

    scratch = [pltpu.VMEM((2, depth, cols), BF16), pltpu.SemaphoreType.DMA((2, pieces))]
    if rows_at is None:
        ins, more = [("smem", jnp.zeros((1,), jnp.int32)), ("vmem", x)], []
    else:
        ins, more = [("smem", rows_at), ("hbm", x)], [("vmem", struct(x.shape, BF16))]
        scratch.append(pltpu.SemaphoreType.DMA((wid.size,)))
    return call(
        body, ins + [("hbm", w) for w in weights] + [("any", y) for y in after],
        [("vmem", struct((2, tokens, cols), F32))] * wid.rows
        + [("vmem", struct((2, held, cols), BF16))] * (wid.cores - 1)
        + more + [("vmem", struct((8, 128), F32))],
        scratch, 8, 4 * total * depth * cols, "teacher_sums",
    )


def teacher_down_blocks(plane, pieces, weight):
    depth, width = weight.shape
    count = plane.size
    cols = width // count
    rows = [row[0].shape[0] for row in pieces]
    total = sum(rows)
    deeps = [part.shape[1] for part in pieces[0]]
    spots = plane.spots()

    def body(ins, outs, own):
        place, parts, w = ins[0], ins[1:-1], ins[-1]
        whole, buf, result, sems = own

        def copy(k):
            here = pl.ds(sum(deeps[:k]), deeps[k])
            return pltpu.make_async_copy(w.at[here, :], buf.at[here, :], sems.at[k])

        for k in range(len(deeps)):
            copy(k).start()
        yield
        n = row = 0
        for i, line in enumerate(pieces):
            col = 0
            for part in line:
                whole[row : row + rows[i], col : col + part.shape[1]] = parts[n][...]
                col += part.shape[1]
                n += 1
            row += rows[i]
        for k in range(len(deeps)):
            copy(k).wait()
            here = slice(sum(deeps[:k]), sum(deeps[: k + 1]))
            part = dot(whole[:, here], buf[here, :])
            result[...] = part if k == 0 else result[...] + part
        for r in plane.order():
            i, j = spots[r]
            block = result[:, aligned(place[r], cols)].astype(BF16)
            if j is None:
                outs[i][...] = block
            else:
                outs[i][j] = block

    return call(
        body, [("smem", plane.to)] + [("load", x) for x in flat(pieces)] + [("hbm", weight)],
        plane.shapes(total, cols),
        [
            pltpu.VMEM((total, depth), BF16),
            pltpu.VMEM((depth, width), BF16),
            pltpu.VMEM((total, width), F32),
            pltpu.SemaphoreType.DMA((len(deeps),)),
        ],
        10, 2 * total * depth * width, "teacher_down",
    )


def student_forward(student_in, norm_gain, gate_weight, up_weight, down_weight, after):
    tokens, width = student_in.shape
    cols = gate_weight.shape[1]
    count = 8
    deep = width // count

    def body(ins, outs, own):
        x, gain, wg, wu, wd = ins[:5]
        normed, gate, up, hidden, branch, inverse, token = outs
        buf, down, sems, down_sems = own

        def copy(i, k):
            return pltpu.make_async_copy(
                (wg, wu)[i].at[pl.ds(k * deep, deep), :], buf.at[i, k], sems.at[i, k]
            )

        def copy_down(k):
            here = pl.ds(k * (cols // 2), cols // 2)
            return pltpu.make_async_copy(wd.at[here, :], down.at[here, :], down_sems.at[k])

        for k in range(count):
            for i in range(2):
                copy(i, k).start()
        for k in range(2):
            copy_down(k).start()
        yield
        values = x[...].astype(F32)
        inv = lax.rsqrt(jnp.sum(values * values, axis=-1, keepdims=True) / width + 1e-05)
        inverse[...] = inv
        normed[...] = (values * inv * gain[...]).astype(BF16)
        sums = [None, None]
        for k in range(count):
            for i in range(2):
                copy(i, k).wait()
                part = dot(normed[:, k * deep : (k + 1) * deep], buf[i, k])
                sums[i] = part if k == 0 else sums[i] + part
        gate[...] = sums[0]
        up[...] = sums[1]
        hidden[...] = (sums[0] * jax.nn.sigmoid(sums[0]) * sums[1]).astype(BF16)
        for k in range(2):
            copy_down(k).wait()
        for k in range(count):
            here = slice(k * deep, (k + 1) * deep)
            branch[:, here] = dot(hidden[...], down[:, here]).astype(BF16)
        token[...] = jnp.zeros((8, 128), F32)

    return call(
        body,
        [("load", student_in), ("load", norm_gain.reshape(1, width))]
        + [("hbm", w) for w in (gate_weight, up_weight, down_weight)] + [("any", y) for y in after],
        [
            ("store", struct((tokens, width), BF16)),
            ("store", struct((tokens, cols), F32)),
            ("store", struct((tokens, cols), F32)),
            ("store", struct((tokens, cols), BF16)),
            ("store", struct((tokens, width), BF16)),
            ("vmem", struct((tokens, 1), F32)),
            ("vmem", struct((8, 128), F32)),
        ],
        [
            pltpu.VMEM((2, count, deep, cols), BF16),
            pltpu.VMEM((cols, width), BF16),
            pltpu.SemaphoreType.DMA((2, count)),
            pltpu.SemaphoreType.DMA((2,)),
        ],
        6, 6 * tokens * width * cols, "student_forward",
    )


def student_features(branch, student_in, matrix):
    tokens, width = student_in.shape
    count = 8
    cols = width // count
    out_cols = matrix.shape[1]

    def body(ins, outs, own):
        x, b, w = ins
        summed, features = outs
        buf, sems = own

        def copy(r):
            return pltpu.make_async_copy(w.at[pl.ds(r * cols, cols), :], buf.at[r], sems.at[r])

        for r in range(count):
            copy(r).start()
        yield
        total = None
        for r in range(count):
            here = slice(r * cols, (r + 1) * cols)
            block = (x[:, here].astype(F32) + b[:, here].astype(F32)).astype(BF16)
            summed[:, here] = block
            copy(r).wait()
            part = dot(block, buf[r])
            total = part if total is None else total + part
        features[...] = total

    return call(
        body, [("load", student_in), ("load", branch), ("hbm", matrix)],
        [("store", struct((tokens, width), BF16)), ("vmem", struct((tokens, out_cols), F32))],
        [pltpu.VMEM((count, cols, out_cols), BF16), pltpu.SemaphoreType.DMA((count,))],
        4, 2 * tokens * width * out_cols, "student_features",
    )


def error_grad(plane, order, target, features, matrix, scale, after):
    tokens, out_cols = features.shape
    width = matrix.shape[0]
    count = plane.size
    cols = width // count
    parts = len(target)
    share = out_cols // parts
    spots = plane.spots()

    def body(ins, outs, own):
        where, place, feats, w = ins[:4]
        pieces = ins[4 : 4 + parts]
        error = outs[-1]
        held, buf, sems = own

        def copy(r):
            return pltpu.make_async_copy(w.at[aligned(where[r], cols), :], buf.at[r], sems.at[r])

        for r in plane.order():
            copy(r).start()
        yield
        for r in range(parts):
            held[place[r]] = pieces[r][...]
        for r in range(parts):
            here = slice(r * share, (r + 1) * share)
            error[:, here] = ((feats[:, here] - held[r].astype(F32)) * scale).astype(BF16)
        for r in plane.order():
            i, j = spots[r]
            copy(r).wait()
            block = dot_t(error[...], buf[r]).astype(BF16)
            if j is None:
                outs[i][...] = block
            else:
                outs[i][j] = block

    out = call(
        body,
        [("smem", plane.to), ("smem", order), ("vmem", features), ("hbm", matrix)]
        + [("load", x) for x in target] + [("hbm", x) for x in after],
        plane.shapes(tokens, cols) + [("store", struct((tokens, out_cols), BF16))],
        [
            pltpu.VMEM((parts, tokens, share), BF16),
            pltpu.VMEM((count, cols, out_cols), BF16),
            pltpu.SemaphoreType.DMA((count,)),
        ],
        4, 2 * tokens * width * out_cols, "error_grad",
    )
    return out[-1], out[:-1]


def hidden_grads(branch_grad, gate, up, weight, after):
    tokens, units = gate.shape
    width = weight.shape[1]
    count = 8
    cols = width // count

    def body(ins, outs, own):
        x, gate_ref, up_ref, w = ins[:4]
        grads, moment = outs
        buf, sems = own

        def copy(r):
            return pltpu.make_async_copy(w.at[:, pl.ds(r * cols, cols)], buf.at[r], sems.at[r])

        for r in range(count):
            copy(r).start()
        yield
        total = None
        for r in range(count):
            copy(r).wait()
            part = dot_t(x[:, r * cols : (r + 1) * cols], buf[r])
            total = part if total is None else total + part
        g, u = gate_ref[...], up_ref[...]
        sigma = jax.nn.sigmoid(g)
        dg = (total * u * sigma * (1.0 + g * (1.0 - sigma))).astype(BF16)
        du = (total * g * sigma).astype(BF16)
        grads[:, :units] = dg
        grads[:, units:] = du
        moment[...] = jnp.sum(dg.astype(F32) * g + du.astype(F32) * u, axis=-1, keepdims=True)

    return call(
        body,
        [("vmem", branch_grad), ("load", gate), ("load", up), ("hbm", weight)]
        + [("hbm", x) for x in after],
        [("vmem", struct((tokens, 2 * units), BF16)), ("vmem", struct((tokens, 1), F32))],
        [pltpu.VMEM((count, units, cols), BF16), pltpu.SemaphoreType.DMA((count,))],
        6, 2 * tokens * width * units, "hidden_grads",
    )


def normed_grads(plane, grads, gate_weight, up_weight):
    tokens, units = grads.shape[0], grads.shape[1] // 2
    width = gate_weight.shape[0]
    count = plane.size
    cols = width // count
    spots = plane.spots()

    def body(ins, outs, own):
        where, x, wg, wu = ins
        buf, sems = own

        def copy(i, r):
            return pltpu.make_async_copy(
                (wg, wu)[i].at[aligned(where[r], cols), :], buf.at[i, r], sems.at[i, r]
            )

        for r in plane.order():
            for i in range(2):
                copy(i, r).start()
        yield
        dg, du = x[:, :units], x[:, units:]
        for r in plane.order():
            i, j = spots[r]
            copy(0, r).wait()
            copy(1, r).wait()
            block = (dot_t(dg, buf[0, r]) + dot_t(du, buf[1, r])).astype(BF16)
            if j is None:
                outs[i][...] = block
            else:
                outs[i][j] = block

    return call(
        body, [("smem", plane.to), ("vmem", grads), ("hbm", gate_weight), ("hbm", up_weight)],
        plane.shapes(tokens, cols),
        [pltpu.VMEM((2, count, cols, units), BF16), pltpu.SemaphoreType.DMA((2, count))],
        6, 4 * tokens * width * units, "normed_grads",
    )


def token_products(left, right):
    tokens, rows = left[0].shape
    cols = right[0].shape[1] // 2
    count = len(left)

    def body(ins, outs, own):
        lefts, rights = ins[:count], ins[count:]
        flipped, held = own
        yield
        for r in range(count):
            here = slice(r * tokens, (r + 1) * tokens)
            flipped[:, here] = lefts[r][...].T
            held[here, :] = rights[r][...]
        for i in range(2):
            for start in range(0, cols, 256):
                size = min(256, cols - start)
                part = dot(flipped[...], held[:, i * cols + start : i * cols + start + size])
                outs[i][:, start : start + size] = part.astype(BF16)

    return call(
        body, [("load", x) for x in [*left, *right]], [("vmem", struct((rows, cols), BF16))] * 2,
        [pltpu.VMEM((rows, count * tokens), BF16), pltpu.VMEM((count * tokens, 2 * cols), BF16)],
        6, 4 * count * tokens * rows * cols, "token_products",
    )


def shards(
    student_in,
    norm_gain,
    gate_weight,
    up_weight,
    down_weight,
    projection,
    teacher_in,
    teacher_gate,
    teacher_up,
    teacher_down,
):
    wid, plane = Wid(), Plane()
    tokens, width = student_in.shape
    total_tokens = tokens * wid.size
    share = projection.shape[2]

    rows_at = jnp.stack(
        [wid.at(drow, dcore) for dcore in range(wid.cores) for drow in range(wid.rows)]
    ).astype(jnp.int32)
    units = teacher_gate.shape[1]
    tile = next((t for t in (256, 128) if units % t == 0), units // 2)
    first = (units // tile + 1) // 2 * tile
    x, after, sums = teacher_in, (), []
    for start, stop in ((0, first), (first, units)):
        *parts, token = teacher_sums(
            wid, None if start else rows_at, x, (teacher_gate, teacher_up), start, stop - start, after
        )
        if not start:
            x = parts.pop()
        rows = []
        for r in range(wid.rows):
            row = parts[r]
            for c, part in enumerate(parts[wid.rows :]):
                got = wid.send(part, 0, c + 1) if r == 0 else got
                row = row + got[:, r * tokens : (r + 1) * tokens].astype(F32)
            rows.append(wid.send(row.astype(BF16), r, 0) if r else row)
        sums.append(rows)
        if not start:
            normed, gate_sum, up_sum, hidden, branch, inverse_rms, token = student_forward(
                student_in, norm_gain, gate_weight, up_weight, down_weight, (token,)
            )
            after = (token,)

    hidden_blocks = [[[] for _ in range(wid.rows)] for _ in range(wid.cores)]
    for rows in sums:
        gate_rows, up_rows = (sum([row[i].astype(F32) for row in rows[1:]], rows[0][i]) for i in range(2))
        teacher_hidden = (gate_rows * jax.nn.sigmoid(gate_rows) * up_rows).astype(BF16)
        for drow, group in enumerate(wid.gather(teacher_hidden)):
            for dcore, block in enumerate(group):
                hidden_blocks[dcore][drow].append(block)
    pieces = flat(hidden_blocks)
    places = [(drow, dcore) for dcore in range(wid.cores) for drow in range(wid.rows)]

    branch = lax.psum(branch, ("grp", "hid"))

    if share % 128 == 0:
        blocks = teacher_down_blocks(plane, pieces, teacher_down)
    else:
        rows = [jnp.concatenate(row, axis=1) for row in pieces]
        blocks = plane.split(dot(jnp.concatenate(rows, axis=0), teacher_down).astype(BF16))

    target, order, marker = [], [], []
    cols = plane.scatter_sum(blocks, marker).astype(BF16)
    for i, (drow, dcore) in enumerate(places):
        block = cols[i * tokens : (i + 1) * tokens]
        target.append(wid.send(block, drow, dcore) if drow + dcore else block)
        order.append(wid.at(-drow, -dcore))
    order = jnp.stack(order).astype(jnp.int32)

    matrix = lax.optimization_barrier((projection, marker[-1]))[0].reshape(width, -1)
    summed, features = student_features(branch, student_in, matrix)

    swap_at = jnp.stack([wid.at(-drow, -dcore) for drow, dcore in places]).astype(jnp.int32)

    def swap(x, place="load", whole=(), after=()):
        made, copies = cut(swap_at, x, place, whole, after)
        return [
            wid.send(block, -drow, -dcore) if drow + dcore else block
            for block, (drow, dcore) in zip(made, places)
        ], copies

    def everyone(x):
        groups = wid.gather(x)
        return [groups[drow][dcore] for drow, dcore in places]

    normed_cols, (hidden_late,) = swap(normed, "load", (hidden,), (blocks[0],))
    hidden_all = everyone(hidden_late)

    feature_error, blocks = error_grad(
        plane, order, target, features, matrix, 1.0 / math.sqrt(total_tokens),
        normed_cols[1:] + hidden_all[1:],
    )
    summed_cols, _ = swap(summed, "load", (), (blocks[0],))
    error_all = everyone(feature_error)
    feature_share = plane.scatter_sum(blocks)
    branch_grad = assemble(plane.source, plane.gather(feature_share.astype(BF16)))
    branch_cols, _ = swap(branch_grad, "vmem")
    grads, moment = hidden_grads(
        branch_grad, gate_sum, up_sum, down_weight, summed_cols[1:] + error_all[1:]
    )
    paired_all = everyone(grads)
    moment = plane.total(moment)
    normed_share = plane.scatter_sum(normed_grads(plane, grads, gate_weight, up_weight))
    units = gate_sum.shape[1]
    share_cols = normed_share.shape[1]
    offset = plane.index * share_cols
    gain_share = lax.dynamic_slice_in_dim(norm_gain, offset, share_cols, 0)
    inputs_share = lax.dynamic_slice_in_dim(student_in, offset, share_cols, 1).astype(F32)
    input_grad = feature_share + inverse_rms * (
        normed_share * gain_share - inputs_share * inverse_rms * (moment / width)
    )

    def stack(blocks):
        return jnp.concatenate(blocks, axis=0)

    grad_proj = dot(stack(summed_cols).T, stack(error_all)).astype(BF16)
    grad_proj = grad_proj.reshape(-1, wid.size, share)
    grad_gate, grad_up = token_products(normed_cols, paired_all)
    grad_down = dot(stack(hidden_all).T, stack(branch_cols)).astype(BF16)
    return (grad_gate, grad_up, grad_down, grad_proj, input_grad)


def solution(mesh):
    in_specs = (
        P("wid", None),
        P(),
        P(None, ("grp", "hid")),
        P(None, ("grp", "hid")),
        P(("grp", "hid"), None),
        P(None, None, ("grp", "hid")),
        P(None, "wid"),
        P("wid", ("grp", "hid")),
        P("wid", ("grp", "hid")),
        P(("grp", "hid"), "wid"),
    )
    out_specs = (
        P("wid", ("grp", "hid")),
        P("wid", ("grp", "hid")),
        P(("grp", "hid"), "wid"),
        P("wid", None, ("grp", "hid")),
        P("wid", ("grp", "hid")),
    )
    return jax.shard_map(shards, mesh=mesh, in_specs=in_specs, out_specs=out_specs, check_vma=False)
```

```python
import functools
import math

import jax
import jax.numpy as jnp
from jax import lax
from jax.experimental import pallas as pl
from jax.experimental.pallas import tpu as pltpu
from jax.sharding import PartitionSpec as P

F32 = jnp.float32
BF16 = jnp.bfloat16
CORES = 2
MIB = 1 << 20

SPECS = {
    "smem": pl.BlockSpec(memory_space=pltpu.SMEM),
    "vmem": pl.BlockSpec(memory_space=pltpu.VMEM),
    "any": pl.BlockSpec(memory_space=pl.ANY),
    "load": pl.BlockSpec(memory_space=pl.ANY),
}


def dot(a, b):
    return jnp.dot(a, b, preferred_element_type=F32)


def dot_t(a, b):
    return lax.dot_general(a, b, (((1,), (1,)), ((), ())), preferred_element_type=F32)


def size_of(x):
    return x.size * jnp.dtype(x.dtype).itemsize


def call(body, ins, outs, scratch, limit, flops, name):
    loads = [i for i, (place, _) in enumerate(ins) if place == "load"]
    rooms = [pltpu.VMEM(ins[i][1].shape, ins[i][1].dtype) for i in loads]
    sems = [pltpu.SemaphoreType.DMA((len(loads),))] if loads else []

    def kernel(*refs):
        given, made = list(refs[: len(ins)]), list(refs[len(ins) : len(ins) + len(outs)])
        rest = refs[len(ins) + len(outs) :]
        own, held = rest[: len(scratch)], rest[len(scratch) : len(scratch) + len(loads)]
        arriving = []
        for k, i in enumerate(loads):
            arriving.append(pltpu.make_async_copy(given[i], held[k], rest[-1].at[k]))
            given[i] = held[k]
        for copy in arriving:
            copy.start()
        steps = body(given, made, own)
        next(steps)
        for copy in arriving:
            copy.wait()
        for _ in steps:
            pass

    total = sum(size_of(x) for _, x in ins) + sum(size_of(x) for _, x in outs)
    return pl.pallas_call(
        kernel,
        out_shape=[shape for _, shape in outs],
        in_specs=[SPECS[place] for place, _ in ins],
        out_specs=[SPECS[place] for place, _ in outs],
        scratch_shapes=[*scratch, *rooms, *sems],
        compiler_params=pltpu.CompilerParams(vmem_limit_bytes=limit * MIB),
        cost_estimate=pl.CostEstimate(flops=flops, bytes_accessed=total, transcendentals=0),
        name=name,
    )(*[x for _, x in ins])


def tie(x, *others):
    return lax.optimization_barrier((x, *others))[0]


def struct(shape, dtype):
    return jax.ShapeDtypeStruct(tuple(shape), dtype)


def aligned(position, size):
    return pl.ds(pl.multiple_of(position * size, size), size)


def shift(x, axis, step):
    size = lax.axis_size(axis)
    return lax.ppermute(x, axis, [(i, (i + step) % size) for i in range(size)])


class Wid:
    def __init__(self):
        self.size = lax.axis_size("wid")
        self.cores = CORES if self.size % CORES == 0 else 1
        self.rows = self.size // self.cores
        self.index = lax.axis_index("wid")
        self.row = self.index // self.cores
        self.core = self.index % self.cores

    def at(self, drow, dcore):
        return ((self.row + drow) % self.rows) * self.cores + (self.core + dcore) % self.cores

    def send(self, x, drow, dcore):
        pairs = []
        for i in range(self.size):
            row, core = i // self.cores, i % self.cores
            pairs.append((i, ((row + drow) % self.rows) * self.cores + (core + dcore) % self.cores))
        return lax.ppermute(x, "wid", pairs)

    def gather(self, x):
        blocks = []
        for drow in range(self.rows):
            mine = x if drow == 0 else self.send(x, -drow, 0)
            blocks.append([mine] + [self.send(mine, 0, -dcore) for dcore in range(1, self.cores)])
        return blocks


def flat(blocks):
    return [b for group in blocks for b in group]


class Plane:
    def __init__(self):
        self.ngrp, self.nhid = lax.axis_size("grp"), lax.axis_size("hid")
        self.size = self.ngrp * self.nhid
        self.g, self.h = lax.axis_index("grp"), lax.axis_index("hid")
        self.index = self.g * self.nhid + self.h
        steps = [(dg, dh) for dg in range(self.ngrp) for dh in range(self.nhid)]
        self.to = jnp.stack([self.place(dg, dh) for dg, dh in steps]).astype(jnp.int32)
        self.source = jnp.stack([self.place(-dg, -dh) for dg, dh in steps]).astype(jnp.int32)

    def place(self, dg, dh):
        return ((self.g + dg) % self.ngrp) * self.nhid + (self.h + dh) % self.nhid

    def messages(self):
        order = list(range(1, self.nhid)) + [0]
        return [order[i : i + 2] for i in range(0, self.nhid, 2)]

    def shapes(self, rows, cols):
        near = [struct((rows, cols), BF16)] * self.nhid
        far = [struct((len(m), rows, cols), BF16) for m in self.messages()] * (self.ngrp - 1)
        return [("vmem", x) for x in near + far]

    def spots(self):
        spots = [(dh, None) for dh in range(self.nhid)]
        messages = self.messages()
        for dg in range(1, self.ngrp):
            for dh in range(self.nhid):
                j = next(j for j, m in enumerate(messages) if dh in m)
                spots.append((self.nhid + (dg - 1) * len(messages) + j, messages[j].index(dh)))
        return spots

    def order(self):
        return list(range(self.nhid, self.size)) + list(range(self.nhid))

    def split(self, x):
        cols = x.shape[1] // self.size
        near = [
            lax.dynamic_slice_in_dim(x, self.place(0, dh) * cols, cols, 1) for dh in range(self.nhid)
        ]
        far = [
            jnp.stack([lax.dynamic_slice_in_dim(x, self.place(dg, dh) * cols, cols, 1) for dh in m])
            for dg in range(1, self.ngrp)
            for m in self.messages()
        ]
        return near + far

    def scatter_sum(self, blocks, marker=None):
        messages = self.messages()
        terms = [blocks[0].astype(F32)]
        for j, message in enumerate(messages):
            got = [
                shift(blocks[self.nhid + (dg - 1) * len(messages) + j], "grp", dg)
                for dg in range(1, self.ngrp)
            ]
            if message[-1] == 0:
                terms += [x[len(message) - 1].astype(F32) for x in got]
            steps = [dh for dh in message if dh]
            if steps:
                parts = add(got, [blocks[dh] for dh in steps])
                terms += [shift(part, "hid", dh).astype(F32) for part, dh in zip(parts, steps)]
                if marker is not None:
                    marker.append(parts[-1])
        return functools.reduce(lambda a, b: a + b, terms)

    def gather(self, x):
        blocks = [None] * self.size
        for dh in range(self.nhid):
            mine = x if dh == 0 else shift(x, "hid", dh)
            for dg in range(self.ngrp):
                blocks[dg * self.nhid + dh] = mine if dg == 0 else shift(mine, "grp", dg)
        return blocks


def add(received, own):
    def body(ins, outs, _):
        yield
        for i in range(len(own)):
            total = ins[len(received) + i][...].astype(F32)
            for j in range(len(received)):
                total = total + ins[j][i].astype(F32)
            outs[i][...] = total.astype(BF16)

    return call(
        body, [("vmem", x) for x in [*received, *own]], [("vmem", struct(x.shape, BF16)) for x in own],
        [], 8, len(own) * own[0].size, "add_blocks",
    )


def cut(at, x, whole=()):
    tokens, width = x.shape
    count = at.shape[0]
    cols = width // count

    def body(ins, outs, _):
        yield
        for r in range(count):
            outs[r][...] = ins[1][:, aligned(ins[0][r], cols)]
        for i in range(len(whole)):
            outs[count + i][...] = ins[2 + i][...]

    out = call(
        body, [("smem", at), ("vmem", x)] + [("vmem", y) for y in whole],
        [("vmem", struct((tokens, cols), x.dtype))] * count
        + [("vmem", struct(y.shape, y.dtype)) for y in whole],
        [], 8, x.size, "cut",
    )
    return out[:count], out[count:]


def teacher_sums(wid, rows_at, x, weights, first, cols):
    total, depth = x.shape
    tokens = total // wid.size
    held = wid.rows * tokens
    pieces = 4
    deep = depth // pieces

    def body(ins, outs, own):
        at, given, gate, up = ins[:4]
        buf, sems = own[:2]
        ordered = given if rows_at is None else outs[-1]

        def rows(r):
            return pltpu.make_async_copy(
                given.at[aligned(at[r], tokens), :], ordered.at[pl.ds(r * tokens, tokens), :], own[2].at[r]
            )

        def copy(i, k):
            here = pl.ds(k * deep, deep)
            return pltpu.make_async_copy(
                (gate, up)[i].at[here, pl.ds(first, cols)], buf.at[i, here, :], sems.at[i, k]
            )

        if rows_at is not None:
            for r in range(wid.size):
                rows(r).start()
        for i in range(2):
            for k in range(pieces):
                copy(i, k).start()
        yield
        if rows_at is not None:
            for r in range(wid.size):
                rows(r).wait()
        for i in range(2):
            for k in range(pieces):
                copy(i, k).wait()
            part = dot(ordered[...], buf[i])
            for r in range(wid.rows):
                outs[r][i] = part[r * tokens : (r + 1) * tokens]
            for c in range(1, wid.cores):
                outs[wid.rows + c - 1][i] = part[c * held : (c + 1) * held].astype(BF16)

    scratch = [pltpu.VMEM((2, depth, cols), BF16), pltpu.SemaphoreType.DMA((2, pieces))]
    if rows_at is None:
        ins, more = [("smem", jnp.zeros((1,), jnp.int32)), ("vmem", x)], []
    else:
        ins, more = [("smem", rows_at), ("any", x)], [("vmem", struct(x.shape, BF16))]
        scratch.append(pltpu.SemaphoreType.DMA((wid.size,)))
    return call(
        body, ins + [("any", w) for w in weights],
        [("vmem", struct((2, tokens, cols), F32))] * wid.rows
        + [("vmem", struct((2, held, cols), BF16))] * (wid.cores - 1)
        + more,
        scratch, 60, 4 * total * depth * cols, "teacher_sums",
    )


def teacher_down_blocks(plane, pieces, weight):
    depth, width = weight.shape
    count = plane.size
    cols = width // count
    rows = [row[0].shape[0] for row in pieces]
    total = sum(rows)
    deeps = [part.shape[1] for part in pieces[0]]
    spots = plane.spots()

    def body(ins, outs, own):
        place, parts, w = ins[0], ins[1:-1], ins[-1]
        whole, buf, result, sems = own

        def copy(k):
            here = pl.ds(sum(deeps[:k]), deeps[k])
            return pltpu.make_async_copy(w.at[here, :], buf.at[here, :], sems.at[k])

        for k in range(len(deeps)):
            copy(k).start()
        yield
        n = row = 0
        for i, line in enumerate(pieces):
            col = 0
            for part in line:
                whole[row : row + rows[i], col : col + part.shape[1]] = parts[n][...]
                col += part.shape[1]
                n += 1
            row += rows[i]
        for k in range(len(deeps)):
            copy(k).wait()
            here = slice(sum(deeps[:k]), sum(deeps[: k + 1]))
            part = dot(whole[:, here], buf[here, :])
            result[...] = part if k == 0 else result[...] + part
        for r in plane.order():
            i, j = spots[r]
            block = result[:, aligned(place[r], cols)].astype(BF16)
            if j is None:
                outs[i][...] = block
            else:
                outs[i][j] = block

    return call(
        body, [("smem", plane.to)] + [("load", x) for x in flat(pieces)] + [("any", weight)],
        plane.shapes(total, cols),
        [
            pltpu.VMEM((total, depth), BF16),
            pltpu.VMEM((depth, width), BF16),
            pltpu.VMEM((total, width), F32),
            pltpu.SemaphoreType.DMA((len(deeps),)),
        ],
        60, 2 * total * depth * width, "teacher_down",
    )


def student_forward(plane, student_in, norm_gain, gate_weight, up_weight, down_weight):
    tokens, width = student_in.shape
    spots = plane.spots()
    cols = gate_weight.shape[1]
    count = 8
    deep = width // count

    def body(ins, outs, own):
        where, x, gain, wg, wu, wd = ins
        normed, gate, up, hidden, inverse = outs[:5]
        branches = outs[5:]
        buf, down, sems, down_sems = own

        def copy(i, k):
            return pltpu.make_async_copy(
                (wg, wu)[i].at[pl.ds(k * deep, deep), :], buf.at[i, k], sems.at[i, k]
            )

        def copy_down(k):
            here = pl.ds(k * (cols // 2), cols // 2)
            return pltpu.make_async_copy(wd.at[here, :], down.at[here, :], down_sems.at[k])

        for k in range(count):
            for i in range(2):
                copy(i, k).start()
        for k in range(2):
            copy_down(k).start()
        yield
        values = x[...].astype(F32)
        inv = lax.rsqrt(jnp.sum(values * values, axis=-1, keepdims=True) / width + 1e-05)
        inverse[...] = inv
        normed[...] = (values * inv * gain[...]).astype(BF16)
        sums = [None, None]
        for k in range(count):
            for i in range(2):
                copy(i, k).wait()
                part = dot(normed[:, k * deep : (k + 1) * deep], buf[i, k])
                sums[i] = part if k == 0 else sums[i] + part
        gate[...] = sums[0]
        up[...] = sums[1]
        hidden[...] = (sums[0] * jax.nn.sigmoid(sums[0]) * sums[1]).astype(BF16)
        for k in range(2):
            copy_down(k).wait()
        share = width // plane.size
        for r in plane.order():
            i, j = spots[r]
            block = dot(hidden[...], down[:, aligned(where[r], share)]).astype(BF16)
            if j is None:
                branches[i][...] = block
            else:
                branches[i][j] = block

    return call(
        body,
        [("smem", plane.to), ("load", student_in), ("load", norm_gain.reshape(1, width))]
        + [("any", w) for w in (gate_weight, up_weight, down_weight)],
        [
            ("vmem", struct((tokens, width), BF16)),
            ("vmem", struct((tokens, cols), F32)),
            ("vmem", struct((tokens, cols), F32)),
            ("vmem", struct((tokens, cols), BF16)),
            ("vmem", struct((tokens, 1), F32)),
        ]
        + plane.shapes(tokens, width // plane.size),
        [
            pltpu.VMEM((2, count, deep, cols), BF16),
            pltpu.VMEM((cols, width), BF16),
            pltpu.SemaphoreType.DMA((2, count)),
            pltpu.SemaphoreType.DMA((2,)),
        ],
        60, 6 * tokens * width * cols, "student_forward",
    )


def student_features(at, branch, student_in, matrix):
    tokens, width = student_in.shape
    count = len(branch)
    cols = width // count
    out_cols = matrix.shape[1]

    def body(ins, outs, own):
        where, x, w = ins[:3]
        pieces = ins[3:]
        summed, features = outs
        buf, sems = own

        def copy(r):
            return pltpu.make_async_copy(w.at[aligned(where[r], cols), :], buf.at[r], sems.at[r])

        for r in range(count):
            copy(r).start()
        yield
        total = None
        for r in range(count):
            place = aligned(where[r], cols)
            block = (x[:, place].astype(F32) + pieces[r][...].astype(F32)).astype(BF16)
            summed[:, place] = block
            copy(r).wait()
            part = dot(block, buf[r])
            total = part if total is None else total + part
        features[...] = total

    return call(
        body, [("smem", at), ("load", student_in), ("any", matrix)] + [("load", x) for x in branch],
        [("vmem", struct((tokens, width), BF16)), ("vmem", struct((tokens, out_cols), F32))],
        [pltpu.VMEM((count, cols, out_cols), BF16), pltpu.SemaphoreType.DMA((count,))],
        60, 2 * tokens * width * out_cols, "student_features",
    )


def error_grad(plane, order, target, features, matrix, scale):
    tokens, out_cols = features.shape
    width = matrix.shape[0]
    count = plane.size
    cols = width // count
    parts = len(target)
    share = out_cols // parts
    spots = plane.spots()

    def body(ins, outs, own):
        where, place, feats, w = ins[:4]
        pieces = ins[4 : 4 + parts]
        error = outs[-1]
        held, buf, sems = own

        def copy(r):
            return pltpu.make_async_copy(w.at[aligned(where[r], cols), :], buf.at[r], sems.at[r])

        for r in plane.order():
            copy(r).start()
        yield
        for r in range(parts):
            held[place[r]] = pieces[r][...]
        for r in range(parts):
            here = slice(r * share, (r + 1) * share)
            error[:, here] = ((feats[:, here] - held[r].astype(F32)) * scale).astype(BF16)
        for r in plane.order():
            i, j = spots[r]
            copy(r).wait()
            block = dot_t(error[...], buf[r]).astype(BF16)
            if j is None:
                outs[i][...] = block
            else:
                outs[i][j] = block

    out = call(
        body,
        [("smem", plane.to), ("smem", order), ("load", features), ("any", matrix)]
        + [("load", x) for x in target],
        plane.shapes(tokens, cols) + [("vmem", struct((tokens, out_cols), BF16))],
        [
            pltpu.VMEM((parts, tokens, share), BF16),
            pltpu.VMEM((count, cols, out_cols), BF16),
            pltpu.SemaphoreType.DMA((count,)),
        ],
        60, 2 * tokens * width * out_cols, "error_grad",
    )
    return out[-1], out[:-1]


SPARE = 16


def hidden_grads(at, pieces, gate, up, weight):
    tokens, units = gate.shape
    width = weight.shape[1]
    count = len(pieces)
    cols = width // count

    def body(ins, outs, own):
        where, gate_ref, up_ref, w = ins[:4]
        blocks = ins[4:]
        branch_grad, grads, moment = outs
        buf, sems = own

        def copy(r):
            return pltpu.make_async_copy(w.at[:, aligned(where[r], cols)], buf.at[r], sems.at[r])

        for r in range(count):
            copy(r).start()
        yield
        total = None
        for r in range(count):
            block = blocks[r][...]
            branch_grad[:, aligned(where[r], cols)] = block
            copy(r).wait()
            part = dot_t(block, buf[r])
            total = part if total is None else total + part
        g, u = gate_ref[...], up_ref[...]
        sigma = jax.nn.sigmoid(g)
        dg = (total * u * sigma * (1.0 + g * (1.0 - sigma))).astype(BF16)
        du = (total * g * sigma).astype(BF16)
        grads[:, :units] = dg
        grads[:, units:] = du
        terms = (dg.astype(F32) * g + du.astype(F32) * u).astype(BF16)
        moment[...] = dot_t(jnp.ones((SPARE, units), BF16), terms)

    return call(
        body,
        [("smem", at), ("load", gate), ("load", up), ("any", weight)] + [("load", x) for x in pieces],
        [
            ("vmem", struct((tokens, width), BF16)),
            ("vmem", struct((tokens, 2 * units), BF16)),
            ("vmem", struct((SPARE, tokens), F32)),
        ],
        [pltpu.VMEM((count, units, cols), BF16), pltpu.SemaphoreType.DMA((count,))],
        60, 2 * tokens * width * units, "hidden_grads",
    )


def normed_grads(plane, grads, moment, gate_weight, up_weight):
    tokens, units = grads.shape[0], grads.shape[1] // 2
    width = gate_weight.shape[0]
    count = plane.size
    cols = width // count
    spots = plane.spots()

    def body(ins, outs, own):
        where, x, row, wg, wu = ins
        buf, sems = own

        def copy(i, r):
            return pltpu.make_async_copy(
                (wg, wu)[i].at[aligned(where[r], cols), :], buf.at[i, r], sems.at[i, r]
            )

        for r in plane.order():
            for i in range(2):
                copy(i, r).start()
        yield
        dg, du = x[:, :units], x[:, units:]
        for r in plane.order():
            i, j = spots[r]
            copy(0, r).wait()
            copy(1, r).wait()
            block = (dot_t(dg, buf[0, r]) + dot_t(du, buf[1, r])).astype(BF16)
            out = outs[i] if j is None else outs[i].at[j]
            out[:tokens, :] = block
            out[tokens:, :] = jnp.zeros((SPARE, cols), BF16)
            out[tokens:, :tokens] = row[...].astype(BF16)

    return call(
        body,
        [("smem", plane.to), ("load", grads), ("load", moment), ("any", gate_weight), ("any", up_weight)],
        plane.shapes(tokens + SPARE, cols),
        [pltpu.VMEM((2, count, cols, units), BF16), pltpu.SemaphoreType.DMA((2, count))],
        60, 4 * tokens * width * units, "normed_grads",
    )


def token_products(left, right):
    tokens, rows = left[0].shape
    cols = right[0].shape[1] // 2
    count = len(left)

    def body(ins, outs, own):
        lefts, rights = ins[:count], ins[count:]
        flipped, held = own
        yield
        for r in range(count):
            here = slice(r * tokens, (r + 1) * tokens)
            flipped[:, here] = lefts[r][...].T
            held[here, :] = rights[r][...]
        for i in range(2):
            for start in range(0, cols, 256):
                size = min(256, cols - start)
                part = dot(flipped[...], held[:, i * cols + start : i * cols + start + size])
                outs[i][:, start : start + size] = part.astype(BF16)

    return call(
        body, [("load", x) for x in [*left, *right]], [("vmem", struct((rows, cols), BF16))] * 2,
        [pltpu.VMEM((rows, count * tokens), BF16), pltpu.VMEM((count * tokens, 2 * cols), BF16)],
        60, 4 * count * tokens * rows * cols, "token_products",
    )


def shards(
    student_in,
    norm_gain,
    gate_weight,
    up_weight,
    down_weight,
    projection,
    teacher_in,
    teacher_gate,
    teacher_up,
    teacher_down,
):
    wid, plane = Wid(), Plane()
    tokens, width = student_in.shape
    total_tokens = tokens * wid.size
    share = projection.shape[2]

    rows_at = jnp.stack(
        [wid.at(drow, dcore) for dcore in range(wid.cores) for drow in range(wid.rows)]
    ).astype(jnp.int32)
    units = teacher_gate.shape[1]
    tile = next((t for t in (256, 128) if units % t == 0), units // 2)
    number = units // tile
    last = max(number * 2 // 7, 1)
    marks = [0, number - 2 * last, number - last, number] if number > 2 * last else [0, number]
    x, sums, sent = teacher_in, [], []
    for k, (start, stop) in enumerate(zip(marks, marks[1:])):
        if k >= 2:
            x = tie(x, *sent[k - 2])
        parts = teacher_sums(
            wid, None if k else rows_at, x, (teacher_gate, teacher_up), start * tile, (stop - start) * tile
        )
        if not k:
            *parts, x = parts
        got = [wid.send(part, 0, c + 1) for c, part in enumerate(parts[wid.rows :])]
        rows, sends = [], []
        for r in range(wid.rows):
            row = parts[r]
            for block in got:
                row = row + block[:, r * tokens : (r + 1) * tokens].astype(F32)
            if r:
                sends.append(row.astype(BF16))
                row = wid.send(sends[-1], r, 0)
            rows.append(row)
        sums.append(rows)
        sent.append(sends)

    normed, gate_sum, up_sum, hidden, inverse_rms, *blocks = student_forward(
        plane, tie(student_in, parts[0], *sent[-2 if len(sent) > 1 else -1]),
        norm_gain, gate_weight, up_weight, down_weight,
    )

    hidden_blocks = [[[] for _ in range(wid.rows)] for _ in range(wid.cores)]
    for rows in sums:
        gate_rows, up_rows = (sum([row[i].astype(F32) for row in rows[1:]], rows[0][i]) for i in range(2))
        teacher_hidden = (gate_rows * jax.nn.sigmoid(gate_rows) * up_rows).astype(BF16)
        for drow, group in enumerate(wid.gather(teacher_hidden)):
            for dcore, block in enumerate(group):
                hidden_blocks[dcore][drow].append(block)
    pieces = flat(hidden_blocks)
    places = [(drow, dcore) for dcore in range(wid.cores) for drow in range(wid.rows)]

    branch_all = plane.gather(plane.scatter_sum(blocks).astype(BF16))

    if share % 128 == 0:
        blocks = teacher_down_blocks(plane, pieces, teacher_down)
    else:
        rows = [jnp.concatenate(row, axis=1) for row in pieces]
        blocks = plane.split(dot(jnp.concatenate(rows, axis=0), teacher_down).astype(BF16))

    target, order, marker = [], [], []
    cols = plane.scatter_sum(blocks, marker).astype(BF16)
    for i, (drow, dcore) in enumerate(places):
        block = cols[i * tokens : (i + 1) * tokens]
        target.append(wid.send(block, drow, dcore) if drow + dcore else block)
        order.append(wid.at(-drow, -dcore))
    order = jnp.stack(order).astype(jnp.int32)

    matrix = tie(projection, *marker).reshape(width, -1)
    summed, features = student_features(plane.source, branch_all, student_in, matrix)

    swap_at = jnp.stack([wid.at(-drow, -dcore) for drow, dcore in places]).astype(jnp.int32)

    def swap(x, whole=()):
        made, copies = cut(swap_at, x, whole)
        return [
            wid.send(block, -drow, -dcore) if drow + dcore else block
            for block, (drow, dcore) in zip(made, places)
        ], copies

    def everyone(x):
        groups = wid.gather(x)
        return [groups[drow][dcore] for drow, dcore in places]

    normed_cols, (hidden_late,) = swap(tie(normed, blocks[0]), (hidden,))
    hidden_all = everyone(hidden_late)

    feature_error, blocks = error_grad(
        plane, order, target, tie(features, *normed_cols, *hidden_all), matrix,
        1.0 / math.sqrt(total_tokens),
    )
    summed_cols, _ = swap(tie(summed, blocks[0]))
    error_all = everyone(feature_error)
    feature_share = plane.scatter_sum(blocks)
    branch_grad, grads, moment = hidden_grads(
        plane.source, plane.gather(feature_share.astype(BF16)),
        tie(gate_sum, *summed_cols, *error_all), up_sum, down_weight,
    )
    paired_all = everyone(grads)
    blocks = normed_grads(plane, grads, moment, gate_weight, up_weight)
    marker = []
    normed_share = plane.scatter_sum(blocks, marker)
    branch_cols, _ = swap(tie(branch_grad, blocks[0]))
    moment = normed_share[tokens, :tokens].reshape(tokens, 1)
    normed_share = normed_share[:tokens]
    units = gate_sum.shape[1]
    share_cols = normed_share.shape[1]
    offset = plane.index * share_cols
    gain_share = lax.dynamic_slice_in_dim(norm_gain, offset, share_cols, 0)
    inputs_share = lax.dynamic_slice_in_dim(student_in, offset, share_cols, 1).astype(F32)
    input_grad = feature_share + inverse_rms * (
        normed_share * gain_share - inputs_share * inverse_rms * (moment / width)
    )

    def stack(blocks):
        return jnp.concatenate(blocks, axis=0)

    grad_proj = dot(stack(tie(tuple(summed_cols), *marker)).T, stack(error_all)).astype(BF16)
    grad_proj = grad_proj.reshape(-1, wid.size, share)
    grad_gate, grad_up = token_products(normed_cols, paired_all)
    grad_down = dot(stack(hidden_all).T, stack(branch_cols)).astype(BF16)
    return (grad_gate, grad_up, grad_down, grad_proj, input_grad)


def solution(mesh):
    in_specs = (
        P("wid", None),
        P(),
        P(None, ("grp", "hid")),
        P(None, ("grp", "hid")),
        P(("grp", "hid"), None),
        P(None, None, ("grp", "hid")),
        P(None, "wid"),
        P("wid", ("grp", "hid")),
        P("wid", ("grp", "hid")),
        P(("grp", "hid"), "wid"),
    )
    out_specs = (
        P("wid", ("grp", "hid")),
        P("wid", ("grp", "hid")),
        P(("grp", "hid"), "wid"),
        P("wid", None, ("grp", "hid")),
        P("wid", ("grp", "hid")),
    )
    return jax.shard_map(shards, mesh=mesh, in_specs=in_specs, out_specs=out_specs, check_vma=False)
```

```python
import functools
import math

import jax
import jax.numpy as jnp
from jax import lax
from jax.experimental import pallas as pl
from jax.experimental.pallas import tpu as pltpu
from jax.sharding import PartitionSpec as P

F32 = jnp.float32
BF16 = jnp.bfloat16
CORES = 2
MIB = 1 << 20

SPECS = {
    "smem": pl.BlockSpec(memory_space=pltpu.SMEM),
    "vmem": pl.BlockSpec(memory_space=pltpu.VMEM),
    "any": pl.BlockSpec(memory_space=pl.ANY),
    "load": pl.BlockSpec(memory_space=pl.ANY),
}


def dot(a, b):
    return jnp.dot(a, b, preferred_element_type=F32)


def dot_t(a, b):
    return lax.dot_general(a, b, (((1,), (1,)), ((), ())), preferred_element_type=F32)


def size_of(x):
    return x.size * jnp.dtype(x.dtype).itemsize


def call(body, ins, outs, scratch, limit, flops, name):
    loads = [i for i, (place, _) in enumerate(ins) if place == "load"]
    rooms = [pltpu.VMEM(ins[i][1].shape, ins[i][1].dtype) for i in loads]
    sems = [pltpu.SemaphoreType.DMA((len(loads),))] if loads else []

    def kernel(*refs):
        given, made = list(refs[: len(ins)]), list(refs[len(ins) : len(ins) + len(outs)])
        rest = refs[len(ins) + len(outs) :]
        own, held = rest[: len(scratch)], rest[len(scratch) : len(scratch) + len(loads)]
        arriving = []
        for k, i in enumerate(loads):
            arriving.append(pltpu.make_async_copy(given[i], held[k], rest[-1].at[k]))
            given[i] = held[k]
        for copy in arriving:
            copy.start()
        steps = body(given, made, own)
        next(steps)
        for copy in arriving:
            copy.wait()
        for _ in steps:
            pass

    moved = sum(size_of(x) for _, x in ins) + sum(size_of(x) for _, x in outs)
    return pl.pallas_call(
        kernel,
        out_shape=[shape for _, shape in outs],
        in_specs=[SPECS[place] for place, _ in ins],
        out_specs=[SPECS[place] for place, _ in outs],
        scratch_shapes=[*scratch, *rooms, *sems],
        compiler_params=pltpu.CompilerParams(vmem_limit_bytes=limit * MIB),
        cost_estimate=pl.CostEstimate(flops=flops, bytes_accessed=moved, transcendentals=0),
        name=name,
    )(*[x for _, x in ins])


def stream(copies, ahead):
    for copy in copies[:ahead]:
        copy.start()

    def arrive(k):
        copies[k].wait()
        if k + ahead < len(copies):
            copies[k + ahead].start()

    return arrive


def tie(x, *others):
    return lax.optimization_barrier((x, *others))[0]


def struct(shape, dtype):
    return jax.ShapeDtypeStruct(tuple(shape), dtype)


def aligned(position, size):
    return pl.ds(pl.multiple_of(position * size, size), size)


def shift(x, axis, step):
    size = lax.axis_size(axis)
    return lax.ppermute(x, axis, [(i, (i + step) % size) for i in range(size)])


class Wid:
    def __init__(self):
        self.size = lax.axis_size("wid")
        self.cores = CORES if self.size % CORES == 0 else 1
        self.rows = self.size // self.cores
        self.index = lax.axis_index("wid")
        self.row = self.index // self.cores
        self.core = self.index % self.cores

    def at(self, drow, dcore):
        return ((self.row + drow) % self.rows) * self.cores + (self.core + dcore) % self.cores

    def send(self, x, drow, dcore):
        pairs = []
        for i in range(self.size):
            row, core = i // self.cores, i % self.cores
            pairs.append((i, ((row + drow) % self.rows) * self.cores + (core + dcore) % self.cores))
        return lax.ppermute(x, "wid", pairs)

    def gather(self, x):
        blocks = []
        for drow in range(self.rows):
            mine = x if drow == 0 else self.send(x, -drow, 0)
            blocks.append([mine] + [self.send(mine, 0, -dcore) for dcore in range(1, self.cores)])
        return blocks


def flat(blocks):
    return [b for group in blocks for b in group]


class Plane:
    def __init__(self):
        self.ngrp, self.nhid = lax.axis_size("grp"), lax.axis_size("hid")
        self.size = self.ngrp * self.nhid
        self.g, self.h = lax.axis_index("grp"), lax.axis_index("hid")
        self.index = self.g * self.nhid + self.h
        steps = [(dg, dh) for dg in range(self.ngrp) for dh in range(self.nhid)]
        self.to = jnp.stack([self.place(dg, dh) for dg, dh in steps]).astype(jnp.int32)
        self.source = jnp.stack([self.place(-dg, -dh) for dg, dh in steps]).astype(jnp.int32)

    def place(self, dg, dh):
        return ((self.g + dg) % self.ngrp) * self.nhid + (self.h + dh) % self.nhid

    def messages(self):
        order = list(range(1, self.nhid)) + [0]
        return [order[i : i + 2] for i in range(0, self.nhid, 2)]

    def shapes(self, rows, cols):
        near = [struct((rows, cols), BF16)] * self.nhid
        far = [struct((len(m), rows, cols), BF16) for m in self.messages()] * (self.ngrp - 1)
        return [("vmem", x) for x in near + far]

    def spots(self):
        spots = [(dh, None) for dh in range(self.nhid)]
        messages = self.messages()
        for dg in range(1, self.ngrp):
            for dh in range(self.nhid):
                j = next(j for j, m in enumerate(messages) if dh in m)
                spots.append((self.nhid + (dg - 1) * len(messages) + j, messages[j].index(dh)))
        return spots

    def order(self):
        return list(range(self.nhid, self.size)) + list(range(self.nhid))

    def split(self, x):
        cols = x.shape[1] // self.size
        near = [
            lax.dynamic_slice_in_dim(x, self.place(0, dh) * cols, cols, 1) for dh in range(self.nhid)
        ]
        far = [
            jnp.stack([lax.dynamic_slice_in_dim(x, self.place(dg, dh) * cols, cols, 1) for dh in m])
            for dg in range(1, self.ngrp)
            for m in self.messages()
        ]
        return near + far

    def scatter_sum(self, blocks, marker=None):
        messages = self.messages()
        terms = [blocks[0].astype(F32)]
        got = []
        for j, message in enumerate(messages):
            far = [blocks[self.nhid + dg * len(messages) + j] for dg in range(self.ngrp - 1)]
            far = [tie(x, *got) if got else x for x in far]
            got = [shift(x, "grp", dg) for dg, x in enumerate(far, 1)]
            if message[-1] == 0:
                terms += [x[len(message) - 1].astype(F32) for x in got]
            steps = [dh for dh in message if dh]
            if steps:
                parts = add(got, [blocks[dh] for dh in steps])
                terms += [shift(part, "hid", dh).astype(F32) for part, dh in zip(parts, steps)]
                if marker is not None:
                    marker.append(parts[-1])
        return functools.reduce(lambda a, b: a + b, terms)

    def gather(self, x):
        blocks = [None] * self.size
        for dh in range(self.nhid):
            mine = x if dh == 0 else shift(x, "hid", dh)
            for dg in range(self.ngrp):
                blocks[dg * self.nhid + dh] = mine if dg == 0 else shift(mine, "grp", dg)
        return blocks


def add(received, own):
    def body(ins, outs, _):
        yield
        for i in range(len(own)):
            total = ins[len(received) + i][...].astype(F32)
            for j in range(len(received)):
                total = total + ins[j][i].astype(F32)
            outs[i][...] = total.astype(BF16)

    return call(
        body, [("vmem", x) for x in [*received, *own]], [("vmem", struct(x.shape, BF16)) for x in own],
        [], 8, len(own) * own[0].size, "add_blocks",
    )


def cut(at, x, whole=()):
    tokens, width = x.shape
    count = at.shape[0]
    cols = width // count

    def body(ins, outs, _):
        yield
        for r in range(count):
            outs[r][...] = ins[1][:, aligned(ins[0][r], cols)]
        for i in range(len(whole)):
            outs[count + i][...] = ins[2 + i][...]

    out = call(
        body, [("smem", at), ("vmem", x)] + [("vmem", y) for y in whole],
        [("vmem", struct((tokens, cols), x.dtype))] * count
        + [("vmem", struct(y.shape, y.dtype)) for y in whole],
        [], 8, x.size, "cut",
    )
    return out[:count], out[count:]


def teacher_sums(wid, rows_at, x, weights, first, cols):
    total, depth = x.shape
    tokens = total // wid.size
    held = wid.rows * tokens
    pieces = 4
    deep = depth // pieces

    def body(ins, outs, own):
        at, given, gate, up = ins[:4]
        buf, sems = own[:2]
        ordered = given if rows_at is None else outs[-1]

        def rows(r):
            return pltpu.make_async_copy(
                given.at[aligned(at[r], tokens), :], ordered.at[pl.ds(r * tokens, tokens), :], own[2].at[r]
            )

        def copy(i, k):
            here = pl.ds(k * deep, deep)
            return pltpu.make_async_copy(
                (gate, up)[i].at[here, pl.ds(first, cols)], buf.at[i, here, :], sems.at[i, k]
            )

        if rows_at is not None:
            for r in range(wid.size):
                rows(r).start()
        arrive = stream([copy(i, k) for i in range(2) for k in range(pieces)], pieces)
        yield
        if rows_at is not None:
            for r in range(wid.size):
                rows(r).wait()
        for i in range(2):
            part = None
            for half in range(2):
                here = slice(half * depth // 2, (half + 1) * depth // 2)
                for k in range(half * pieces // 2, (half + 1) * pieces // 2):
                    arrive(i * pieces + k)
                more = dot(ordered[:, here], buf[i, here, :])
                part = more if half == 0 else part + more
            for r in range(wid.rows):
                outs[r][i] = part[r * tokens : (r + 1) * tokens]
            for c in range(1, wid.cores):
                outs[wid.rows + c - 1][i] = part[c * held : (c + 1) * held].astype(BF16)

    scratch = [pltpu.VMEM((2, depth, cols), BF16), pltpu.SemaphoreType.DMA((2, pieces))]
    if rows_at is None:
        ins, more = [("smem", jnp.zeros((1,), jnp.int32)), ("vmem", x)], []
    else:
        ins, more = [("smem", rows_at), ("any", x)], [("vmem", struct(x.shape, BF16))]
        scratch.append(pltpu.SemaphoreType.DMA((wid.size,)))
    return call(
        body, ins + [("any", w) for w in weights],
        [("vmem", struct((2, tokens, cols), F32))] * wid.rows
        + [("vmem", struct((2, held, cols), BF16))] * (wid.cores - 1)
        + more,
        scratch, 60, 4 * total * depth * cols, "teacher_sums",
    )


def teacher_down_blocks(plane, pieces, weight):
    depth, width = weight.shape
    count = plane.size
    cols = width // count
    rows = [row[0].shape[0] for row in pieces]
    total = sum(rows)
    deeps = [part.shape[1] for part in pieces[0]]
    spots = plane.spots()

    def body(ins, outs, own):
        place, parts, w = ins[0], ins[1:-1], ins[-1]
        whole, buf, result, sems = own

        def copy(k):
            here = pl.ds(sum(deeps[:k]), deeps[k])
            return pltpu.make_async_copy(w.at[here, :], buf.at[here, :], sems.at[k])

        arrive = stream([copy(k) for k in range(len(deeps))], 2)
        yield
        n = row = 0
        for i, line in enumerate(pieces):
            col = 0
            for part in line:
                whole[row : row + rows[i], col : col + part.shape[1]] = parts[n][...]
                col += part.shape[1]
                n += 1
            row += rows[i]
        for k in range(len(deeps)):
            arrive(k)
            here = slice(sum(deeps[:k]), sum(deeps[: k + 1]))
            part = dot(whole[:, here], buf[here, :])
            result[...] = part if k == 0 else result[...] + part
        for r in plane.order():
            i, j = spots[r]
            block = result[:, aligned(place[r], cols)].astype(BF16)
            if j is None:
                outs[i][...] = block
            else:
                outs[i][j] = block

    return call(
        body, [("smem", plane.to)] + [("load", x) for x in flat(pieces)] + [("any", weight)],
        plane.shapes(total, cols),
        [
            pltpu.VMEM((total, depth), BF16),
            pltpu.VMEM((depth, width), BF16),
            pltpu.VMEM((total, width), F32),
            pltpu.SemaphoreType.DMA((len(deeps),)),
        ],
        60, 2 * total * depth * width, "teacher_down",
    )


def student_forward(plane, student_in, norm_gain, gate_weight, up_weight, down_weight):
    tokens, width = student_in.shape
    spots = plane.spots()
    cols = gate_weight.shape[1]
    count = 8
    deep = width // count

    def body(ins, outs, own):
        where, x, gain, wg, wu, wd = ins
        normed, gate, up, hidden, inverse = outs[:5]
        branches = outs[5:]
        buf, down, sems, down_sems = own

        def copy(i, k):
            return pltpu.make_async_copy(
                (wg, wu)[i].at[pl.ds(k * deep, deep), :], buf.at[i, k], sems.at[i, k]
            )

        def copy_down(k):
            here = pl.ds(k * (cols // 2), cols // 2)
            return pltpu.make_async_copy(wd.at[here, :], down.at[here, :], down_sems.at[k])

        arrive = stream(
            [copy(i, k) for k in range(count) for i in range(2)] + [copy_down(k) for k in range(2)], 4
        )
        yield
        values = x[...].astype(F32)
        inv = lax.rsqrt(jnp.sum(values * values, axis=-1, keepdims=True) / width + 1e-05)
        inverse[...] = inv
        normed[...] = (values * inv * gain[...]).astype(BF16)
        sums = [None, None]
        for k in range(count):
            for i in range(2):
                arrive(2 * k + i)
                part = dot(normed[:, k * deep : (k + 1) * deep], buf[i, k])
                sums[i] = part if k == 0 else sums[i] + part
        gate[...] = sums[0]
        up[...] = sums[1]
        hidden[...] = (sums[0] * jax.nn.sigmoid(sums[0]) * sums[1]).astype(BF16)
        for k in range(2):
            arrive(2 * count + k)
        share = width // plane.size
        for r in plane.order():
            i, j = spots[r]
            block = dot(hidden[...], down[:, aligned(where[r], share)]).astype(BF16)
            if j is None:
                branches[i][...] = block
            else:
                branches[i][j] = block

    return call(
        body,
        [("smem", plane.to), ("load", student_in), ("load", norm_gain.reshape(1, width))]
        + [("any", w) for w in (gate_weight, up_weight, down_weight)],
        [
            ("vmem", struct((tokens, width), BF16)),
            ("vmem", struct((tokens, cols), F32)),
            ("vmem", struct((tokens, cols), F32)),
            ("vmem", struct((tokens, cols), BF16)),
            ("vmem", struct((tokens, 1), F32)),
        ]
        + plane.shapes(tokens, width // plane.size),
        [
            pltpu.VMEM((2, count, deep, cols), BF16),
            pltpu.VMEM((cols, width), BF16),
            pltpu.SemaphoreType.DMA((2, count)),
            pltpu.SemaphoreType.DMA((2,)),
        ],
        60, 6 * tokens * width * cols, "student_forward",
    )


def student_features(at, branch, student_in, matrix):
    tokens, width = student_in.shape
    count = len(branch)
    cols = width // count
    out_cols = matrix.shape[1]

    def body(ins, outs, own):
        where, x, w = ins[:3]
        pieces = ins[3:]
        summed, features = outs
        buf, sems = own

        def copy(r):
            return pltpu.make_async_copy(w.at[aligned(where[r], cols), :], buf.at[r], sems.at[r])

        arrive = stream([copy(r) for r in range(count)], 3)
        yield
        total = None
        for r in range(count):
            place = aligned(where[r], cols)
            block = (x[:, place].astype(F32) + pieces[r][...].astype(F32)).astype(BF16)
            summed[:, place] = block
            arrive(r)
            part = dot(block, buf[r])
            total = part if total is None else total + part
        features[...] = total

    return call(
        body, [("smem", at), ("load", student_in), ("any", matrix)] + [("load", x) for x in branch],
        [("vmem", struct((tokens, width), BF16)), ("vmem", struct((tokens, out_cols), F32))],
        [pltpu.VMEM((count, cols, out_cols), BF16), pltpu.SemaphoreType.DMA((count,))],
        60, 2 * tokens * width * out_cols, "student_features",
    )


def error_grad(plane, order, target, features, matrix, scale):
    tokens, out_cols = features.shape
    width = matrix.shape[0]
    count = plane.size
    cols = width // count
    parts = len(target)
    share = out_cols // parts
    spots = plane.spots()

    def body(ins, outs, own):
        where, place, feats, w = ins[:4]
        pieces = ins[4 : 4 + parts]
        error = outs[-1]
        held, buf, sems = own

        def copy(r):
            return pltpu.make_async_copy(w.at[aligned(where[r], cols), :], buf.at[r], sems.at[r])

        arrive = stream([copy(r) for r in plane.order()], 3)
        yield
        for r in range(parts):
            held[place[r]] = pieces[r][...]
        for r in range(parts):
            here = slice(r * share, (r + 1) * share)
            error[:, here] = ((feats[:, here] - held[r].astype(F32)) * scale).astype(BF16)
        for k, r in enumerate(plane.order()):
            i, j = spots[r]
            arrive(k)
            block = dot_t(error[...], buf[r]).astype(BF16)
            if j is None:
                outs[i][...] = block
            else:
                outs[i][j] = block

    out = call(
        body,
        [("smem", plane.to), ("smem", order), ("load", features), ("any", matrix)]
        + [("load", x) for x in target],
        plane.shapes(tokens, cols) + [("vmem", struct((tokens, out_cols), BF16))],
        [
            pltpu.VMEM((parts, tokens, share), BF16),
            pltpu.VMEM((count, cols, out_cols), BF16),
            pltpu.SemaphoreType.DMA((count,)),
        ],
        60, 2 * tokens * width * out_cols, "error_grad",
    )
    return out[-1], out[:-1]


SPARE = 16


def hidden_grads(at, pieces, gate, up, weight):
    tokens, units = gate.shape
    width = weight.shape[1]
    count = len(pieces)
    cols = width // count

    def body(ins, outs, own):
        where, gate_ref, up_ref, w = ins[:4]
        blocks = ins[4:]
        branch_grad, grads, moment = outs
        buf, sems = own

        def copy(r):
            return pltpu.make_async_copy(w.at[:, aligned(where[r], cols)], buf.at[r], sems.at[r])

        arrive = stream([copy(r) for r in range(count)], 3)
        yield
        total = None
        for r in range(count):
            block = blocks[r][...]
            branch_grad[:, aligned(where[r], cols)] = block
            arrive(r)
            part = dot_t(block, buf[r])
            total = part if total is None else total + part
        g, u = gate_ref[...], up_ref[...]
        sigma = jax.nn.sigmoid(g)
        dg = (total * u * sigma * (1.0 + g * (1.0 - sigma))).astype(BF16)
        du = (total * g * sigma).astype(BF16)
        grads[:, :units] = dg
        grads[:, units:] = du
        terms = (dg.astype(F32) * g + du.astype(F32) * u).astype(BF16)
        moment[...] = dot_t(jnp.ones((SPARE, units), BF16), terms)

    return call(
        body,
        [("smem", at), ("load", gate), ("load", up), ("any", weight)] + [("load", x) for x in pieces],
        [
            ("vmem", struct((tokens, width), BF16)),
            ("vmem", struct((tokens, 2 * units), BF16)),
            ("vmem", struct((SPARE, tokens), F32)),
        ],
        [pltpu.VMEM((count, units, cols), BF16), pltpu.SemaphoreType.DMA((count,))],
        60, 2 * tokens * width * units, "hidden_grads",
    )


def normed_grads(plane, grads, moment, gate_weight, up_weight):
    tokens, units = grads.shape[0], grads.shape[1] // 2
    width = gate_weight.shape[0]
    count = plane.size
    cols = width // count
    spots = plane.spots()

    def body(ins, outs, own):
        where, x, row, wg, wu = ins
        buf, dg, du, sems = own

        def copy(i, r):
            return pltpu.make_async_copy(
                (wg, wu)[i].at[aligned(where[r], cols), :], buf.at[i, r], sems.at[i, r]
            )

        arrive = stream([copy(i, r) for r in plane.order() for i in range(2)], 4)
        yield
        dg[...] = x[:, :units]
        du[...] = x[:, units:]
        for k, r in enumerate(plane.order()):
            i, j = spots[r]
            arrive(2 * k)
            arrive(2 * k + 1)
            block = (dot_t(dg[...], buf[0, r]) + dot_t(du[...], buf[1, r])).astype(BF16)
            out = outs[i] if j is None else outs[i].at[j]
            out[:tokens, :] = block
            out[tokens:, :] = jnp.zeros((SPARE, cols), BF16)
            out[tokens:, :tokens] = row[...].astype(BF16)

    return call(
        body,
        [("smem", plane.to), ("load", grads), ("load", moment), ("any", gate_weight), ("any", up_weight)],
        plane.shapes(tokens + SPARE, cols),
        [
            pltpu.VMEM((2, count, cols, units), BF16),
            pltpu.VMEM((tokens, units), BF16),
            pltpu.VMEM((tokens, units), BF16),
            pltpu.SemaphoreType.DMA((2, count)),
        ],
        60, 4 * tokens * width * units, "normed_grads",
    )


def token_products(left, right):
    tokens, rows = left[0].shape
    cols = right[0].shape[1] // 2
    count = len(left)

    def body(ins, outs, own):
        lefts, rights = ins[:count], ins[count:]
        flipped, held = own
        yield
        for r in range(count):
            here = slice(r * tokens, (r + 1) * tokens)
            flipped[:, here] = lefts[r][...].T
            held[here, :] = rights[r][...]
        for i in range(2):
            for start in range(0, cols, 256):
                size = min(256, cols - start)
                part = dot(flipped[...], held[:, i * cols + start : i * cols + start + size])
                outs[i][:, start : start + size] = part.astype(BF16)

    return call(
        body, [("load", x) for x in [*left, *right]], [("vmem", struct((rows, cols), BF16))] * 2,
        [pltpu.VMEM((rows, count * tokens), BF16), pltpu.VMEM((count * tokens, 2 * cols), BF16)],
        60, 4 * count * tokens * rows * cols, "token_products",
    )


def shards(
    student_in,
    norm_gain,
    gate_weight,
    up_weight,
    down_weight,
    projection,
    teacher_in,
    teacher_gate,
    teacher_up,
    teacher_down,
):
    wid, plane = Wid(), Plane()
    tokens, width = student_in.shape
    total_tokens = tokens * wid.size
    share = projection.shape[2]

    rows_at = jnp.stack(
        [wid.at(drow, dcore) for dcore in range(wid.cores) for drow in range(wid.rows)]
    ).astype(jnp.int32)
    units = teacher_gate.shape[1]
    tile = next((t for t in (256, 128) if units % t == 0), units // 2)
    middle = (units // tile + 1) // 2 * tile
    x, sums, sends = teacher_in, [], []
    for start, stop in ((0, middle), (middle, units)):
        if start:
            x = tie(x, student[3], *sends)
        parts = teacher_sums(
            wid, None if start else rows_at, x, (teacher_gate, teacher_up), start, stop - start
        )
        if not start:
            *parts, x = parts
            student = student_forward(
                plane, tie(student_in, parts[0]), norm_gain, gate_weight, up_weight, down_weight
            )
        rows, got = [], [wid.send(part, 0, c + 1) for c, part in enumerate(parts[wid.rows :])]
        for r in range(wid.rows):
            row = parts[r]
            if r and start:
                row = tie(row, *sums[0][1:])
            for block in got:
                row = row + block[:, r * tokens : (r + 1) * tokens].astype(F32)
            if r:
                sends.append(row.astype(BF16))
                row = wid.send(sends[-1], r, 0)
            rows.append(row)
        sums.append(rows)

    normed, gate_sum, up_sum, hidden, inverse_rms, *blocks = student
    branch = plane.scatter_sum(blocks).astype(BF16)
    branch_all = plane.gather(branch)

    hidden_blocks = [[[] for _ in range(wid.rows)] for _ in range(wid.cores)]
    for rows in sums:
        gate_rows, up_rows = (sum([row[i].astype(F32) for row in rows[1:]], rows[0][i]) for i in range(2))
        teacher_hidden = (gate_rows * jax.nn.sigmoid(gate_rows) * up_rows).astype(BF16)
        for drow, group in enumerate(wid.gather(teacher_hidden)):
            for dcore, block in enumerate(group):
                hidden_blocks[dcore][drow].append(block)
    pieces = flat(hidden_blocks)
    places = [(drow, dcore) for dcore in range(wid.cores) for drow in range(wid.rows)]

    pieces[0][0] = tie(pieces[0][0], branch)
    if share % 128 == 0:
        blocks = teacher_down_blocks(plane, pieces, teacher_down)
    else:
        rows = [jnp.concatenate(row, axis=1) for row in pieces]
        blocks = plane.split(dot(jnp.concatenate(rows, axis=0), teacher_down).astype(BF16))
    blocks = list(blocks)
    blocks[-1] = tie(blocks[-1], *branch_all)

    target, order, marker = [], [], []
    cols = plane.scatter_sum(blocks, marker).astype(BF16)
    for i, (drow, dcore) in enumerate(places):
        block = cols[i * tokens : (i + 1) * tokens]
        target.append(wid.send(block, drow, dcore) if drow + dcore else block)
        order.append(wid.at(-drow, -dcore))
    order = jnp.stack(order).astype(jnp.int32)

    matrix = tie(projection, *marker).reshape(width, -1)
    summed, features = student_features(plane.source, branch_all, student_in, matrix)

    swap_at = jnp.stack([wid.at(-drow, -dcore) for drow, dcore in places]).astype(jnp.int32)

    def swap(x, whole=()):
        made, copies = cut(swap_at, x, whole)
        return [
            wid.send(block, -drow, -dcore) if drow + dcore else block
            for block, (drow, dcore) in zip(made, places)
        ], copies

    def everyone(x):
        groups = wid.gather(x)
        return [groups[drow][dcore] for drow, dcore in places]

    normed_cols, (hidden_late,) = swap(tie(normed, blocks[0]), (hidden,))
    hidden_all = everyone(hidden_late)

    feature_error, blocks = error_grad(
        plane, order, target, tie(features, *normed_cols, *hidden_all), matrix,
        1.0 / math.sqrt(total_tokens),
    )
    summed_cols, _ = swap(tie(summed, blocks[0]))
    error_all = everyone(feature_error)
    feature_share = plane.scatter_sum(blocks)
    branch_grad, grads, moment = hidden_grads(
        plane.source, plane.gather(feature_share.astype(BF16)),
        tie(gate_sum, *summed_cols, *error_all), up_sum, down_weight,
    )
    paired_all = everyone(grads)
    blocks = normed_grads(plane, grads, moment, gate_weight, up_weight)
    marker = []
    normed_share = plane.scatter_sum(blocks, marker)
    branch_cols, _ = swap(tie(branch_grad, blocks[0]))
    moment = normed_share[tokens, :tokens].reshape(tokens, 1)
    normed_share = normed_share[:tokens]
    units = gate_sum.shape[1]
    share_cols = normed_share.shape[1]
    offset = plane.index * share_cols
    gain_share = lax.dynamic_slice_in_dim(norm_gain, offset, share_cols, 0)
    inputs_share = lax.dynamic_slice_in_dim(student_in, offset, share_cols, 1).astype(F32)
    input_grad = feature_share + inverse_rms * (
        normed_share * gain_share - inputs_share * inverse_rms * (moment / width)
    )

    def stack(blocks):
        return jnp.concatenate(blocks, axis=0)

    grad_proj = dot(stack(tie(tuple(summed_cols), *marker)).T, stack(error_all)).astype(BF16)
    grad_proj = grad_proj.reshape(-1, wid.size, share)
    grad_gate, grad_up = token_products(normed_cols, paired_all)
    grad_down = dot(stack(hidden_all).T, stack(branch_cols)).astype(BF16)
    return (grad_gate, grad_up, grad_down, grad_proj, input_grad)


def solution(mesh):
    in_specs = (
        P("wid", None),
        P(),
        P(None, ("grp", "hid")),
        P(None, ("grp", "hid")),
        P(("grp", "hid"), None),
        P(None, None, ("grp", "hid")),
        P(None, "wid"),
        P("wid", ("grp", "hid")),
        P("wid", ("grp", "hid")),
        P(("grp", "hid"), "wid"),
    )
    out_specs = (
        P("wid", ("grp", "hid")),
        P("wid", ("grp", "hid")),
        P(("grp", "hid"), "wid"),
        P("wid", None, ("grp", "hid")),
        P("wid", ("grp", "hid")),
    )
    return jax.shard_map(shards, mesh=mesh, in_specs=in_specs, out_specs=out_specs, check_vma=False)
```

```python
import functools
import math

import jax
import jax.numpy as jnp
from jax import lax
from jax.experimental import pallas as pl
from jax.experimental.pallas import tpu as pltpu
from jax.sharding import PartitionSpec as P

F32 = jnp.float32
BF16 = jnp.bfloat16
CORES = 2
MIB = 1 << 20

SPECS = {
    "smem": pl.BlockSpec(memory_space=pltpu.SMEM),
    "vmem": pl.BlockSpec(memory_space=pltpu.VMEM),
    "any": pl.BlockSpec(memory_space=pl.ANY),
    "load": pl.BlockSpec(memory_space=pl.ANY),
}


def dot(a, b):
    return jnp.dot(a, b, preferred_element_type=F32)


def dot_t(a, b):
    return lax.dot_general(a, b, (((1,), (1,)), ((), ())), preferred_element_type=F32)


def size_of(x):
    return x.size * jnp.dtype(x.dtype).itemsize


def call(body, ins, outs, scratch, limit, flops, name):
    loads = [i for i, (place, _) in enumerate(ins) if place == "load"]
    rooms = [pltpu.VMEM(ins[i][1].shape, ins[i][1].dtype) for i in loads]
    sems = [pltpu.SemaphoreType.DMA((len(loads),))] if loads else []

    def kernel(*refs):
        given, made = list(refs[: len(ins)]), list(refs[len(ins) : len(ins) + len(outs)])
        rest = refs[len(ins) + len(outs) :]
        own, held = rest[: len(scratch)], rest[len(scratch) : len(scratch) + len(loads)]
        arriving = []
        for k, i in enumerate(loads):
            arriving.append(pltpu.make_async_copy(given[i], held[k], rest[-1].at[k]))
            given[i] = held[k]
        for copy in arriving:
            copy.start()
        steps = body(given, made, own)
        next(steps)
        for copy in arriving:
            copy.wait()
        for _ in steps:
            pass

    moved = sum(size_of(x) for _, x in ins) + sum(size_of(x) for _, x in outs)
    return pl.pallas_call(
        kernel,
        out_shape=[shape for _, shape in outs],
        in_specs=[SPECS[place] for place, _ in ins],
        out_specs=[SPECS[place] for place, _ in outs],
        scratch_shapes=[*scratch, *rooms, *sems],
        compiler_params=pltpu.CompilerParams(vmem_limit_bytes=limit * MIB),
        cost_estimate=pl.CostEstimate(flops=flops, bytes_accessed=moved, transcendentals=0),
        name=name,
    )(*[x for _, x in ins])


def stream(copies, ahead):
    for copy in copies[:ahead]:
        copy.start()

    def arrive(k):
        copies[k].wait()
        if k + ahead < len(copies):
            copies[k + ahead].start()

    return arrive


def tie(x, *others):
    return lax.optimization_barrier((x, *others))[0]


def struct(shape, dtype):
    return jax.ShapeDtypeStruct(tuple(shape), dtype)


def aligned(position, size):
    return pl.ds(pl.multiple_of(position * size, size), size)


def shift(x, axis, step):
    size = lax.axis_size(axis)
    return lax.ppermute(x, axis, [(i, (i + step) % size) for i in range(size)])


class Wid:
    def __init__(self):
        self.size = lax.axis_size("wid")
        self.cores = CORES if self.size % CORES == 0 else 1
        self.rows = self.size // self.cores
        self.index = lax.axis_index("wid")
        self.row = self.index // self.cores
        self.core = self.index % self.cores

    def at(self, drow, dcore):
        return ((self.row + drow) % self.rows) * self.cores + (self.core + dcore) % self.cores

    def send(self, x, drow, dcore):
        pairs = []
        for i in range(self.size):
            row, core = i // self.cores, i % self.cores
            pairs.append((i, ((row + drow) % self.rows) * self.cores + (core + dcore) % self.cores))
        return lax.ppermute(x, "wid", pairs)

    def gather(self, x):
        blocks = []
        for drow in range(self.rows):
            mine = x if drow == 0 else self.send(x, -drow, 0)
            blocks.append([mine] + [self.send(mine, 0, -dcore) for dcore in range(1, self.cores)])
        return blocks


def flat(blocks):
    return [b for group in blocks for b in group]


class Plane:
    def __init__(self):
        self.ngrp, self.nhid = lax.axis_size("grp"), lax.axis_size("hid")
        self.size = self.ngrp * self.nhid
        self.g, self.h = lax.axis_index("grp"), lax.axis_index("hid")
        self.index = self.g * self.nhid + self.h
        steps = [(dg, dh) for dg in range(self.ngrp) for dh in range(self.nhid)]
        self.to = jnp.stack([self.place(dg, dh) for dg, dh in steps]).astype(jnp.int32)
        self.source = jnp.stack([self.place(-dg, -dh) for dg, dh in steps]).astype(jnp.int32)

    def place(self, dg, dh):
        return ((self.g + dg) % self.ngrp) * self.nhid + (self.h + dh) % self.nhid

    def messages(self):
        order = list(range(1, self.nhid)) + [0]
        return [order[i : i + 2] for i in range(0, self.nhid, 2)]

    def shapes(self, rows, cols):
        near = [struct((rows, cols), BF16)] * self.nhid
        far = [struct((len(m), rows, cols), BF16) for m in self.messages()] * (self.ngrp - 1)
        return [("vmem", x) for x in near + far]

    def spots(self):
        spots = [(dh, None) for dh in range(self.nhid)]
        messages = self.messages()
        for dg in range(1, self.ngrp):
            for dh in range(self.nhid):
                j = next(j for j, m in enumerate(messages) if dh in m)
                spots.append((self.nhid + (dg - 1) * len(messages) + j, messages[j].index(dh)))
        return spots

    def order(self):
        return list(range(self.nhid, self.size)) + list(range(self.nhid))

    def split(self, x):
        cols = x.shape[1] // self.size
        near = [
            lax.dynamic_slice_in_dim(x, self.place(0, dh) * cols, cols, 1) for dh in range(self.nhid)
        ]
        far = [
            jnp.stack([lax.dynamic_slice_in_dim(x, self.place(dg, dh) * cols, cols, 1) for dh in m])
            for dg in range(1, self.ngrp)
            for m in self.messages()
        ]
        return near + far

    def send_message(self, blocks, j, after=()):
        count = len(self.messages())
        far = [blocks[self.nhid + dg * count + j] for dg in range(self.ngrp - 1)]
        if after:
            far = [tie(x, *after) for x in far]
        return [shift(x, "grp", dg) for dg, x in enumerate(far, 1)]

    def scatter_sum(self, blocks, got=None, between=None):
        messages = self.messages()
        terms = [blocks[0].astype(F32)]
        got = got or self.send_message(blocks, 0)
        done = ()
        for j, message in enumerate(messages):
            if j:
                got = self.send_message(blocks, j, got)
            if message[-1] == 0:
                terms += [x[len(message) - 1].astype(F32) for x in got]
            steps = [dh for dh in message if dh]
            if steps:
                own = [blocks[dh] for dh in steps]
                if j == len(messages) - 1 and done:
                    own[0] = tie(own[0], *done)
                parts = add(got, own)
                terms += [shift(part, "hid", dh).astype(F32) for part, dh in zip(parts, steps)]
                if j == 0 and between is not None:
                    done = between(parts)
        return functools.reduce(lambda a, b: a + b, terms)

    def gather(self, x):
        blocks = [None] * self.size
        for dh in range(self.nhid):
            mine = x if dh == 0 else shift(x, "hid", dh)
            for dg in range(self.ngrp):
                blocks[dg * self.nhid + dh] = mine if dg == 0 else shift(mine, "grp", dg)
        return blocks


def add(received, own):
    def body(ins, outs, _):
        yield
        for i in range(len(own)):
            total = ins[len(received) + i][...].astype(F32)
            for j in range(len(received)):
                total = total + ins[j][i].astype(F32)
            outs[i][...] = total.astype(BF16)

    return call(
        body, [("vmem", x) for x in [*received, *own]], [("vmem", struct(x.shape, BF16)) for x in own],
        [], 8, len(own) * own[0].size, "add_blocks",
    )


def cut(at, x, whole=()):
    tokens, width = x.shape
    count = at.shape[0]
    cols = width // count

    def body(ins, outs, _):
        yield
        for r in range(count):
            outs[r][...] = ins[1][:, aligned(ins[0][r], cols)]
        for i in range(len(whole)):
            outs[count + i][...] = ins[2 + i][...]

    out = call(
        body, [("smem", at), ("vmem", x)] + [("vmem", y) for y in whole],
        [("vmem", struct((tokens, cols), x.dtype))] * count
        + [("vmem", struct(y.shape, y.dtype)) for y in whole],
        [], 8, x.size, "cut",
    )
    return out[:count], out[count:]


def teacher_sums(wid, rows_at, x, weights, first, cols):
    total, depth = x.shape
    tokens = total // wid.size
    held = wid.rows * tokens
    pieces = 4
    deep = depth // pieces

    def body(ins, outs, own):
        at, given, gate, up = ins[:4]
        buf, sems = own[:2]
        ordered = given if rows_at is None else outs[-1]

        def rows(r):
            return pltpu.make_async_copy(
                given.at[aligned(at[r], tokens), :], ordered.at[pl.ds(r * tokens, tokens), :], own[2].at[r]
            )

        def copy(i, k):
            here = pl.ds(k * deep, deep)
            return pltpu.make_async_copy(
                (gate, up)[i].at[here, pl.ds(first, cols)], buf.at[i, here, :], sems.at[i, k]
            )

        if rows_at is not None:
            for r in range(wid.size):
                rows(r).start()
        arrive = stream([copy(i, k) for i in range(2) for k in range(pieces)], pieces)
        yield
        if rows_at is not None:
            for r in range(wid.size):
                rows(r).wait()
        for i in range(2):
            part = None
            for half in range(2):
                here = slice(half * depth // 2, (half + 1) * depth // 2)
                for k in range(half * pieces // 2, (half + 1) * pieces // 2):
                    arrive(i * pieces + k)
                more = dot(ordered[:, here], buf[i, here, :])
                part = more if half == 0 else part + more
            for r in range(wid.rows):
                outs[r][i] = part[r * tokens : (r + 1) * tokens]
            for c in range(1, wid.cores):
                outs[wid.rows + c - 1][i] = part[c * held : (c + 1) * held].astype(BF16)

    scratch = [pltpu.VMEM((2, depth, cols), BF16), pltpu.SemaphoreType.DMA((2, pieces))]
    if rows_at is None:
        ins, more = [("smem", jnp.zeros((1,), jnp.int32)), ("vmem", x)], []
    else:
        ins, more = [("smem", rows_at), ("any", x)], [("vmem", struct(x.shape, BF16))]
        scratch.append(pltpu.SemaphoreType.DMA((wid.size,)))
    return call(
        body, ins + [("any", w) for w in weights],
        [("vmem", struct((2, tokens, cols), F32))] * wid.rows
        + [("vmem", struct((2, held, cols), BF16))] * (wid.cores - 1)
        + more,
        scratch, 60, 4 * total * depth * cols, "teacher_sums",
    )


def teacher_down_blocks(plane, pieces, weight):
    depth, width = weight.shape
    count = plane.size
    cols = width // count
    rows = [row[0].shape[0] for row in pieces]
    total = sum(rows)
    deeps = [part.shape[1] for part in pieces[0]]
    spots = plane.spots()

    def body(ins, outs, own):
        place, parts, w = ins[0], ins[1:-1], ins[-1]
        whole, buf, result, sems = own

        def copy(k):
            here = pl.ds(sum(deeps[:k]), deeps[k])
            return pltpu.make_async_copy(w.at[here, :], buf.at[here, :], sems.at[k])

        arrive = stream([copy(k) for k in range(len(deeps))], 2)
        yield
        n = row = 0
        for i, line in enumerate(pieces):
            col = 0
            for part in line:
                whole[row : row + rows[i], col : col + part.shape[1]] = parts[n][...]
                col += part.shape[1]
                n += 1
            row += rows[i]
        for k in range(len(deeps)):
            arrive(k)
            here = slice(sum(deeps[:k]), sum(deeps[: k + 1]))
            part = dot(whole[:, here], buf[here, :])
            result[...] = part if k == 0 else result[...] + part
        for r in plane.order():
            i, j = spots[r]
            block = result[:, aligned(place[r], cols)].astype(BF16)
            if j is None:
                outs[i][...] = block
            else:
                outs[i][j] = block

    return call(
        body, [("smem", plane.to)] + [("load", x) for x in flat(pieces)] + [("any", weight)],
        plane.shapes(total, cols),
        [
            pltpu.VMEM((total, depth), BF16),
            pltpu.VMEM((depth, width), BF16),
            pltpu.VMEM((total, width), F32),
            pltpu.SemaphoreType.DMA((len(deeps),)),
        ],
        60, 2 * total * depth * width, "teacher_down",
    )


def student_forward(plane, student_in, norm_gain, gate_weight, up_weight, down_weight):
    tokens, width = student_in.shape
    spots = plane.spots()
    cols = gate_weight.shape[1]
    count = 8
    deep = width // count

    def body(ins, outs, own):
        where, x, gain, wg, wu, wd = ins
        normed, gate, up, hidden, inverse = outs[:5]
        branches = outs[5:]
        buf, down, sems, down_sems = own

        def copy(i, k):
            return pltpu.make_async_copy(
                (wg, wu)[i].at[pl.ds(k * deep, deep), :], buf.at[i, k], sems.at[i, k]
            )

        def copy_down(k):
            here = pl.ds(k * (cols // 2), cols // 2)
            return pltpu.make_async_copy(wd.at[here, :], down.at[here, :], down_sems.at[k])

        arrive = stream(
            [copy(i, k) for k in range(count) for i in range(2)] + [copy_down(k) for k in range(2)], 4
        )
        yield
        values = x[...].astype(F32)
        inv = lax.rsqrt(jnp.sum(values * values, axis=-1, keepdims=True) / width + 1e-05)
        inverse[...] = inv
        normed[...] = (values * inv * gain[...]).astype(BF16)
        sums = [None, None]
        for k in range(count):
            for i in range(2):
                arrive(2 * k + i)
                part = dot(normed[:, k * deep : (k + 1) * deep], buf[i, k])
                sums[i] = part if k == 0 else sums[i] + part
        gate[...] = sums[0]
        up[...] = sums[1]
        hidden[...] = (sums[0] * jax.nn.sigmoid(sums[0]) * sums[1]).astype(BF16)
        for k in range(2):
            arrive(2 * count + k)
        share = width // plane.size
        for r in plane.order():
            i, j = spots[r]
            block = dot(hidden[...], down[:, aligned(where[r], share)]).astype(BF16)
            if j is None:
                branches[i][...] = block
            else:
                branches[i][j] = block

    return call(
        body,
        [("smem", plane.to), ("load", student_in), ("load", norm_gain.reshape(1, width))]
        + [("any", w) for w in (gate_weight, up_weight, down_weight)],
        [
            ("vmem", struct((tokens, width), BF16)),
            ("vmem", struct((tokens, cols), F32)),
            ("vmem", struct((tokens, cols), F32)),
            ("vmem", struct((tokens, cols), BF16)),
            ("vmem", struct((tokens, 1), F32)),
        ]
        + plane.shapes(tokens, width // plane.size),
        [
            pltpu.VMEM((2, count, deep, cols), BF16),
            pltpu.VMEM((cols, width), BF16),
            pltpu.SemaphoreType.DMA((2, count)),
            pltpu.SemaphoreType.DMA((2,)),
        ],
        60, 6 * tokens * width * cols, "student_forward",
    )


def student_features(at, branch, student_in, matrix):
    tokens, width = student_in.shape
    count = len(branch)
    cols = width // count
    out_cols = matrix.shape[1]

    def body(ins, outs, own):
        where, x, w = ins[:3]
        pieces = ins[3:]
        summed, features = outs
        buf, sems = own

        def copy(r):
            return pltpu.make_async_copy(w.at[aligned(where[r], cols), :], buf.at[r], sems.at[r])

        arrive = stream([copy(r) for r in range(count)], 3)
        yield
        total = None
        for r in range(count):
            place = aligned(where[r], cols)
            block = (x[:, place].astype(F32) + pieces[r][...].astype(F32)).astype(BF16)
            summed[:, place] = block
            arrive(r)
            part = dot(block, buf[r])
            total = part if total is None else total + part
        features[...] = total

    return call(
        body, [("smem", at), ("load", student_in), ("any", matrix)] + [("load", x) for x in branch],
        [("vmem", struct((tokens, width), BF16)), ("vmem", struct((tokens, out_cols), F32))],
        [pltpu.VMEM((count, cols, out_cols), BF16), pltpu.SemaphoreType.DMA((count,))],
        60, 2 * tokens * width * out_cols, "student_features",
    )


def error_grad(plane, order, target, features, matrix, scale):
    tokens, out_cols = features.shape
    width = matrix.shape[0]
    count = plane.size
    cols = width // count
    parts = len(target)
    share = out_cols // parts
    spots = plane.spots()

    def body(ins, outs, own):
        where, place, feats, w = ins[:4]
        pieces = ins[4 : 4 + parts]
        error = outs[-1]
        held, buf, sems = own

        def copy(r):
            return pltpu.make_async_copy(w.at[aligned(where[r], cols), :], buf.at[r], sems.at[r])

        arrive = stream([copy(r) for r in plane.order()], 3)
        yield
        for r in range(parts):
            held[place[r]] = pieces[r][...]
        for r in range(parts):
            here = slice(r * share, (r + 1) * share)
            error[:, here] = ((feats[:, here] - held[r].astype(F32)) * scale).astype(BF16)
        for k, r in enumerate(plane.order()):
            i, j = spots[r]
            arrive(k)
            block = dot_t(error[...], buf[r]).astype(BF16)
            if j is None:
                outs[i][...] = block
            else:
                outs[i][j] = block

    out = call(
        body,
        [("smem", plane.to), ("smem", order), ("load", features), ("any", matrix)]
        + [("load", x) for x in target],
        plane.shapes(tokens, cols) + [("vmem", struct((tokens, out_cols), BF16))],
        [
            pltpu.VMEM((parts, tokens, share), BF16),
            pltpu.VMEM((count, cols, out_cols), BF16),
            pltpu.SemaphoreType.DMA((count,)),
        ],
        60, 2 * tokens * width * out_cols, "error_grad",
    )
    return out[-1], out[:-1]


SPARE = 16


def hidden_grads(at, pieces, gate, up, weight):
    tokens, units = gate.shape
    width = weight.shape[1]
    count = len(pieces)
    cols = width // count

    def body(ins, outs, own):
        where, gate_ref, up_ref, w = ins[:4]
        blocks = ins[4:]
        branch_grad, grads, moment = outs
        buf, sems = own

        def copy(r):
            return pltpu.make_async_copy(w.at[:, aligned(where[r], cols)], buf.at[r], sems.at[r])

        arrive = stream([copy(r) for r in range(count)], 3)
        yield
        total = None
        for r in range(count):
            block = blocks[r][...]
            branch_grad[:, aligned(where[r], cols)] = block
            arrive(r)
            part = dot_t(block, buf[r])
            total = part if total is None else total + part
        g, u = gate_ref[...], up_ref[...]
        sigma = jax.nn.sigmoid(g)
        dg = (total * u * sigma * (1.0 + g * (1.0 - sigma))).astype(BF16)
        du = (total * g * sigma).astype(BF16)
        grads[:, :units] = dg
        grads[:, units:] = du
        terms = (dg.astype(F32) * g + du.astype(F32) * u).astype(BF16)
        moment[...] = dot_t(jnp.ones((SPARE, units), BF16), terms)

    return call(
        body,
        [("smem", at), ("load", gate), ("load", up), ("any", weight)] + [("load", x) for x in pieces],
        [
            ("vmem", struct((tokens, width), BF16)),
            ("vmem", struct((tokens, 2 * units), BF16)),
            ("vmem", struct((SPARE, tokens), F32)),
        ],
        [pltpu.VMEM((count, units, cols), BF16), pltpu.SemaphoreType.DMA((count,))],
        60, 2 * tokens * width * units, "hidden_grads",
    )


def normed_grads(plane, grads, moment, gate_weight, up_weight):
    tokens, units = grads.shape[0], grads.shape[1] // 2
    width = gate_weight.shape[0]
    count = plane.size
    cols = width // count
    spots = plane.spots()

    def body(ins, outs, own):
        where, x, row, wg, wu = ins
        buf, dg, du, sems = own

        def copy(i, r):
            return pltpu.make_async_copy(
                (wg, wu)[i].at[aligned(where[r], cols), :], buf.at[i, r], sems.at[i, r]
            )

        arrive = stream([copy(i, r) for r in plane.order() for i in range(2)], 4)
        yield
        dg[...] = x[:, :units]
        du[...] = x[:, units:]
        for k, r in enumerate(plane.order()):
            i, j = spots[r]
            arrive(2 * k)
            arrive(2 * k + 1)
            block = (dot_t(dg[...], buf[0, r]) + dot_t(du[...], buf[1, r])).astype(BF16)
            out = outs[i] if j is None else outs[i].at[j]
            out[:tokens, :] = block
            out[tokens:, :] = jnp.zeros((SPARE, cols), BF16)
            out[tokens:, :tokens] = row[...].astype(BF16)

    return call(
        body,
        [("smem", plane.to), ("load", grads), ("load", moment), ("any", gate_weight), ("any", up_weight)],
        plane.shapes(tokens + SPARE, cols),
        [
            pltpu.VMEM((2, count, cols, units), BF16),
            pltpu.VMEM((tokens, units), BF16),
            pltpu.VMEM((tokens, units), BF16),
            pltpu.SemaphoreType.DMA((2, count)),
        ],
        60, 4 * tokens * width * units, "normed_grads",
    )


def token_products(left, right):
    tokens, rows = left[0].shape
    cols = right[0].shape[1] // 2
    count = len(left)

    def body(ins, outs, own):
        lefts, rights = ins[:count], ins[count:]
        flipped, held = own
        yield
        for r in range(count):
            here = slice(r * tokens, (r + 1) * tokens)
            flipped[:, here] = lefts[r][...].T
            held[here, :] = rights[r][...]
        for i in range(2):
            for start in range(0, cols, 256):
                size = min(256, cols - start)
                part = dot(flipped[...], held[:, i * cols + start : i * cols + start + size])
                outs[i][:, start : start + size] = part.astype(BF16)

    return call(
        body, [("load", x) for x in [*left, *right]], [("vmem", struct((rows, cols), BF16))] * 2,
        [pltpu.VMEM((rows, count * tokens), BF16), pltpu.VMEM((count * tokens, 2 * cols), BF16)],
        60, 4 * count * tokens * rows * cols, "token_products",
    )


def shards(
    student_in,
    norm_gain,
    gate_weight,
    up_weight,
    down_weight,
    projection,
    teacher_in,
    teacher_gate,
    teacher_up,
    teacher_down,
):
    wid, plane = Wid(), Plane()
    tokens, width = student_in.shape
    total_tokens = tokens * wid.size
    share = projection.shape[2]

    rows_at = jnp.stack(
        [wid.at(drow, dcore) for dcore in range(wid.cores) for drow in range(wid.rows)]
    ).astype(jnp.int32)
    units = teacher_gate.shape[1]
    tile = next((t for t in (256, 128) if units % t == 0), units // 2)
    middle = (units // tile + 1) // 2 * tile
    x, sums, sends = teacher_in, [], []
    for start, stop in ((0, middle), (middle, units)):
        if start:
            x = tie(x, student[3], *sends)
            first = plane.send_message(student[5:], 0)
        parts = teacher_sums(
            wid, None if start else rows_at, x, (teacher_gate, teacher_up), start, stop - start
        )
        if start:
            *mine, theirs = parts
            parts = (*mine, tie(theirs, *sums[0][1:], *first))
        if not start:
            *parts, x = parts
            student = student_forward(
                plane, tie(student_in, parts[0]), norm_gain, gate_weight, up_weight, down_weight
            )
        rows, got = [], [wid.send(part, 0, c + 1) for c, part in enumerate(parts[wid.rows :])]
        for r in range(wid.rows):
            row = parts[r]
            for block in got:
                row = row + block[:, r * tokens : (r + 1) * tokens].astype(F32)
            if r:
                sends.append(row.astype(BF16))
                row = wid.send(sends[-1], r, 0)
            rows.append(row)
        sums.append(rows)

    normed, gate_sum, up_sum, hidden, inverse_rms, *blocks = student
    branch = plane.scatter_sum(blocks, first).astype(BF16)
    branch_all = plane.gather(branch)

    hidden_blocks = [[[] for _ in range(wid.rows)] for _ in range(wid.cores)]
    for rows in sums:
        gate_rows, up_rows = (sum([row[i].astype(F32) for row in rows[1:]], rows[0][i]) for i in range(2))
        teacher_hidden = (gate_rows * jax.nn.sigmoid(gate_rows) * up_rows).astype(BF16)
        for drow, group in enumerate(wid.gather(teacher_hidden)):
            for dcore, block in enumerate(group):
                hidden_blocks[dcore][drow].append(block)
    pieces = flat(hidden_blocks)
    places = [(drow, dcore) for dcore in range(wid.cores) for drow in range(wid.rows)]

    pieces[0][0] = tie(pieces[0][0], *branch_all)
    if share % 128 == 0:
        blocks = teacher_down_blocks(plane, pieces, teacher_down)
    else:
        rows = [jnp.concatenate(row, axis=1) for row in pieces]
        blocks = plane.split(dot(jnp.concatenate(rows, axis=0), teacher_down).astype(BF16))

    swap_at = jnp.stack([wid.at(-drow, -dcore) for drow, dcore in places]).astype(jnp.int32)

    def swap(x, whole=()):
        made, copies = cut(swap_at, x, whole)
        return [
            wid.send(block, -drow, -dcore) if drow + dcore else block
            for block, (drow, dcore) in zip(made, places)
        ], copies

    def everyone(x):
        groups = wid.gather(x)
        return [groups[drow][dcore] for drow, dcore in places]

    normed_cols, (hidden_late,) = swap(tie(normed, blocks[0]), (hidden,))
    hidden_all = everyone(hidden_late)

    relaid = []

    def relay(parts):
        relaid.append(tie(projection, *parts).reshape(width, -1))
        return relaid

    cols = plane.scatter_sum(blocks, None, relay).astype(BF16)
    (matrix,) = relaid
    summed, features = student_features(plane.source, branch_all, student_in, matrix)
    cols = tie(cols, features)
    target, order = [], []
    for i, (drow, dcore) in enumerate(places):
        block = cols[i * tokens : (i + 1) * tokens]
        target.append(wid.send(block, drow, dcore) if drow + dcore else block)
        order.append(wid.at(-drow, -dcore))
    order = jnp.stack(order).astype(jnp.int32)

    feature_error, blocks = error_grad(
        plane, order, target, tie(features, *normed_cols, *hidden_all), matrix,
        1.0 / math.sqrt(total_tokens),
    )
    summed_cols, _ = swap(tie(summed, blocks[0]))
    error_all = everyone(feature_error)
    feature_share = plane.scatter_sum(blocks)
    branch_grad, grads, moment = hidden_grads(
        plane.source, plane.gather(feature_share.astype(BF16)),
        tie(gate_sum, *summed_cols, *error_all), up_sum, down_weight,
    )
    paired_all = everyone(grads)
    blocks = normed_grads(plane, grads, moment, gate_weight, up_weight)
    units = gate_sum.shape[1]

    def stack(blocks):
        return jnp.concatenate(blocks, axis=0)

    branch_cols, _ = swap(tie(branch_grad, blocks[0]))
    sent = []

    def keep(parts):
        sent.extend(parts)
        return ()

    normed_share = plane.scatter_sum(blocks, None, keep)
    grad_proj = dot(stack(tie(tuple(summed_cols), *sent)).T, stack(error_all)).astype(BF16)
    grad_proj = grad_proj.reshape(-1, wid.size, share)
    grad_down = dot(stack(tie(tuple(hidden_all), *sent)).T, stack(branch_cols)).astype(BF16)
    grad_gate, grad_up = token_products(normed_cols, paired_all)

    normed_share = tie(normed_share, grad_gate, grad_proj)
    moment = normed_share[tokens, :tokens].reshape(tokens, 1)
    normed_share = normed_share[:tokens]
    share_cols = normed_share.shape[1]
    offset = plane.index * share_cols
    gain_share = lax.dynamic_slice_in_dim(norm_gain, offset, share_cols, 0)
    inputs_share = lax.dynamic_slice_in_dim(student_in, offset, share_cols, 1).astype(F32)
    input_grad = feature_share + inverse_rms * (
        normed_share * gain_share - inputs_share * inverse_rms * (moment / width)
    )
    return (grad_gate, grad_up, grad_down, grad_proj, input_grad)


def solution(mesh):
    in_specs = (
        P("wid", None),
        P(),
        P(None, ("grp", "hid")),
        P(None, ("grp", "hid")),
        P(("grp", "hid"), None),
        P(None, None, ("grp", "hid")),
        P(None, "wid"),
        P("wid", ("grp", "hid")),
        P("wid", ("grp", "hid")),
        P(("grp", "hid"), "wid"),
    )
    out_specs = (
        P("wid", ("grp", "hid")),
        P("wid", ("grp", "hid")),
        P(("grp", "hid"), "wid"),
        P("wid", None, ("grp", "hid")),
        P("wid", ("grp", "hid")),
    )
    return jax.shard_map(shards, mesh=mesh, in_specs=in_specs, out_specs=out_specs, check_vma=False)
```

```python
import functools
import math

import jax
import jax.numpy as jnp
from jax import lax
from jax.experimental import pallas as pl
from jax.experimental.pallas import tpu as pltpu
from jax.sharding import PartitionSpec as P

F32 = jnp.float32
BF16 = jnp.bfloat16
CORES = 2
MIB = 1 << 20

SPECS = {
    "smem": pl.BlockSpec(memory_space=pltpu.SMEM),
    "vmem": pl.BlockSpec(memory_space=pltpu.VMEM),
    "any": pl.BlockSpec(memory_space=pl.ANY),
    "load": pl.BlockSpec(memory_space=pl.ANY),
}


def dot(a, b):
    return jnp.dot(a, b, preferred_element_type=F32)


def dot_t(a, b):
    return lax.dot_general(a, b, (((1,), (1,)), ((), ())), preferred_element_type=F32)


def size_of(x):
    return x.size * jnp.dtype(x.dtype).itemsize


def call(body, ins, outs, scratch, limit, flops, name):
    loads = [i for i, (place, _) in enumerate(ins) if place == "load"]
    rooms = [pltpu.VMEM(ins[i][1].shape, ins[i][1].dtype) for i in loads]
    sems = [pltpu.SemaphoreType.DMA((len(loads),))] if loads else []

    def kernel(*refs):
        given, made = list(refs[: len(ins)]), list(refs[len(ins) : len(ins) + len(outs)])
        rest = refs[len(ins) + len(outs) :]
        own, held = rest[: len(scratch)], rest[len(scratch) : len(scratch) + len(loads)]
        arriving = []
        for k, i in enumerate(loads):
            arriving.append(pltpu.make_async_copy(given[i], held[k], rest[-1].at[k]))
            given[i] = held[k]
        for copy in arriving:
            copy.start()
        steps = body(given, made, own)
        next(steps)
        for copy in arriving:
            copy.wait()
        for _ in steps:
            pass

    moved = sum(size_of(x) for _, x in ins) + sum(size_of(x) for _, x in outs)
    return pl.pallas_call(
        kernel,
        out_shape=[shape for _, shape in outs],
        in_specs=[SPECS[place] for place, _ in ins],
        out_specs=[SPECS[place] for place, _ in outs],
        scratch_shapes=[*scratch, *rooms, *sems],
        compiler_params=pltpu.CompilerParams(vmem_limit_bytes=limit * MIB),
        cost_estimate=pl.CostEstimate(flops=flops, bytes_accessed=moved, transcendentals=0),
        name=name,
    )(*[x for _, x in ins])


def stream(copies, ahead):
    for copy in copies[:ahead]:
        copy.start()

    def arrive(k):
        copies[k].wait()
        if k + ahead < len(copies):
            copies[k + ahead].start()

    return arrive


def tie(x, *others):
    return lax.optimization_barrier((x, *others))[0]


def struct(shape, dtype):
    return jax.ShapeDtypeStruct(tuple(shape), dtype)


def aligned(position, size):
    return pl.ds(pl.multiple_of(position * size, size), size)


def shift(x, axis, step):
    size = lax.axis_size(axis)
    return lax.ppermute(x, axis, [(i, (i + step) % size) for i in range(size)])


class Wid:
    def __init__(self):
        self.size = lax.axis_size("wid")
        self.cores = CORES if self.size % CORES == 0 else 1
        self.rows = self.size // self.cores
        self.index = lax.axis_index("wid")
        self.row = self.index // self.cores
        self.core = self.index % self.cores

    def at(self, drow, dcore):
        return ((self.row + drow) % self.rows) * self.cores + (self.core + dcore) % self.cores

    def send(self, x, drow, dcore):
        pairs = []
        for i in range(self.size):
            row, core = i // self.cores, i % self.cores
            pairs.append((i, ((row + drow) % self.rows) * self.cores + (core + dcore) % self.cores))
        return lax.ppermute(x, "wid", pairs)

    def gather(self, x):
        blocks = []
        for drow in range(self.rows):
            mine = x if drow == 0 else self.send(x, -drow, 0)
            blocks.append([mine] + [self.send(mine, 0, -dcore) for dcore in range(1, self.cores)])
        return blocks


def flat(blocks):
    return [b for group in blocks for b in group]


class Plane:
    def __init__(self):
        self.ngrp, self.nhid = lax.axis_size("grp"), lax.axis_size("hid")
        self.size = self.ngrp * self.nhid
        self.g, self.h = lax.axis_index("grp"), lax.axis_index("hid")
        self.index = self.g * self.nhid + self.h
        steps = [(dg, dh) for dg in range(self.ngrp) for dh in range(self.nhid)]
        self.to = jnp.stack([self.place(dg, dh) for dg, dh in steps]).astype(jnp.int32)
        self.source = jnp.stack([self.place(-dg, -dh) for dg, dh in steps]).astype(jnp.int32)

    def place(self, dg, dh):
        return ((self.g + dg) % self.ngrp) * self.nhid + (self.h + dh) % self.nhid

    def messages(self):
        return [[dh] for dh in [*range(1, self.nhid), 0]]

    def shapes(self, rows, cols):
        near = [struct((rows, cols), BF16)] * self.nhid
        far = [struct((len(m), rows, cols), BF16) for m in self.messages()] * (self.ngrp - 1)
        return [("vmem", x) for x in near + far]

    def spots(self):
        spots = [(dh, None) for dh in range(self.nhid)]
        messages = self.messages()
        for dg in range(1, self.ngrp):
            for dh in range(self.nhid):
                j = next(j for j, m in enumerate(messages) if dh in m)
                spots.append((self.nhid + (dg - 1) * len(messages) + j, messages[j].index(dh)))
        return spots

    def order(self):
        return list(range(self.nhid, self.size)) + list(range(self.nhid))

    def split(self, x):
        cols = x.shape[1] // self.size
        near = [
            lax.dynamic_slice_in_dim(x, self.place(0, dh) * cols, cols, 1) for dh in range(self.nhid)
        ]
        far = [
            jnp.stack([lax.dynamic_slice_in_dim(x, self.place(dg, dh) * cols, cols, 1) for dh in m])
            for dg in range(1, self.ngrp)
            for m in self.messages()
        ]
        return near + far

    def send_message(self, blocks, j, after=()):
        count = len(self.messages())
        far = [blocks[self.nhid + dg * count + j] for dg in range(self.ngrp - 1)]
        if after:
            far = [tie(x, *after) for x in far]
        return [shift(x, "grp", dg) for dg, x in enumerate(far, 1)]

    def scatter_sum(self, blocks, first=None, after=(), between=None):
        terms = [blocks[0].astype(F32)]
        done = ()
        arrived = [first or self.send_message(blocks, 0)]
        arrived += [self.send_message(blocks, j, after) for j in range(1, len(self.messages()))]
        for message, got in zip(self.messages(), arrived):
            if message[-1] == 0:
                terms += [x[len(message) - 1].astype(F32) for x in got]
            steps = [dh for dh in message if dh]
            if steps:
                own = [blocks[dh] for dh in steps]
                if done:
                    own[0] = tie(own[0], *done)
                parts = add(got, own)
                terms += [shift(part, "hid", dh).astype(F32) for part, dh in zip(parts, steps)]
                done = between(parts) if between is not None else ()
        return functools.reduce(lambda a, b: a + b, terms)

    def gather(self, x, before=()):
        blocks = [None] * self.size
        for dh in range(self.nhid):
            mine = x if dh == 0 else shift(x, "hid", dh)
            for dg in range(self.ngrp):
                sent = tie(mine, *before) if before and dh == self.nhid - 1 else mine
                blocks[dg * self.nhid + dh] = mine if dg == 0 else shift(sent, "grp", dg)
        return blocks


def add(received, own):
    def body(ins, outs, _):
        yield
        for i in range(len(own)):
            total = ins[len(received) + i][...].astype(F32)
            for j in range(len(received)):
                total = total + ins[j][i].astype(F32)
            outs[i][...] = total.astype(BF16)

    return call(
        body, [("vmem", x) for x in [*received, *own]], [("vmem", struct(x.shape, BF16)) for x in own],
        [], 8, len(own) * own[0].size, "add_blocks",
    )


def cut(at, x, whole=()):
    tokens, width = x.shape
    count = at.shape[0]
    cols = width // count

    def body(ins, outs, _):
        yield
        for r in range(count):
            outs[r][...] = ins[1][:, aligned(ins[0][r], cols)]
        for i in range(len(whole)):
            outs[count + i][...] = ins[2 + i][...]

    out = call(
        body, [("smem", at), ("vmem", x)] + [("vmem", y) for y in whole],
        [("vmem", struct((tokens, cols), x.dtype))] * count
        + [("vmem", struct(y.shape, y.dtype)) for y in whole],
        [], 8, x.size, "cut",
    )
    return out[:count], out[count:]


def teacher_sums(wid, rows_at, x, weights, first, cols):
    total, depth = x.shape
    tokens = total // wid.size
    held = wid.rows * tokens
    pieces = 4
    deep = depth // pieces

    def body(ins, outs, own):
        at, given, gate, up = ins[:4]
        buf, sems = own[:2]
        ordered = given if rows_at is None else outs[-1]

        def rows(r):
            return pltpu.make_async_copy(
                given.at[aligned(at[r], tokens), :], ordered.at[pl.ds(r * tokens, tokens), :], own[2].at[r]
            )

        def copy(i, k):
            here = pl.ds(k * deep, deep)
            return pltpu.make_async_copy(
                (gate, up)[i].at[here, pl.ds(first, cols)], buf.at[i, here, :], sems.at[i, k]
            )

        if rows_at is not None:
            for r in range(wid.size):
                rows(r).start()
        arrive = stream([copy(i, k) for i in range(2) for k in range(pieces)], pieces)
        yield
        if rows_at is not None:
            for r in range(wid.size):
                rows(r).wait()
        for i in range(2):
            part = None
            for half in range(2):
                here = slice(half * depth // 2, (half + 1) * depth // 2)
                for k in range(half * pieces // 2, (half + 1) * pieces // 2):
                    arrive(i * pieces + k)
                more = dot(ordered[:, here], buf[i, here, :])
                part = more if half == 0 else part + more
            for r in range(wid.rows):
                outs[r][i] = part[r * tokens : (r + 1) * tokens]
            for c in range(1, wid.cores):
                outs[wid.rows + c - 1][i] = part[c * held : (c + 1) * held].astype(BF16)

    scratch = [pltpu.VMEM((2, depth, cols), BF16), pltpu.SemaphoreType.DMA((2, pieces))]
    if rows_at is None:
        ins, more = [("smem", jnp.zeros((1,), jnp.int32)), ("vmem", x)], []
    else:
        ins, more = [("smem", rows_at), ("any", x)], [("vmem", struct(x.shape, BF16))]
        scratch.append(pltpu.SemaphoreType.DMA((wid.size,)))
    return call(
        body, ins + [("any", w) for w in weights],
        [("vmem", struct((2, tokens, cols), F32))] * wid.rows
        + [("vmem", struct((2, held, cols), BF16))] * (wid.cores - 1)
        + more,
        scratch, 60, 4 * total * depth * cols, "teacher_sums",
    )


def teacher_down_blocks(plane, pieces, weight):
    depth, width = weight.shape
    count = plane.size
    cols = width // count
    rows = [row[0].shape[0] for row in pieces]
    total = sum(rows)
    deeps = [part.shape[1] for part in pieces[0]]
    spots = plane.spots()

    def body(ins, outs, own):
        place, parts, w = ins[0], ins[1:-1], ins[-1]
        whole, buf, result, sems = own

        def copy(k):
            here = pl.ds(sum(deeps[:k]), deeps[k])
            return pltpu.make_async_copy(w.at[here, :], buf.at[here, :], sems.at[k])

        arrive = stream([copy(k) for k in range(len(deeps))], 2)
        yield
        n = row = 0
        for i, line in enumerate(pieces):
            col = 0
            for part in line:
                whole[row : row + rows[i], col : col + part.shape[1]] = parts[n][...]
                col += part.shape[1]
                n += 1
            row += rows[i]
        for k in range(len(deeps)):
            arrive(k)
            here = slice(sum(deeps[:k]), sum(deeps[: k + 1]))
            part = dot(whole[:, here], buf[here, :])
            result[...] = part if k == 0 else result[...] + part
        for r in plane.order():
            i, j = spots[r]
            block = result[:, aligned(place[r], cols)].astype(BF16)
            if j is None:
                outs[i][...] = block
            else:
                outs[i][j] = block

    return call(
        body, [("smem", plane.to)] + [("load", x) for x in flat(pieces)] + [("any", weight)],
        plane.shapes(total, cols),
        [
            pltpu.VMEM((total, depth), BF16),
            pltpu.VMEM((depth, width), BF16),
            pltpu.VMEM((total, width), F32),
            pltpu.SemaphoreType.DMA((len(deeps),)),
        ],
        60, 2 * total * depth * width, "teacher_down",
    )


def student_forward(plane, student_in, norm_gain, gate_weight, up_weight, down_weight):
    tokens, width = student_in.shape
    spots = plane.spots()
    cols = gate_weight.shape[1]
    count = 8
    deep = width // count

    def body(ins, outs, own):
        where, x, gain, wg, wu, wd = ins
        normed, gate, up, hidden, inverse = outs[:5]
        branches = outs[5:]
        buf, down, sems, down_sems = own

        def copy(i, k):
            return pltpu.make_async_copy(
                (wg, wu)[i].at[pl.ds(k * deep, deep), :], buf.at[i, k], sems.at[i, k]
            )

        def copy_down(k):
            here = pl.ds(k * (cols // 2), cols // 2)
            return pltpu.make_async_copy(wd.at[here, :], down.at[here, :], down_sems.at[k])

        arrive = stream(
            [copy(i, k) for k in range(count) for i in range(2)] + [copy_down(k) for k in range(2)], 4
        )
        yield
        values = x[...].astype(F32)
        inv = lax.rsqrt(jnp.sum(values * values, axis=-1, keepdims=True) / width + 1e-05)
        inverse[...] = inv
        normed[...] = (values * inv * gain[...]).astype(BF16)
        sums = [None, None]
        for k in range(count):
            for i in range(2):
                arrive(2 * k + i)
                part = dot(normed[:, k * deep : (k + 1) * deep], buf[i, k])
                sums[i] = part if k == 0 else sums[i] + part
        gate[...] = sums[0]
        up[...] = sums[1]
        hidden[...] = (sums[0] * jax.nn.sigmoid(sums[0]) * sums[1]).astype(BF16)
        for k in range(2):
            arrive(2 * count + k)
        share = width // plane.size
        for r in plane.order():
            i, j = spots[r]
            block = dot(hidden[...], down[:, aligned(where[r], share)]).astype(BF16)
            if j is None:
                branches[i][...] = block
            else:
                branches[i][j] = block

    return call(
        body,
        [("smem", plane.to), ("load", student_in), ("load", norm_gain.reshape(1, width))]
        + [("any", w) for w in (gate_weight, up_weight, down_weight)],
        [
            ("vmem", struct((tokens, width), BF16)),
            ("vmem", struct((tokens, cols), F32)),
            ("vmem", struct((tokens, cols), F32)),
            ("vmem", struct((tokens, cols), BF16)),
            ("vmem", struct((tokens, 1), F32)),
        ]
        + plane.shapes(tokens, width // plane.size),
        [
            pltpu.VMEM((2, count, deep, cols), BF16),
            pltpu.VMEM((cols, width), BF16),
            pltpu.SemaphoreType.DMA((2, count)),
            pltpu.SemaphoreType.DMA((2,)),
        ],
        60, 6 * tokens * width * cols, "student_forward",
    )


def student_features(at, branch, student_in, matrix):
    tokens, width = student_in.shape
    count = len(branch)
    cols = width // count
    out_cols = matrix.shape[1]

    def body(ins, outs, own):
        where, x, w = ins[:3]
        pieces = ins[3:]
        summed, features = outs
        buf, sems = own

        def copy(r):
            return pltpu.make_async_copy(w.at[aligned(where[r], cols), :], buf.at[r], sems.at[r])

        arrive = stream([copy(r) for r in range(count)], 3)
        yield
        total = None
        for r in range(count):
            place = aligned(where[r], cols)
            block = (x[:, place].astype(F32) + pieces[r][...].astype(F32)).astype(BF16)
            summed[:, place] = block
            arrive(r)
            part = dot(block, buf[r])
            total = part if total is None else total + part
        features[...] = total

    return call(
        body, [("smem", at), ("load", student_in), ("any", matrix)] + [("load", x) for x in branch],
        [("vmem", struct((tokens, width), BF16)), ("vmem", struct((tokens, out_cols), F32))],
        [pltpu.VMEM((count, cols, out_cols), BF16), pltpu.SemaphoreType.DMA((count,))],
        60, 2 * tokens * width * out_cols, "student_features",
    )


def error_grad(plane, order, target, features, matrix, scale):
    tokens, out_cols = features.shape
    width = matrix.shape[0]
    count = plane.size
    cols = width // count
    parts = len(target)
    share = out_cols // parts
    spots = plane.spots()

    def body(ins, outs, own):
        where, place, feats, w = ins[:4]
        pieces = ins[4 : 4 + parts]
        error = outs[-1]
        held, buf, sems = own

        def copy(r):
            return pltpu.make_async_copy(w.at[aligned(where[r], cols), :], buf.at[r], sems.at[r])

        arrive = stream([copy(r) for r in plane.order()], 3)
        yield
        for r in range(parts):
            held[place[r]] = pieces[r][...]
        for r in range(parts):
            here = slice(r * share, (r + 1) * share)
            error[:, here] = ((feats[:, here] - held[r].astype(F32)) * scale).astype(BF16)
        for k, r in enumerate(plane.order()):
            i, j = spots[r]
            arrive(k)
            block = dot_t(error[...], buf[r]).astype(BF16)
            if j is None:
                outs[i][...] = block
            else:
                outs[i][j] = block

    out = call(
        body,
        [("smem", plane.to), ("smem", order), ("load", features), ("any", matrix)]
        + [("load", x) for x in target],
        plane.shapes(tokens, cols) + [("vmem", struct((tokens, out_cols), BF16))],
        [
            pltpu.VMEM((parts, tokens, share), BF16),
            pltpu.VMEM((count, cols, out_cols), BF16),
            pltpu.SemaphoreType.DMA((count,)),
        ],
        60, 2 * tokens * width * out_cols, "error_grad",
    )
    return out[-1], out[:-1]


SPARE = 16


def hidden_grads(at, pieces, gate, up, weight):
    tokens, units = gate.shape
    width = weight.shape[1]
    count = len(pieces)
    cols = width // count

    def body(ins, outs, own):
        where, gate_ref, up_ref, w = ins[:4]
        blocks = ins[4:]
        branch_grad, grads, moment = outs
        buf, sems = own

        def copy(r):
            return pltpu.make_async_copy(w.at[:, aligned(where[r], cols)], buf.at[r], sems.at[r])

        arrive = stream([copy(r) for r in range(count)], 3)
        yield
        total = None
        for r in range(count):
            block = blocks[r][...]
            branch_grad[:, aligned(where[r], cols)] = block
            arrive(r)
            part = dot_t(block, buf[r])
            total = part if total is None else total + part
        g, u = gate_ref[...], up_ref[...]
        sigma = jax.nn.sigmoid(g)
        dg = (total * u * sigma * (1.0 + g * (1.0 - sigma))).astype(BF16)
        du = (total * g * sigma).astype(BF16)
        grads[:, :units] = dg
        grads[:, units:] = du
        terms = (dg.astype(F32) * g + du.astype(F32) * u).astype(BF16)
        moment[...] = dot_t(jnp.ones((SPARE, units), BF16), terms)

    return call(
        body,
        [("smem", at), ("load", gate), ("load", up), ("any", weight)] + [("load", x) for x in pieces],
        [
            ("vmem", struct((tokens, width), BF16)),
            ("vmem", struct((tokens, 2 * units), BF16)),
            ("vmem", struct((SPARE, tokens), F32)),
        ],
        [pltpu.VMEM((count, units, cols), BF16), pltpu.SemaphoreType.DMA((count,))],
        60, 2 * tokens * width * units, "hidden_grads",
    )


def normed_grads(plane, grads, moment, gate_weight, up_weight):
    tokens, units = grads.shape[0], grads.shape[1] // 2
    width = gate_weight.shape[0]
    count = plane.size
    cols = width // count
    spots = plane.spots()

    def body(ins, outs, own):
        where, x, row, wg, wu = ins
        buf, dg, du, sems = own

        def copy(i, r):
            return pltpu.make_async_copy(
                (wg, wu)[i].at[aligned(where[r], cols), :], buf.at[i, r], sems.at[i, r]
            )

        arrive = stream([copy(i, r) for r in plane.order() for i in range(2)], 4)
        yield
        dg[...] = x[:, :units]
        du[...] = x[:, units:]
        for k, r in enumerate(plane.order()):
            i, j = spots[r]
            arrive(2 * k)
            arrive(2 * k + 1)
            block = (dot_t(dg[...], buf[0, r]) + dot_t(du[...], buf[1, r])).astype(BF16)
            out = outs[i] if j is None else outs[i].at[j]
            out[:tokens, :] = block
            out[tokens:, :] = jnp.zeros((SPARE, cols), BF16)
            out[tokens:, :tokens] = row[...].astype(BF16)

    return call(
        body,
        [("smem", plane.to), ("load", grads), ("load", moment), ("any", gate_weight), ("any", up_weight)],
        plane.shapes(tokens + SPARE, cols),
        [
            pltpu.VMEM((2, count, cols, units), BF16),
            pltpu.VMEM((tokens, units), BF16),
            pltpu.VMEM((tokens, units), BF16),
            pltpu.SemaphoreType.DMA((2, count)),
        ],
        60, 4 * tokens * width * units, "normed_grads",
    )


def token_products(left, right):
    tokens, rows = left[0].shape
    cols = right[0].shape[1] // 2
    count = len(left)

    def body(ins, outs, own):
        lefts, rights = ins[:count], ins[count:]
        flipped, held = own
        yield
        for r in range(count):
            here = slice(r * tokens, (r + 1) * tokens)
            flipped[:, here] = lefts[r][...].T
            held[here, :] = rights[r][...]
        for i in range(2):
            for start in range(0, cols, 256):
                size = min(256, cols - start)
                part = dot(flipped[...], held[:, i * cols + start : i * cols + start + size])
                outs[i][:, start : start + size] = part.astype(BF16)

    return call(
        body, [("load", x) for x in [*left, *right]], [("vmem", struct((rows, cols), BF16))] * 2,
        [pltpu.VMEM((rows, count * tokens), BF16), pltpu.VMEM((count * tokens, 2 * cols), BF16)],
        60, 4 * count * tokens * rows * cols, "token_products",
    )


def shards(
    student_in,
    norm_gain,
    gate_weight,
    up_weight,
    down_weight,
    projection,
    teacher_in,
    teacher_gate,
    teacher_up,
    teacher_down,
):
    wid, plane = Wid(), Plane()
    tokens, width = student_in.shape
    total_tokens = tokens * wid.size
    share = projection.shape[2]

    rows_at = jnp.stack(
        [wid.at(drow, dcore) for dcore in range(wid.cores) for drow in range(wid.rows)]
    ).astype(jnp.int32)
    units = teacher_gate.shape[1]
    tile = next((t for t in (256, 128) if units % t == 0), units // 2)
    middle = (units // tile + 1) // 2 * tile
    x, sums, sends = teacher_in, [], []
    for start, stop in ((0, middle), (middle, units)):
        if start:
            x = tie(x, student[3], *sends)
            first = plane.send_message(student[5:], 0)
        parts = teacher_sums(
            wid, None if start else rows_at, x, (teacher_gate, teacher_up), start, stop - start
        )
        if start:
            *mine, theirs = parts
            parts = (*mine, tie(theirs, *sums[0][1:], *first))
        if not start:
            *parts, x = parts
            student = student_forward(
                plane, tie(student_in, parts[0]), norm_gain, gate_weight, up_weight, down_weight
            )
        rows, got = [], [wid.send(part, 0, c + 1) for c, part in enumerate(parts[wid.rows :])]
        for r in range(wid.rows):
            row = parts[r]
            for block in got:
                row = row + block[:, r * tokens : (r + 1) * tokens].astype(F32)
            if r:
                sends.append(row.astype(BF16))
                row = wid.send(sends[-1], r, 0)
            rows.append(row)
        sums.append(rows)

    normed, gate_sum, up_sum, hidden, inverse_rms, *blocks = student
    branch = plane.scatter_sum(blocks, first, tuple(sends[wid.rows - 1 :])).astype(BF16)
    branch_all = plane.gather(branch)

    hidden_blocks = [[[] for _ in range(wid.rows)] for _ in range(wid.cores)]
    for rows in sums:
        gate_rows, up_rows = (sum([row[i].astype(F32) for row in rows[1:]], rows[0][i]) for i in range(2))
        teacher_hidden = (gate_rows * jax.nn.sigmoid(gate_rows) * up_rows).astype(BF16)
        for drow, group in enumerate(wid.gather(teacher_hidden)):
            for dcore, block in enumerate(group):
                hidden_blocks[dcore][drow].append(block)
    pieces = flat(hidden_blocks)
    places = [(drow, dcore) for dcore in range(wid.cores) for drow in range(wid.rows)]

    if share % 128 == 0:
        blocks = teacher_down_blocks(plane, pieces, teacher_down)
    else:
        rows = [jnp.concatenate(row, axis=1) for row in pieces]
        blocks = plane.split(dot(jnp.concatenate(rows, axis=0), teacher_down).astype(BF16))

    swap_at = jnp.stack([wid.at(-drow, -dcore) for drow, dcore in places]).astype(jnp.int32)

    def swap(x, whole=()):
        made, copies = cut(swap_at, x, whole)
        return [
            wid.send(block, -drow, -dcore) if drow + dcore else block
            for block, (drow, dcore) in zip(made, places)
        ], copies

    def everyone(x):
        groups = wid.gather(x)
        return [groups[drow][dcore] for drow, dcore in places]

    blocks = list(blocks)
    blocks[-1] = tie(blocks[-1], *branch_all)
    normed_cols, (hidden_late,) = swap(tie(normed, blocks[0]), (hidden,))
    hidden_all = everyone(hidden_late)

    relaid = []

    def relay(parts):
        if relaid:
            return ()
        relaid.append(tie(projection, *parts).reshape(width, -1))
        return tuple(relaid)

    cols = plane.scatter_sum(blocks, between=relay).astype(BF16)
    (matrix,) = relaid
    summed, features = student_features(plane.source, branch_all, student_in, matrix)
    cols = tie(cols, features)
    target, order = [], []
    for i, (drow, dcore) in enumerate(places):
        block = cols[i * tokens : (i + 1) * tokens]
        target.append(wid.send(block, drow, dcore) if drow + dcore else block)
        order.append(wid.at(-drow, -dcore))
    order = jnp.stack(order).astype(jnp.int32)

    feature_error, blocks = error_grad(
        plane, order, target, tie(features, *normed_cols, *hidden_all), matrix,
        1.0 / math.sqrt(total_tokens),
    )
    summed_cols, _ = swap(tie(summed, blocks[0]))
    error_all = everyone(feature_error)
    feature_share = plane.scatter_sum(blocks)

    def stack(blocks):
        return jnp.concatenate(blocks, axis=0)

    grad_proj = dot(stack(tie(tuple(summed_cols), feature_share)).T, stack(error_all)).astype(BF16)
    grad_proj = grad_proj.reshape(-1, wid.size, share)
    branch_grad, grads, moment = hidden_grads(
        plane.source, plane.gather(feature_share.astype(BF16), (grad_proj,)),
        gate_sum, up_sum, down_weight,
    )
    paired_all = everyone(grads)
    blocks = normed_grads(plane, grads, moment, gate_weight, up_weight)
    units = gate_sum.shape[1]

    branch_cols, _ = swap(tie(branch_grad, blocks[0]))
    sent = []

    def keep(parts):
        sent.extend(parts)
        return ()

    normed_share = plane.scatter_sum(blocks, between=keep)
    grad_down = dot(stack(tie(tuple(hidden_all), sent[-1])).T, stack(branch_cols)).astype(BF16)
    grad_gate, grad_up = token_products(normed_cols, paired_all)

    normed_share = tie(normed_share, grad_gate)
    moment = normed_share[tokens, :tokens].reshape(tokens, 1)
    normed_share = normed_share[:tokens]
    share_cols = normed_share.shape[1]
    offset = plane.index * share_cols
    gain_share = lax.dynamic_slice_in_dim(norm_gain, offset, share_cols, 0)
    inputs_share = lax.dynamic_slice_in_dim(student_in, offset, share_cols, 1).astype(F32)
    input_grad = feature_share + inverse_rms * (
        normed_share * gain_share - inputs_share * inverse_rms * (moment / width)
    )
    return (grad_gate, grad_up, grad_down, grad_proj, input_grad)


def solution(mesh):
    in_specs = (
        P("wid", None),
        P(),
        P(None, ("grp", "hid")),
        P(None, ("grp", "hid")),
        P(("grp", "hid"), None),
        P(None, None, ("grp", "hid")),
        P(None, "wid"),
        P("wid", ("grp", "hid")),
        P("wid", ("grp", "hid")),
        P(("grp", "hid"), "wid"),
    )
    out_specs = (
        P("wid", ("grp", "hid")),
        P("wid", ("grp", "hid")),
        P(("grp", "hid"), "wid"),
        P("wid", None, ("grp", "hid")),
        P("wid", ("grp", "hid")),
    )
    return jax.shard_map(shards, mesh=mesh, in_specs=in_specs, out_specs=out_specs, check_vma=False)
```

```python
import functools
import math

import jax
import jax.numpy as jnp
from jax import lax
from jax.experimental import pallas as pl
from jax.experimental.pallas import tpu as pltpu
from jax.sharding import PartitionSpec as P

F32 = jnp.float32
BF16 = jnp.bfloat16
CORES = 2
MIB = 1 << 20

SPECS = {
    "smem": pl.BlockSpec(memory_space=pltpu.SMEM),
    "vmem": pl.BlockSpec(memory_space=pltpu.VMEM),
    "any": pl.BlockSpec(memory_space=pl.ANY),
    "load": pl.BlockSpec(memory_space=pl.ANY),
}


def dot(a, b):
    return jnp.dot(a, b, preferred_element_type=F32)


def dot_t(a, b):
    return lax.dot_general(a, b, (((1,), (1,)), ((), ())), preferred_element_type=F32)


def size_of(x):
    return x.size * jnp.dtype(x.dtype).itemsize


def call(body, ins, outs, scratch, limit, flops, name):
    loads = [i for i, (place, _) in enumerate(ins) if place == "load"]
    rooms = [pltpu.VMEM(ins[i][1].shape, ins[i][1].dtype) for i in loads]
    sems = [pltpu.SemaphoreType.DMA((len(loads),))] if loads else []

    def kernel(*refs):
        given, made = list(refs[: len(ins)]), list(refs[len(ins) : len(ins) + len(outs)])
        rest = refs[len(ins) + len(outs) :]
        own, held = rest[: len(scratch)], rest[len(scratch) : len(scratch) + len(loads)]
        arriving = []
        for k, i in enumerate(loads):
            arriving.append(pltpu.make_async_copy(given[i], held[k], rest[-1].at[k]))
            given[i] = held[k]
        for copy in arriving:
            copy.start()
        steps = body(given, made, own)
        next(steps)
        for copy in arriving:
            copy.wait()
        for _ in steps:
            pass

    moved = sum(size_of(x) for _, x in ins) + sum(size_of(x) for _, x in outs)
    return pl.pallas_call(
        kernel,
        out_shape=[shape for _, shape in outs],
        in_specs=[SPECS[place] for place, _ in ins],
        out_specs=[SPECS[place] for place, _ in outs],
        scratch_shapes=[*scratch, *rooms, *sems],
        compiler_params=pltpu.CompilerParams(vmem_limit_bytes=limit * MIB),
        cost_estimate=pl.CostEstimate(flops=flops, bytes_accessed=moved, transcendentals=0),
        name=name,
    )(*[x for _, x in ins])


def stream(copies, ahead):
    for copy in copies[:ahead]:
        copy.start()

    def arrive(k):
        copies[k].wait()
        if k + ahead < len(copies):
            copies[k + ahead].start()

    return arrive


def tie(x, *others):
    return lax.optimization_barrier((x, *others))[0]


def struct(shape, dtype):
    return jax.ShapeDtypeStruct(tuple(shape), dtype)


def aligned(position, size):
    return pl.ds(pl.multiple_of(position * size, size), size)


def shift(x, axis, step):
    size = lax.axis_size(axis)
    return lax.ppermute(x, axis, [(i, (i + step) % size) for i in range(size)])


class Wid:
    def __init__(self):
        self.size = lax.axis_size("wid")
        self.cores = CORES if self.size % CORES == 0 else 1
        self.rows = self.size // self.cores
        self.index = lax.axis_index("wid")
        self.row = self.index // self.cores
        self.core = self.index % self.cores

    def at(self, drow, dcore):
        return ((self.row + drow) % self.rows) * self.cores + (self.core + dcore) % self.cores

    def send(self, x, drow, dcore):
        pairs = []
        for i in range(self.size):
            row, core = i // self.cores, i % self.cores
            pairs.append((i, ((row + drow) % self.rows) * self.cores + (core + dcore) % self.cores))
        return lax.ppermute(x, "wid", pairs)

    def gather(self, x):
        blocks = []
        for drow in range(self.rows):
            mine = x if drow == 0 else self.send(x, -drow, 0)
            blocks.append([mine] + [self.send(mine, 0, -dcore) for dcore in range(1, self.cores)])
        return blocks


def flat(blocks):
    return [b for group in blocks for b in group]


class Plane:
    def __init__(self):
        self.ngrp, self.nhid = lax.axis_size("grp"), lax.axis_size("hid")
        self.size = self.ngrp * self.nhid
        self.g, self.h = lax.axis_index("grp"), lax.axis_index("hid")
        self.index = self.g * self.nhid + self.h
        steps = [(dg, dh) for dg in range(self.ngrp) for dh in range(self.nhid)]
        self.to = jnp.stack([self.place(dg, dh) for dg, dh in steps]).astype(jnp.int32)
        self.source = jnp.stack([self.place(-dg, -dh) for dg, dh in steps]).astype(jnp.int32)

    def place(self, dg, dh):
        return ((self.g + dg) % self.ngrp) * self.nhid + (self.h + dh) % self.nhid

    def messages(self):
        return [[dh] for dh in [*range(1, self.nhid), 0]]

    def shapes(self, rows, cols):
        near = [struct((rows, cols), BF16)] * self.nhid
        far = [struct((len(m), rows, cols), BF16) for m in self.messages()] * (self.ngrp - 1)
        return [("vmem", x) for x in near + far]

    def spots(self):
        spots = [(dh, None) for dh in range(self.nhid)]
        messages = self.messages()
        for dg in range(1, self.ngrp):
            for dh in range(self.nhid):
                j = next(j for j, m in enumerate(messages) if dh in m)
                spots.append((self.nhid + (dg - 1) * len(messages) + j, messages[j].index(dh)))
        return spots

    def order(self):
        return list(range(self.nhid, self.size)) + list(range(self.nhid))

    def split(self, x):
        cols = x.shape[1] // self.size
        near = [
            lax.dynamic_slice_in_dim(x, self.place(0, dh) * cols, cols, 1) for dh in range(self.nhid)
        ]
        far = [
            jnp.stack([lax.dynamic_slice_in_dim(x, self.place(dg, dh) * cols, cols, 1) for dh in m])
            for dg in range(1, self.ngrp)
            for m in self.messages()
        ]
        return near + far

    def send_message(self, blocks, j, after=()):
        count = len(self.messages())
        far = [blocks[self.nhid + dg * count + j] for dg in range(self.ngrp - 1)]
        if after:
            far = [tie(x, *after) for x in far]
        return [shift(x, "grp", dg) for dg, x in enumerate(far, 1)]

    def scatter_sum(self, blocks, first=None, after=(), between=None):
        terms = [blocks[0].astype(F32)]
        done = ()
        arrived = [first or self.send_message(blocks, 0)]
        arrived += [self.send_message(blocks, j, after) for j in range(1, len(self.messages()))]
        for message, got in zip(self.messages(), arrived):
            if message[-1] == 0:
                terms += [x[len(message) - 1].astype(F32) for x in got]
            steps = [dh for dh in message if dh]
            if steps:
                own = [blocks[dh] for dh in steps]
                if done:
                    own[0] = tie(own[0], *done)
                parts = add(got, own)
                landed = [shift(part, "hid", dh) for part, dh in zip(parts, steps)]
                terms += [x.astype(F32) for x in landed]
                done = between(parts, landed) if between is not None else ()
        return functools.reduce(lambda a, b: a + b, terms)

    def gather(self, x, before=()):
        blocks = [None] * self.size
        for dh in range(self.nhid):
            mine = x if dh == 0 else shift(x, "hid", dh)
            for dg in range(self.ngrp):
                sent = tie(mine, *before) if before and dh == self.nhid - 1 else mine
                blocks[dg * self.nhid + dh] = mine if dg == 0 else shift(sent, "grp", dg)
        return blocks


def add(received, own):
    def body(ins, outs, _):
        yield
        for i in range(len(own)):
            total = ins[len(received) + i][...].astype(F32)
            for j in range(len(received)):
                total = total + ins[j][i].astype(F32)
            outs[i][...] = total.astype(BF16)

    return call(
        body, [("vmem", x) for x in [*received, *own]], [("vmem", struct(x.shape, BF16)) for x in own],
        [], 8, len(own) * own[0].size, "add_blocks",
    )


def cut(at, x, whole=()):
    tokens, width = x.shape
    count = at.shape[0]
    cols = width // count

    def body(ins, outs, _):
        yield
        for r in range(count):
            outs[r][...] = ins[1][:, aligned(ins[0][r], cols)]
        for i in range(len(whole)):
            outs[count + i][...] = ins[2 + i][...]

    out = call(
        body, [("smem", at), ("vmem", x)] + [("vmem", y) for y in whole],
        [("vmem", struct((tokens, cols), x.dtype))] * count
        + [("vmem", struct(y.shape, y.dtype)) for y in whole],
        [], 8, x.size, "cut",
    )
    return out[:count], out[count:]


def teacher_sums(wid, rows_at, x, weights, first, cols):
    total, depth = x.shape
    tokens = total // wid.size
    held = wid.rows * tokens
    pieces = 4
    deep = depth // pieces

    def body(ins, outs, own):
        at, given, gate, up = ins[:4]
        buf, sems = own[:2]
        ordered = given if rows_at is None else outs[-1]

        def rows(r):
            return pltpu.make_async_copy(
                given.at[aligned(at[r], tokens), :], ordered.at[pl.ds(r * tokens, tokens), :], own[2].at[r]
            )

        def copy(i, k):
            here = pl.ds(k * deep, deep)
            return pltpu.make_async_copy(
                (gate, up)[i].at[here, pl.ds(first, cols)], buf.at[i, here, :], sems.at[i, k]
            )

        if rows_at is not None:
            for r in range(wid.size):
                rows(r).start()
        arrive = stream([copy(i, k) for i in range(2) for k in range(pieces)], pieces)
        yield
        if rows_at is not None:
            for r in range(wid.size):
                rows(r).wait()
        for i in range(2):
            part = None
            for half in range(2):
                here = slice(half * depth // 2, (half + 1) * depth // 2)
                for k in range(half * pieces // 2, (half + 1) * pieces // 2):
                    arrive(i * pieces + k)
                more = dot(ordered[:, here], buf[i, here, :])
                part = more if half == 0 else part + more
            for r in range(wid.rows):
                outs[r][i] = part[r * tokens : (r + 1) * tokens]
            for c in range(1, wid.cores):
                outs[wid.rows + c - 1][i] = part[c * held : (c + 1) * held].astype(BF16)

    scratch = [pltpu.VMEM((2, depth, cols), BF16), pltpu.SemaphoreType.DMA((2, pieces))]
    if rows_at is None:
        ins, more = [("smem", jnp.zeros((1,), jnp.int32)), ("vmem", x)], []
    else:
        ins, more = [("smem", rows_at), ("any", x)], [("vmem", struct(x.shape, BF16))]
        scratch.append(pltpu.SemaphoreType.DMA((wid.size,)))
    return call(
        body, ins + [("any", w) for w in weights],
        [("vmem", struct((2, tokens, cols), F32))] * wid.rows
        + [("vmem", struct((2, held, cols), BF16))] * (wid.cores - 1)
        + more,
        scratch, 60, 4 * total * depth * cols, "teacher_sums",
    )


def teacher_down_blocks(plane, pieces, weight):
    depth, width = weight.shape
    count = plane.size
    cols = width // count
    rows = [row[0].shape[0] for row in pieces]
    total = sum(rows)
    deeps = [part.shape[1] for part in pieces[0]]
    spots = plane.spots()

    def body(ins, outs, own):
        place, parts, w = ins[0], ins[1:-1], ins[-1]
        whole, buf, result, sems = own

        def copy(k):
            here = pl.ds(sum(deeps[:k]), deeps[k])
            return pltpu.make_async_copy(w.at[here, :], buf.at[here, :], sems.at[k])

        arrive = stream([copy(k) for k in range(len(deeps))], 2)
        yield
        n = row = 0
        for i, line in enumerate(pieces):
            col = 0
            for part in line:
                whole[row : row + rows[i], col : col + part.shape[1]] = parts[n][...]
                col += part.shape[1]
                n += 1
            row += rows[i]
        for k in range(len(deeps)):
            arrive(k)
            here = slice(sum(deeps[:k]), sum(deeps[: k + 1]))
            part = dot(whole[:, here], buf[here, :])
            result[...] = part if k == 0 else result[...] + part
        for r in plane.order():
            i, j = spots[r]
            block = result[:, aligned(place[r], cols)].astype(BF16)
            if j is None:
                outs[i][...] = block
            else:
                outs[i][j] = block

    return call(
        body, [("smem", plane.to)] + [("load", x) for x in flat(pieces)] + [("any", weight)],
        plane.shapes(total, cols),
        [
            pltpu.VMEM((total, depth), BF16),
            pltpu.VMEM((depth, width), BF16),
            pltpu.VMEM((total, width), F32),
            pltpu.SemaphoreType.DMA((len(deeps),)),
        ],
        60, 2 * total * depth * width, "teacher_down",
    )


def student_forward(plane, student_in, norm_gain, gate_weight, up_weight, down_weight):
    tokens, width = student_in.shape
    spots = plane.spots()
    cols = gate_weight.shape[1]
    count = 8
    deep = width // count

    def body(ins, outs, own):
        where, x, gain, wg, wu, wd = ins
        normed, gate, up, hidden, inverse = outs[:5]
        branches = outs[5:]
        buf, down, sems, down_sems = own

        def copy(i, k):
            return pltpu.make_async_copy(
                (wg, wu)[i].at[pl.ds(k * deep, deep), :], buf.at[i, k], sems.at[i, k]
            )

        def copy_down(k):
            here = pl.ds(k * (cols // 2), cols // 2)
            return pltpu.make_async_copy(wd.at[here, :], down.at[here, :], down_sems.at[k])

        arrive = stream(
            [copy(i, k) for k in range(count) for i in range(2)] + [copy_down(k) for k in range(2)], 4
        )
        yield
        values = x[...].astype(F32)
        inv = lax.rsqrt(jnp.sum(values * values, axis=-1, keepdims=True) / width + 1e-05)
        inverse[...] = inv
        normed[...] = (values * inv * gain[...]).astype(BF16)
        sums = [None, None]
        for k in range(count):
            for i in range(2):
                arrive(2 * k + i)
                part = dot(normed[:, k * deep : (k + 1) * deep], buf[i, k])
                sums[i] = part if k == 0 else sums[i] + part
        gate[...] = sums[0]
        up[...] = sums[1]
        hidden[...] = (sums[0] * jax.nn.sigmoid(sums[0]) * sums[1]).astype(BF16)
        for k in range(2):
            arrive(2 * count + k)
        share = width // plane.size
        for r in plane.order():
            i, j = spots[r]
            block = dot(hidden[...], down[:, aligned(where[r], share)]).astype(BF16)
            if j is None:
                branches[i][...] = block
            else:
                branches[i][j] = block

    return call(
        body,
        [("smem", plane.to), ("load", student_in), ("load", norm_gain.reshape(1, width))]
        + [("any", w) for w in (gate_weight, up_weight, down_weight)],
        [
            ("vmem", struct((tokens, width), BF16)),
            ("vmem", struct((tokens, cols), F32)),
            ("vmem", struct((tokens, cols), F32)),
            ("vmem", struct((tokens, cols), BF16)),
            ("vmem", struct((tokens, 1), F32)),
        ]
        + plane.shapes(tokens, width // plane.size),
        [
            pltpu.VMEM((2, count, deep, cols), BF16),
            pltpu.VMEM((cols, width), BF16),
            pltpu.SemaphoreType.DMA((2, count)),
            pltpu.SemaphoreType.DMA((2,)),
        ],
        60, 6 * tokens * width * cols, "student_forward",
    )


def student_features(at, branch, student_in, matrix):
    tokens, width = student_in.shape
    count = len(branch)
    cols = width // count
    out_cols = matrix.shape[1]

    def body(ins, outs, own):
        where, x, w = ins[:3]
        pieces = ins[3:]
        summed, features = outs
        buf, sems = own

        def copy(r):
            return pltpu.make_async_copy(w.at[aligned(where[r], cols), :], buf.at[r], sems.at[r])

        arrive = stream([copy(r) for r in range(count)], 3)
        yield
        total = None
        for r in range(count):
            place = aligned(where[r], cols)
            block = (x[:, place].astype(F32) + pieces[r][...].astype(F32)).astype(BF16)
            summed[:, place] = block
            arrive(r)
            part = dot(block, buf[r])
            total = part if total is None else total + part
        features[...] = total

    return call(
        body, [("smem", at), ("load", student_in), ("any", matrix)] + [("load", x) for x in branch],
        [("vmem", struct((tokens, width), BF16)), ("vmem", struct((tokens, out_cols), F32))],
        [pltpu.VMEM((count, cols, out_cols), BF16), pltpu.SemaphoreType.DMA((count,))],
        60, 2 * tokens * width * out_cols, "student_features",
    )


def error_grad(plane, order, target, features, matrix, scale):
    tokens, out_cols = features.shape
    width = matrix.shape[0]
    count = plane.size
    cols = width // count
    parts = len(target)
    share = out_cols // parts
    spots = plane.spots()

    def body(ins, outs, own):
        where, place, feats, w = ins[:4]
        pieces = ins[4 : 4 + parts]
        error = outs[-1]
        held, buf, sems = own

        def copy(r):
            return pltpu.make_async_copy(w.at[aligned(where[r], cols), :], buf.at[r], sems.at[r])

        arrive = stream([copy(r) for r in plane.order()], 3)
        yield
        for r in range(parts):
            held[place[r]] = pieces[r][...]
        for r in range(parts):
            here = slice(r * share, (r + 1) * share)
            error[:, here] = ((feats[:, here] - held[r].astype(F32)) * scale).astype(BF16)
        for k, r in enumerate(plane.order()):
            i, j = spots[r]
            arrive(k)
            block = dot_t(error[...], buf[r]).astype(BF16)
            if j is None:
                outs[i][...] = block
            else:
                outs[i][j] = block

    out = call(
        body,
        [("smem", plane.to), ("smem", order), ("load", features), ("any", matrix)]
        + [("load", x) for x in target],
        plane.shapes(tokens, cols) + [("vmem", struct((tokens, out_cols), BF16))],
        [
            pltpu.VMEM((parts, tokens, share), BF16),
            pltpu.VMEM((count, cols, out_cols), BF16),
            pltpu.SemaphoreType.DMA((count,)),
        ],
        60, 2 * tokens * width * out_cols, "error_grad",
    )
    return out[-1], out[:-1]


SPARE = 16


def hidden_grads(at, pieces, gate, up, weight):
    tokens, units = gate.shape
    width = weight.shape[1]
    count = len(pieces)
    cols = width // count

    def body(ins, outs, own):
        where, gate_ref, up_ref, w = ins[:4]
        blocks = ins[4:]
        branch_grad, grads, moment = outs
        buf, sems = own

        def copy(r):
            return pltpu.make_async_copy(w.at[:, aligned(where[r], cols)], buf.at[r], sems.at[r])

        arrive = stream([copy(r) for r in range(count)], 3)
        yield
        total = None
        for r in range(count):
            block = blocks[r][...]
            branch_grad[:, aligned(where[r], cols)] = block
            arrive(r)
            part = dot_t(block, buf[r])
            total = part if total is None else total + part
        g, u = gate_ref[...], up_ref[...]
        sigma = jax.nn.sigmoid(g)
        dg = (total * u * sigma * (1.0 + g * (1.0 - sigma))).astype(BF16)
        du = (total * g * sigma).astype(BF16)
        grads[:, :units] = dg
        grads[:, units:] = du
        terms = (dg.astype(F32) * g + du.astype(F32) * u).astype(BF16)
        moment[...] = dot_t(jnp.ones((SPARE, units), BF16), terms)

    return call(
        body,
        [("smem", at), ("load", gate), ("load", up), ("any", weight)] + [("load", x) for x in pieces],
        [
            ("vmem", struct((tokens, width), BF16)),
            ("vmem", struct((tokens, 2 * units), BF16)),
            ("vmem", struct((SPARE, tokens), F32)),
        ],
        [pltpu.VMEM((count, units, cols), BF16), pltpu.SemaphoreType.DMA((count,))],
        60, 2 * tokens * width * units, "hidden_grads",
    )


def normed_grads(plane, grads, moment, gate_weight, up_weight):
    tokens, units = grads.shape[0], grads.shape[1] // 2
    width = gate_weight.shape[0]
    count = plane.size
    cols = width // count
    spots = plane.spots()

    def body(ins, outs, own):
        where, x, row, wg, wu = ins
        buf, dg, du, sems = own

        def copy(i, r):
            return pltpu.make_async_copy(
                (wg, wu)[i].at[aligned(where[r], cols), :], buf.at[i, r], sems.at[i, r]
            )

        arrive = stream([copy(i, r) for r in plane.order() for i in range(2)], 4)
        yield
        dg[...] = x[:, :units]
        du[...] = x[:, units:]
        for k, r in enumerate(plane.order()):
            i, j = spots[r]
            arrive(2 * k)
            arrive(2 * k + 1)
            block = (dot_t(dg[...], buf[0, r]) + dot_t(du[...], buf[1, r])).astype(BF16)
            out = outs[i] if j is None else outs[i].at[j]
            out[:tokens, :] = block
            out[tokens:, :] = jnp.zeros((SPARE, cols), BF16)
            out[tokens:, :tokens] = row[...].astype(BF16)

    return call(
        body,
        [("smem", plane.to), ("load", grads), ("load", moment), ("any", gate_weight), ("any", up_weight)],
        plane.shapes(tokens + SPARE, cols),
        [
            pltpu.VMEM((2, count, cols, units), BF16),
            pltpu.VMEM((tokens, units), BF16),
            pltpu.VMEM((tokens, units), BF16),
            pltpu.SemaphoreType.DMA((2, count)),
        ],
        60, 4 * tokens * width * units, "normed_grads",
    )


def token_products(left, right):
    tokens, rows = left[0].shape
    cols = right[0].shape[1] // 2
    count = len(left)

    def body(ins, outs, own):
        lefts, rights = ins[:count], ins[count:]
        flipped, held = own
        yield
        for r in range(count):
            here = slice(r * tokens, (r + 1) * tokens)
            flipped[:, here] = lefts[r][...].T
            held[here, :] = rights[r][...]
        for i in range(2):
            for start in range(0, cols, 256):
                size = min(256, cols - start)
                part = dot(flipped[...], held[:, i * cols + start : i * cols + start + size])
                outs[i][:, start : start + size] = part.astype(BF16)

    return call(
        body, [("load", x) for x in [*left, *right]], [("vmem", struct((rows, cols), BF16))] * 2,
        [pltpu.VMEM((rows, count * tokens), BF16), pltpu.VMEM((count * tokens, 2 * cols), BF16)],
        60, 4 * count * tokens * rows * cols, "token_products",
    )


def shards(
    student_in,
    norm_gain,
    gate_weight,
    up_weight,
    down_weight,
    projection,
    teacher_in,
    teacher_gate,
    teacher_up,
    teacher_down,
):
    wid, plane = Wid(), Plane()
    tokens, width = student_in.shape
    total_tokens = tokens * wid.size
    share = projection.shape[2]

    rows_at = jnp.stack(
        [wid.at(drow, dcore) for dcore in range(wid.cores) for drow in range(wid.rows)]
    ).astype(jnp.int32)
    units = teacher_gate.shape[1]
    tile = next((t for t in (256, 128) if units % t == 0), units // 2)
    middle = (units // tile + 1) // 2 * tile
    x, sums, sends = teacher_in, [], []
    for start, stop in ((0, middle), (middle, units)):
        if start:
            x = tie(x, student[3], *sends)
            first = plane.send_message(student[5:], 0)
        parts = teacher_sums(
            wid, None if start else rows_at, x, (teacher_gate, teacher_up), start, stop - start
        )
        if start:
            *mine, theirs = parts
            parts = (*mine, tie(theirs, *sums[0][1:], *first))
        if not start:
            *parts, x = parts
            student = student_forward(
                plane, tie(student_in, parts[0]), norm_gain, gate_weight, up_weight, down_weight
            )
        rows, got = [], [wid.send(part, 0, c + 1) for c, part in enumerate(parts[wid.rows :])]
        for r in range(wid.rows):
            row = parts[r]
            for block in got:
                row = row + block[:, r * tokens : (r + 1) * tokens].astype(F32)
            if r:
                sends.append(row.astype(BF16))
                row = wid.send(sends[-1], r, 0)
            rows.append(row)
        sums.append(rows)

    normed, gate_sum, up_sum, hidden, inverse_rms, *blocks = student
    branch = plane.scatter_sum(blocks, first, tuple(sends[wid.rows - 1 :])).astype(BF16)
    branch_all = plane.gather(branch)

    hidden_blocks = [[[] for _ in range(wid.rows)] for _ in range(wid.cores)]
    for rows in sums:
        gate_rows, up_rows = (sum([row[i].astype(F32) for row in rows[1:]], rows[0][i]) for i in range(2))
        teacher_hidden = (gate_rows * jax.nn.sigmoid(gate_rows) * up_rows).astype(BF16)
        for drow, group in enumerate(wid.gather(teacher_hidden)):
            for dcore, block in enumerate(group):
                hidden_blocks[dcore][drow].append(block)
    pieces = flat(hidden_blocks)
    places = [(drow, dcore) for dcore in range(wid.cores) for drow in range(wid.rows)]

    if share % 128 == 0:
        blocks = teacher_down_blocks(plane, pieces, teacher_down)
    else:
        rows = [jnp.concatenate(row, axis=1) for row in pieces]
        blocks = plane.split(dot(jnp.concatenate(rows, axis=0), teacher_down).astype(BF16))

    swap_at = jnp.stack([wid.at(-drow, -dcore) for drow, dcore in places]).astype(jnp.int32)

    def swap(x, whole=()):
        made, copies = cut(swap_at, x, whole)
        return [
            wid.send(block, -drow, -dcore) if drow + dcore else block
            for block, (drow, dcore) in zip(made, places)
        ], copies

    def everyone(x):
        groups = wid.gather(x)
        return [groups[drow][dcore] for drow, dcore in places]

    normed_cols, (hidden_late,) = swap(tie(normed, blocks[0]), (hidden,))
    hidden_all = everyone(hidden_late)

    relaid = []

    def relay(parts, landed):
        if relaid:
            return ()
        relaid.append(tie(projection, *parts).reshape(width, -1))
        return (*relaid, *landed)

    cols = plane.scatter_sum(blocks, between=relay).astype(BF16)
    (matrix,) = relaid
    summed, features = student_features(plane.source, branch_all, student_in, matrix)
    cols = tie(cols, features)
    target, order = [], []
    for i, (drow, dcore) in enumerate(places):
        block = cols[i * tokens : (i + 1) * tokens]
        target.append(wid.send(block, drow, dcore) if drow + dcore else block)
        order.append(wid.at(-drow, -dcore))
    order = jnp.stack(order).astype(jnp.int32)

    feature_error, blocks = error_grad(
        plane, order, target, tie(features, *normed_cols, *hidden_all), matrix,
        1.0 / math.sqrt(total_tokens),
    )
    summed_cols, _ = swap(tie(summed, blocks[0]))
    error_all = everyone(feature_error)
    feature_share = plane.scatter_sum(blocks)

    def stack(blocks):
        return jnp.concatenate(blocks, axis=0)

    grad_proj = dot(stack(tie(tuple(summed_cols), feature_share)).T, stack(error_all)).astype(BF16)
    branch_grad, grads, moment = hidden_grads(
        plane.source, plane.gather(feature_share.astype(BF16), (grad_proj,)),
        gate_sum, up_sum, down_weight,
    )
    paired_all = everyone(grads)
    blocks = normed_grads(plane, grads, moment, gate_weight, up_weight)
    units = gate_sum.shape[1]

    branch_cols, _ = swap(tie(branch_grad, blocks[0]))
    sent = []

    def keep(parts, _):
        sent.extend(parts)
        return ()

    normed_share = plane.scatter_sum(blocks, between=keep)
    grad_down = dot(stack(tie(tuple(hidden_all), sent[-1])).T, stack(branch_cols)).astype(BF16)
    grad_proj = tie(grad_proj, sent[-1]).reshape(-1, wid.size, share)
    grad_gate, grad_up = token_products(normed_cols, paired_all)

    normed_share = tie(normed_share, grad_gate)
    moment = normed_share[tokens, :tokens].reshape(tokens, 1)
    normed_share = normed_share[:tokens]
    share_cols = normed_share.shape[1]
    offset = plane.index * share_cols
    gain_share = lax.dynamic_slice_in_dim(norm_gain, offset, share_cols, 0)
    inputs_share = lax.dynamic_slice_in_dim(student_in, offset, share_cols, 1).astype(F32)
    input_grad = feature_share + inverse_rms * (
        normed_share * gain_share - inputs_share * inverse_rms * (moment / width)
    )
    return (grad_gate, grad_up, grad_down, grad_proj, input_grad)


def solution(mesh):
    in_specs = (
        P("wid", None),
        P(),
        P(None, ("grp", "hid")),
        P(None, ("grp", "hid")),
        P(("grp", "hid"), None),
        P(None, None, ("grp", "hid")),
        P(None, "wid"),
        P("wid", ("grp", "hid")),
        P("wid", ("grp", "hid")),
        P(("grp", "hid"), "wid"),
    )
    out_specs = (
        P("wid", ("grp", "hid")),
        P("wid", ("grp", "hid")),
        P(("grp", "hid"), "wid"),
        P("wid", None, ("grp", "hid")),
        P("wid", ("grp", "hid")),
    )
    return jax.shard_map(shards, mesh=mesh, in_specs=in_specs, out_specs=out_specs, check_vma=False)
```

```python
import functools
import math

import jax
import jax.numpy as jnp
from jax import lax
from jax.experimental import pallas as pl
from jax.experimental.pallas import tpu as pltpu
from jax.sharding import PartitionSpec as P

F32 = jnp.float32
BF16 = jnp.bfloat16
CORES = 2
MIB = 1 << 20

ANY = pl.BlockSpec(memory_space=pl.ANY)
VMEM = pl.BlockSpec(memory_space=pltpu.VMEM)
SMEM = pl.BlockSpec(memory_space=pltpu.SMEM)


def dot(a, b):
    return jnp.dot(a, b, preferred_element_type=F32)


def dot_t(a, b):
    return lax.dot_general(a, b, (((1,), (1,)), ((), ())), preferred_element_type=F32)


def call(body, out_shape, in_specs, scratch, limit, flops, moved, name):
    return pl.pallas_call(
        body,
        out_shape=out_shape,
        in_specs=in_specs,
        out_specs=jax.tree.map(lambda _: VMEM, out_shape),
        scratch_shapes=scratch,
        compiler_params=pltpu.CompilerParams(vmem_limit_bytes=limit),
        cost_estimate=pl.CostEstimate(flops=flops, bytes_accessed=moved, transcendentals=0),
        name=name,
    )


def struct(shape, dtype):
    return jax.ShapeDtypeStruct(tuple(shape), dtype)


def aligned(position, size):
    return pl.ds(pl.multiple_of(position * size, size), size)


def shift(x, axis, step):
    size = lax.axis_size(axis)
    return lax.ppermute(x, axis, [(i, (i + step) % size) for i in range(size)])


class Wid:
    def __init__(self):
        self.size = lax.axis_size("wid")
        self.cores = CORES if self.size % CORES == 0 else 1
        self.rows = self.size // self.cores
        self.index = lax.axis_index("wid")
        self.row = self.index // self.cores
        self.core = self.index % self.cores

    def at(self, drow, dcore):
        return ((self.row + drow) % self.rows) * self.cores + (self.core + dcore) % self.cores

    def send(self, x, drow, dcore):
        pairs = []
        for i in range(self.size):
            row, core = i // self.cores, i % self.cores
            pairs.append((i, ((row + drow) % self.rows) * self.cores + (core + dcore) % self.cores))
        return lax.ppermute(x, "wid", pairs)

    def gather(self, x):
        blocks = []
        for drow in range(self.rows):
            mine = x if drow == 0 else self.send(x, -drow, 0)
            blocks.append([mine] + [self.send(mine, 0, -dcore) for dcore in range(1, self.cores)])
        return blocks

    def swap(self, x):
        cols = x.shape[1] // self.size
        blocks = []
        for drow in range(self.rows):
            group = []
            for dcore in range(self.cores):
                block = lax.dynamic_slice_in_dim(x, self.at(-drow, -dcore) * cols, cols, 1)
                group.append(block if drow + dcore == 0 else self.send(block, -drow, -dcore))
            blocks.append(group)
        return blocks


def flat(blocks):
    return [b for group in blocks for b in group]


class Plane:
    def __init__(self):
        self.ngrp, self.nhid = lax.axis_size("grp"), lax.axis_size("hid")
        self.size = self.ngrp * self.nhid
        self.g, self.h = lax.axis_index("grp"), lax.axis_index("hid")
        self.index = self.g * self.nhid + self.h
        steps = [(dg, dh) for dg in range(self.ngrp) for dh in range(self.nhid)]
        self.to = jnp.stack([self.place(dg, dh) for dg, dh in steps]).astype(jnp.int32)
        self.source = jnp.stack([self.place(-dg, -dh) for dg, dh in steps]).astype(jnp.int32)

    def place(self, dg, dh):
        return ((self.g + dg) % self.ngrp) * self.nhid + (self.h + dh) % self.nhid

    def split(self, x):
        cols = x.shape[1] // self.size
        return [
            lax.dynamic_slice_in_dim(x, self.place(dg, dh) * cols, cols, 1)
            for dg in range(self.ngrp)
            for dh in range(self.nhid)
        ]

    def scatter_sum(self, blocks):
        terms = None
        sums = []
        for dh in list(range(1, self.nhid)) + [0]:
            own = blocks[dh]
            got = [shift(blocks[dg * self.nhid + dh], "grp", dg) for dg in range(1, self.ngrp)]
            if dh:
                sums.append(shift(add(own, *got), "hid", dh))
            else:
                terms = [own] + got
        total = terms[0].astype(F32)
        for term in terms[1:] + sums:
            total = total + term.astype(F32)
        return total

    def gather(self, x):
        blocks = [None] * self.size
        for dh in range(self.nhid):
            mine = x if dh == 0 else shift(x, "hid", dh)
            for dg in range(self.ngrp):
                blocks[dg * self.nhid + dh] = mine if dg == 0 else shift(mine, "grp", dg)
        return blocks

    def total(self, x):
        for axis, size in (("grp", self.ngrp), ("hid", self.nhid)):
            x = sum([shift(x, axis, step) for step in range(1, size)], x)
        return x


def add(*blocks):
    def body(*refs):
        total = refs[0][...].astype(F32)
        for ref in refs[1:-1]:
            total = total + ref[...].astype(F32)
        refs[-1][...] = total.astype(BF16)

    x = blocks[0]
    return call(
        body, struct(x.shape, BF16), [VMEM] * len(blocks), [], 16 * MIB,
        x.size, 2 * x.size * (len(blocks) + 1), "add_blocks",
    )(*blocks)


def teacher_sums(wid, rows_at, teacher_in, weights, first, tiles, tile, after):
    total, depth = teacher_in.shape
    tokens = total // wid.size
    cols = tiles * tile
    held = wid.rows * tokens

    def body(at, x, gate, up, *refs):
        outs = refs[len(after) : len(after) + wid.cores]
        ordered, buf, sems = refs[len(after) + wid.cores :]

        def copy(i, t):
            source = (gate, up)[i].at[:, pl.ds(first + t * tile, tile)]
            return pltpu.make_async_copy(source, buf.at[i, t], sems.at[i, t])

        for t in range(tiles):
            for i in range(2):
                copy(i, t).start()
        for r in range(wid.size):
            ordered[r * tokens : (r + 1) * tokens, :] = x[aligned(at[r], tokens), :]
        for t in range(tiles):
            for i in range(2):
                copy(i, t).wait()
                part = dot(ordered[...], buf[i, t])
                for c in range(wid.cores):
                    out = outs[c]
                    out[i, :, t * tile : (t + 1) * tile] = part[c * held : (c + 1) * held].astype(out.dtype)

    out_shape = [struct((2, held, cols), F32 if c == 0 else BF16) for c in range(wid.cores)]
    return call(
        body, out_shape, [SMEM, VMEM, ANY, ANY] + [ANY] * len(after),
        [
            pltpu.VMEM((total, depth), BF16),
            pltpu.VMEM((2, tiles, depth, tile), BF16),
            pltpu.SemaphoreType.DMA((2, tiles)),
        ],
        40 * MIB, 4 * total * depth * cols, 4 * depth * cols, "teacher_sums",
    )(rows_at, teacher_in, *weights, *after)


def expand(at, pieces, weight, name):
    depth, width = weight.shape
    count = at.shape[0]
    cols = width // count
    rows = [row[0].shape[0] for row in pieces]
    total = sum(rows)
    number = sum(len(row) for row in pieces)
    x = flat(pieces)

    def body(where, *refs):
        ins, w, outs = refs[:number], refs[number], refs[number + 1 : number + 1 + count]
        whole, buf, sems = refs[number + 1 + count :]

        def copy(r):
            return pltpu.make_async_copy(w.at[:, aligned(where[r], cols)], buf.at[r], sems.at[r])

        for r in range(count):
            copy(r).start()
        n = row = 0
        for i, parts in enumerate(pieces):
            col = 0
            for part in parts:
                whole[row : row + rows[i], col : col + part.shape[1]] = ins[n][...]
                col += part.shape[1]
                n += 1
            row += rows[i]
        for r in range(count):
            copy(r).wait()
            outs[r][...] = dot(whole[...], buf[r]).astype(BF16)

    return call(
        body, [struct((total, cols), BF16)] * count, [SMEM] + [VMEM] * number + [ANY],
        [
            pltpu.VMEM((total, depth), BF16),
            pltpu.VMEM((count, depth, cols), BF16),
            pltpu.SemaphoreType.DMA((count,)),
        ],
        32 * MIB, 2 * total * depth * width, 2 * depth * width, name,
    )(at, *x, weight)


def student_hidden(student_in, norm_gain, gate_weight, up_weight, after):
    tokens, width = student_in.shape
    cols = gate_weight.shape[1]
    count = 8
    deep = width // count

    def body(x, gain, wg, wu, *refs):
        normed, inverse, gate, up, hidden = refs[len(after) : len(after) + 5]
        buf, sems = refs[len(after) + 5 :]

        def copy(i, k):
            return pltpu.make_async_copy(
                (wg, wu)[i].at[pl.ds(k * deep, deep), :], buf.at[i, k], sems.at[i, k]
            )

        for k in range(count):
            for i in range(2):
                copy(i, k).start()
        values = x[...].astype(F32)
        inv = lax.rsqrt(jnp.sum(values * values, axis=-1, keepdims=True) / width + 1e-05)
        inverse[...] = inv
        normed[...] = (values * inv * gain[...]).astype(BF16)
        sums = [None, None]
        for k in range(count):
            for i in range(2):
                copy(i, k).wait()
                part = dot(normed[:, k * deep : (k + 1) * deep], buf[i, k])
                sums[i] = part if k == 0 else sums[i] + part
        gate[...] = sums[0]
        up[...] = sums[1]
        hidden[...] = (sums[0] * jax.nn.sigmoid(sums[0]) * sums[1]).astype(BF16)

    return call(
        body,
        [
            struct((tokens, width), BF16),
            struct((tokens, 1), F32),
            struct((tokens, cols), F32),
            struct((tokens, cols), F32),
            struct((tokens, cols), BF16),
        ],
        [VMEM, VMEM, ANY, ANY] + [ANY] * len(after),
        [pltpu.VMEM((2, count, deep, cols), BF16), pltpu.SemaphoreType.DMA((2, count))],
        40 * MIB, 4 * tokens * width * cols, 4 * width * cols, "student_hidden",
    )(student_in, norm_gain.reshape(1, width), gate_weight, up_weight, *after)


def student_features(at, branch, student_in, matrix):
    tokens, width = student_in.shape
    count = len(branch)
    cols = width // count
    out_cols = matrix.shape[1]

    def body(where, x, *refs):
        pieces, w = refs[:count], refs[count]
        summed, features, buf, sems = refs[count + 1 :]

        def copy(r):
            return pltpu.make_async_copy(w.at[aligned(where[r], cols), :], buf.at[r], sems.at[r])

        for r in range(count):
            copy(r).start()
        total = None
        for r in range(count):
            place = aligned(where[r], cols)
            block = (x[:, place].astype(F32) + pieces[r][...].astype(F32)).astype(BF16)
            summed[:, place] = block
            copy(r).wait()
            part = dot(block, buf[r])
            total = part if total is None else total + part
        features[...] = total

    return call(
        body, [struct((tokens, width), BF16), struct((tokens, out_cols), F32)],
        [SMEM, VMEM] + [VMEM] * count + [ANY],
        [pltpu.VMEM((count, cols, out_cols), BF16), pltpu.SemaphoreType.DMA((count,))],
        32 * MIB, 2 * tokens * width * out_cols, 2 * width * out_cols, "student_features",
    )(at, student_in, *branch, matrix)


def error_grad(to, order, target, features, matrix, scale):
    tokens, out_cols = features.shape
    width = matrix.shape[0]
    count = to.shape[0]
    cols = width // count
    parts = len(target)
    share = out_cols // parts

    def body(where, place, *refs):
        pieces, feats, w = refs[:parts], refs[parts], refs[parts + 1]
        error, outs = refs[parts + 2], refs[parts + 3 : parts + 3 + count]
        held, buf, sems = refs[parts + 3 + count :]

        def copy(r):
            return pltpu.make_async_copy(w.at[aligned(where[r], cols), :], buf.at[r], sems.at[r])

        for r in range(count):
            copy(r).start()
        for r in range(parts):
            held[place[r]] = pieces[r][...]
        for r in range(parts):
            here = slice(r * share, (r + 1) * share)
            error[:, here] = ((feats[:, here] - held[r].astype(F32)) * scale).astype(BF16)
        for r in range(count):
            copy(r).wait()
            outs[r][...] = dot_t(error[...], buf[r]).astype(BF16)

    return call(
        body, [struct((tokens, out_cols), BF16)] + [struct((tokens, cols), BF16)] * count,
        [SMEM, SMEM] + [VMEM] * (parts + 1) + [ANY],
        [
            pltpu.VMEM((parts, tokens, share), BF16),
            pltpu.VMEM((count, cols, out_cols), BF16),
            pltpu.SemaphoreType.DMA((count,)),
        ],
        32 * MIB, 2 * tokens * width * out_cols, 2 * width * out_cols, "error_grad",
    )(to, order, *target, features, matrix)


def hidden_grads(at, pieces, gate, up, weight):
    tokens, units = gate.shape
    width = weight.shape[1]
    count = len(pieces)
    cols = width // count

    def body(where, gate_ref, up_ref, *refs):
        ins, w = refs[:count], refs[count]
        branch_grad, gate_grad, up_grad, moment, buf, sems = refs[count + 1 :]

        def copy(r):
            return pltpu.make_async_copy(w.at[:, aligned(where[r], cols)], buf.at[r], sems.at[r])

        for r in range(count):
            copy(r).start()
        total = None
        for r in range(count):
            block = ins[r][...]
            branch_grad[:, aligned(where[r], cols)] = block
            copy(r).wait()
            part = dot_t(block, buf[r])
            total = part if total is None else total + part
        g, u = gate_ref[...], up_ref[...]
        sigma = jax.nn.sigmoid(g)
        dg = (total * u * sigma * (1.0 + g * (1.0 - sigma))).astype(BF16)
        du = (total * g * sigma).astype(BF16)
        gate_grad[...] = dg
        up_grad[...] = du
        moment[...] = jnp.sum(dg.astype(F32) * g + du.astype(F32) * u, axis=-1, keepdims=True)

    return call(
        body,
        [
            struct((tokens, width), BF16),
            struct((tokens, units), BF16),
            struct((tokens, units), BF16),
            struct((tokens, 1), F32),
        ],
        [SMEM, VMEM, VMEM] + [VMEM] * count + [ANY],
        [pltpu.VMEM((count, units, cols), BF16), pltpu.SemaphoreType.DMA((count,))],
        32 * MIB, 2 * tokens * width * units, 2 * width * units, "hidden_grads",
    )(at, gate, up, *pieces, weight)


def normed_grads(to, gate_grad, up_grad, gate_weight, up_weight):
    tokens, units = gate_grad.shape
    width = gate_weight.shape[0]
    count = to.shape[0]
    cols = width // count

    def body(where, dg, du, wg, wu, *refs):
        outs = refs[:count]
        buf, sems = refs[count:]

        def copy(i, r):
            return pltpu.make_async_copy(
                (wg, wu)[i].at[aligned(where[r], cols), :], buf.at[i, r], sems.at[i, r]
            )

        for r in range(count):
            for i in range(2):
                copy(i, r).start()
        for r in range(count):
            copy(0, r).wait()
            copy(1, r).wait()
            outs[r][...] = (dot_t(dg[...], buf[0, r]) + dot_t(du[...], buf[1, r])).astype(BF16)

    return call(
        body, [struct((tokens, cols), BF16)] * count, [SMEM, VMEM, VMEM, ANY, ANY],
        [pltpu.VMEM((2, count, cols, units), BF16), pltpu.SemaphoreType.DMA((2, count))],
        40 * MIB, 4 * tokens * width * units, 4 * width * units, "normed_grads",
    )(to, gate_grad, up_grad, gate_weight, up_weight)


def shards(
    student_in,
    norm_gain,
    gate_weight,
    up_weight,
    down_weight,
    projection,
    teacher_in,
    teacher_gate,
    teacher_up,
    teacher_down,
):
    wid, plane = Wid(), Plane()
    tokens, width = student_in.shape
    total_tokens = tokens * wid.size
    share = projection.shape[2]

    rows_at = jnp.stack(
        [wid.at(drow, dcore) for dcore in range(wid.cores) for drow in range(wid.rows)]
    ).astype(jnp.int32)
    units = teacher_gate.shape[1]
    tile = next((t for t in (256, 128) if units % t == 0), units // 2)
    tiles = units // tile
    chunks = [(0, tiles // 2), (tiles // 2, tiles - tiles // 2)]
    after = ()
    hidden_blocks = [[[] for _ in range(wid.cores)] for _ in range(wid.rows)]
    for first, number in chunks:
        parts = teacher_sums(
            wid, rows_at, teacher_in, (teacher_gate, teacher_up), first * tile, number, tile, after
        )
        after = (parts[0],)
        own = parts[0]
        for dcore in range(1, wid.cores):
            own = own + wid.send(parts[dcore], 0, dcore).astype(F32)
        sums = own[:, :tokens]
        for drow in range(1, wid.rows):
            sent = own[:, drow * tokens : (drow + 1) * tokens].astype(BF16)
            sums = sums + wid.send(sent, drow, 0).astype(F32)
        teacher_hidden = (sums[0] * jax.nn.sigmoid(sums[0]) * sums[1]).astype(BF16)
        for drow, group in enumerate(wid.gather(teacher_hidden)):
            for dcore, block in enumerate(group):
                hidden_blocks[drow][dcore].append(block)

    normed, inverse_rms, gate_sum, up_sum, hidden = student_hidden(
        student_in, norm_gain, gate_weight, up_weight, after
    )
    branch = plane.scatter_sum(expand(plane.to, [[hidden]], down_weight, "student_down")).astype(BF16)
    branch_all = plane.gather(branch)

    target, order = [], []
    for drow in range(wid.rows):
        if share % 128 == 0:
            blocks = expand(plane.to, hidden_blocks[drow], teacher_down, "teacher_down")
        else:
            rows = [jnp.concatenate(row, axis=1) for row in hidden_blocks[drow]]
            blocks = plane.split(dot(jnp.concatenate(rows, axis=0), teacher_down).astype(BF16))
        cols = plane.scatter_sum(blocks).astype(BF16)
        for dcore in range(wid.cores):
            block = cols[dcore * tokens : (dcore + 1) * tokens]
            target.append(wid.send(block, drow, dcore) if drow + dcore else block)
            order.append(wid.at(-drow, -dcore))
    order = jnp.stack(order).astype(jnp.int32)
    matrix = lax.optimization_barrier((projection, blocks[0]))[0].reshape(width, -1)
    summed, features = student_features(plane.source, branch_all, student_in, matrix)

    feature_error, *blocks = error_grad(
        plane.to, order, target, features, matrix, 1.0 / math.sqrt(total_tokens)
    )
    feature_share = plane.scatter_sum(blocks)
    branch_grad, gate_grad, up_grad, moment = hidden_grads(
        plane.source, plane.gather(feature_share.astype(BF16)), gate_sum, up_sum, down_weight
    )
    moment = plane.total(moment)
    normed_share = plane.scatter_sum(normed_grads(plane.to, gate_grad, up_grad, gate_weight, up_weight))
    share_cols = normed_share.shape[1]
    offset = plane.index * share_cols
    gain_share = lax.dynamic_slice_in_dim(norm_gain, offset, share_cols, 0)
    inputs_share = lax.dynamic_slice_in_dim(student_in, offset, share_cols, 1).astype(F32)
    input_grad = feature_share + inverse_rms * (
        normed_share * gain_share - inputs_share * inverse_rms * (moment / width)
    )

    def columns(x):
        return jnp.concatenate(flat(wid.swap(x)), axis=0)

    def everyone(x):
        return jnp.concatenate(flat(wid.gather(x)), axis=0)

    normed_cols = columns(normed)
    grad_proj = dot(columns(summed).T, everyone(feature_error)).astype(BF16)
    grad_proj = grad_proj.reshape(-1, wid.size, share)
    grad_down = dot(everyone(hidden).T, columns(branch_grad)).astype(BF16)
    grad_gate = dot(normed_cols.T, everyone(gate_grad)).astype(BF16)
    grad_up = dot(normed_cols.T, everyone(up_grad)).astype(BF16)
    return (grad_gate, grad_up, grad_down, grad_proj, input_grad)


def solution(mesh):
    in_specs = (
        P("wid", None),
        P(),
        P(None, ("grp", "hid")),
        P(None, ("grp", "hid")),
        P(("grp", "hid"), None),
        P(None, None, ("grp", "hid")),
        P(None, "wid"),
        P("wid", ("grp", "hid")),
        P("wid", ("grp", "hid")),
        P(("grp", "hid"), "wid"),
    )
    out_specs = (
        P("wid", ("grp", "hid")),
        P("wid", ("grp", "hid")),
        P(("grp", "hid"), "wid"),
        P("wid", None, ("grp", "hid")),
        P("wid", ("grp", "hid")),
    )
    return jax.shard_map(shards, mesh=mesh, in_specs=in_specs, out_specs=out_specs, check_vma=False)
```
